256 devices in a mesh: dom: 16 (over y_hi, x, core), space: 16 (over y_lo, z).
Axes of the slice: x: 4, y: 4 (y_hi: 2, y_lo: 2; y = y_hi * 2 + y_lo), z: 8, core: 2. Of those that a mesh axis runs over, the one named last changes fastest.
Arguments:
- ensemble: float32 [512, 4, 16, 8192], P('dom', None, None, 'space'), may hold values from -6 to 6
- ancestors: int32 [512], replicated, may hold values from 0 to 511, as said below
- perturbation: float32 [512, 16, 8192], P('dom', None, 'space'), may hold values from -4 to 4
- levels: int32 [16, 8192], P(None, 'space'), may hold values from 0 to 3
- observed: float32 [16, 8192], P(None, 'space'), may hold values from -6 to 6
Outputs:
- forecast: float32 [512, 4, 16, 8192], P('dom', None, None, 'space')
The draws below stay inside these ranges and needn't reach their ends.
Inputs may be any that keep to these rules, and one draw needn't show every extreme that they name: `ancestors`: call slots and particles k*32 to k*32 + 31 block k. In every block k after the first, the first 2 slots copy the last 2 particles of block k-1, each exactly once; in every block k before the last, the last 2 slots copy the first 2 particles of block k+1, each exactly once; every other slot copies a particle of its own block.
All inputs are finite; a program needn't handle non-finite values.
Results may differ from the reference program's by a relative error of at most 0.00012.
Values sent between devices are 32-bit elements; how exact they have to be, the bound alone decides.
A program may use at most 64 MiB of HBM per device.

```python
import jax
import jax.numpy as jnp

PD = 32
F = 4
Y = 16
STEPS = 3
CAP = 2
P_SIZE = 512
NX = 8192


def permute_rows(base_key, row_count, length):

    def one_row(row_key):
        return jax.random.permutation(row_key, length)
    return jax.vmap(one_row)(jax.random.split(base_key, row_count))


def draw_ancestors(key, part):
    key = jax.random.fold_in(key, 7)
    block_count = P_SIZE // PD
    key_list = jax.random.split(key, 3)
    blocks = jnp.arange(block_count, dtype=jnp.int32)[:, None]
    inner = jax.random.randint(key_list[0], (block_count, PD), 0, PD).astype(jnp.int32) + blocks * PD
    low_perm = permute_rows(key_list[1], block_count, CAP).astype(jnp.int32)
    high_perm = permute_rows(key_list[2], block_count, CAP).astype(jnp.int32)
    low_copy = blocks * PD - CAP + low_perm
    high_copy = (blocks + 1) * PD + high_perm
    low_part = jnp.where(blocks > 0, low_copy, inner[:, :CAP])
    high_part = jnp.where(blocks < block_count - 1, high_copy, inner[:, PD - CAP:])
    parents = jnp.concatenate([low_part, inner[:, CAP:PD - CAP], high_part], axis=1).reshape(P_SIZE)
    return parents.astype(jnp.int32)


def place_ends(entries, stream_key, smallest, high):
    index_at = [jax.random.randint(jax.random.fold_in(stream_key, axis), (), 0, length) for axis, length in enumerate(entries.shape)]
    main_axis = entries.shape.index(max(entries.shape))
    next_to = index_at[:main_axis] + [(index_at[main_axis] + 1) % entries.shape[main_axis]] + index_at[main_axis + 1:]
    return entries.at[tuple(index_at)].set(smallest).at[tuple(next_to)].set(high)


def shard_levels(rng, dims, cuts, smallest, top_value):
    def one(position, parts):
        draws = jax.random.uniform(jax.random.fold_in(jax.random.fold_in(rng, 6), position), (parts,), jnp.float32, smallest / len(cuts), top_value / len(cuts))
        return jnp.repeat(jnp.exp(draws), dims[position] // parts).reshape((-1,) + (1,) * (len(dims) - position - 1))

    level = one(*cuts[0])
    for cut in cuts[1:]:
        level = level * one(*cut)
    return level


def gaussian(key, extent, scale, limit, cuts=(), held_as=jnp.bfloat16):
    array = jax.random.normal(key, extent, jnp.float32) * scale
    if len(cuts) > 0:
        array = shard_levels(key, extent, cuts, -0.22, 0.18) * array
    return jnp.clip(array, min=-limit, max=limit).astype(held_as)


def setup_inputs(seed: int = 0) -> dict:
    streams_of = jax.random.split(jax.random.key(seed), 6)
    ensemble = gaussian(streams_of[0], (P_SIZE, F, Y, NX), 1.0, 6.0, ((0, 16), (3, 16)), jnp.float32)
    ancestors = draw_ancestors(jax.random.fold_in(streams_of[5], 71), 0)
    perturbation = gaussian(streams_of[2], (P_SIZE, Y, NX), 0.5, 4.0, ((0, 16), (2, 16)), jnp.float32)
    levels = place_ends(jax.random.randint(streams_of[3], (Y, NX), 0, 4), jax.random.fold_in(streams_of[3], 1), 0, 3).astype(jnp.int32)
    observed = gaussian(streams_of[4], (Y, NX), 1.0, 6.0, ((1, 16),), jnp.float32)
    return dict(ensemble=ensemble, ancestors=ancestors, perturbation=perturbation, levels=levels, observed=observed)


def to_north(field):
    return jnp.concatenate([field[..., 1:, :], jnp.zeros_like(field[..., :1, :])], axis=-2)


def to_south(field):
    return jnp.concatenate([jnp.zeros_like(field[..., :1, :]), field[..., :-1, :]], axis=-2)


def interior(field):
    return field[..., 1:-1]


def laplace(field):
    return field[..., 2:] + field[..., :-2] + interior(to_north(field)) + interior(to_south(field)) - 4.0 * interior(field)


def advance(state, ground):
    east_flow = state[:, 0]
    north_flow = state[:, 1]
    height = state[:, 2]
    tracer = state[:, 3]
    band_rows = state.shape[-2]
    coriolis = (0.2 + 0.6 * jnp.arange(band_rows, dtype=jnp.float32) / band_rows)[:, None]
    sea_depth = ground[0]
    wet_mask = ground[1]
    observed = ground[2]
    grad_x = 0.5 * (height[..., 2:] - height[..., :-2])
    grad_y = 0.5 * interior(to_north(height) - to_south(height))
    east_mid = interior(wet_mask) * (0.95 * interior(east_flow) + 0.2 * coriolis * interior(north_flow) - grad_x + 0.1 * laplace(east_flow))
    north_mid = interior(wet_mask) * (0.95 * interior(north_flow) - 0.2 * coriolis * interior(east_flow) - grad_y + 0.1 * laplace(north_flow))
    spread = 0.5 * (east_mid[..., 2:] - east_mid[..., :-2]) + 0.5 * interior(to_north(north_mid) - to_south(north_mid))
    height_core = interior(interior(height))
    height_new = height_core - interior(interior(sea_depth)) * spread + 0.1 * (interior(interior(observed)) - height_core)
    tracer_mid = interior(tracer)
    slope_x = 0.5 * (tracer_mid[..., 2:] - tracer_mid[..., :-2])
    slope_y = 0.5 * interior(interior(to_north(tracer) - to_south(tracer)))
    tracer_new = interior(tracer_mid) + 0.1 * interior(laplace(tracer)) - 0.2 * (interior(east_mid) * slope_x + interior(north_mid) * slope_y)
    return jnp.stack([interior(east_mid), interior(north_mid), height_new, tracer_new], axis=1)


def reference(ensemble, ancestors, perturbation, levels, observed):
    state = jnp.take(ensemble, ancestors, axis=0)
    state = state.at[:, 2].add(perturbation)
    ground = jnp.stack([0.5 * levels.astype(jnp.float32), (levels > 0).astype(jnp.float32), observed])
    ground_wide = jnp.pad(ground, ((0, 0), (0, 0), (2, 2)), mode="wrap")
    for step_index in range(STEPS):
        widened = jnp.pad(state, ((0, 0), (0, 0), (0, 0), (2, 2)), mode="wrap")
        state = advance(widened, ground_wide)
    return state
```

```python
import functools

import jax
import jax.numpy as jnp
from jax import lax
from jax.experimental import pallas as pl
from jax.experimental.pallas import tpu as pltpu
from jax.sharding import PartitionSpec as P

MESH = pl.DeviceIdType.MESH
STEPS = 3
CAP = 2
EDGE = 2 * STEPS
LANES = 128
TOP = 8
PITCH = 32
UNIT = 4
E_, N_, H_, C_ = range(4)


def lane_of(shape):
    return lax.broadcasted_iota(jnp.int32, shape, len(shape) - 1)


def east(cells, joined):
    turned = pltpu.roll(cells, LANES - 1, 2)
    if not joined:
        return turned
    following = jnp.concatenate([turned[1:], turned[:1]], axis=0)
    return jnp.where(lane_of(cells.shape) == LANES - 1, following, turned)


def west(cells, joined):
    turned = pltpu.roll(cells, 1, 2)
    if not joined:
        return turned
    preceding = jnp.concatenate([turned[-1:], turned[:-1]], axis=0)
    return jnp.where(lane_of(cells.shape) == 0, preceding, turned)


def flow(read, wet, turn, joined):
    e, n, h = read(E_, 0), read(N_, 0), read(H_, 0)
    e_new = wet * (
        (5.5 * e + turn * n)
        + (read(E_, 1) + read(E_, -1))
        + (east(e - h, joined) + west(e + h, joined))
    )
    n_new = wet * (
        (5.5 * n - turn * e)
        + (east(n, joined) + west(n, joined))
        + ((read(N_, 1) - read(H_, 1)) + (read(N_, -1) + read(H_, -1)))
    )
    return e_new, n_new


def level(read, read_new, depth, pull, last, joined):
    e, n = read_new(E_, 0), read_new(N_, 0)
    spread = (east(e, joined) - west(e, joined)) + (read_new(N_, 1) - read_new(N_, -1))
    h_new = ((0.18 if last else 0.9) * read(H_, 0) + pull) - depth * spread
    c = read(C_, 0)
    c_east, c_west = east(c, joined), west(c, joined)
    c_north, c_south = read(C_, 1), read(C_, -1)
    c_new = (
        (6.0 * c + ((c_east + c_west) + (c_north + c_south)))
        - e * (c_east - c_west)
        - n * (c_north - c_south)
    )
    if last:
        c_new = 0.001 * c_new
    return h_new, c_new


def kernel(
    anc, ens, pert, lev, obs, out,
    own, ext, h0, pv, lv, ov, gw, gd, go, s1, s2,
    out1, out2, in1, in2, gs, b0, b1, b2,
    in_sem, dom_out_sem, dom_in_sem, msg_out_sem, msg_in_sem,
):
    pd = ens.shape[0]
    ny = ens.shape[2]
    tiles = ens.shape[3] // LANES
    doms, spaces = lax.axis_size("dom"), lax.axis_size("space")
    k, me = lax.axis_index("dom"), lax.axis_index("space")
    prev_space, next_space = lax.rem(me + spaces - 1, spaces), lax.rem(me + 1, spaces)
    prev_dom, next_dom = lax.rem(k + doms - 1, doms), lax.rem(k + 1, doms)
    early = pd - 2 * CAP
    rows = slice(TOP, TOP + ny)

    barrier = pltpu.get_barrier_semaphore()
    for where in ((k, prev_space), (k, next_space), (prev_dom, me), (next_dom, me)):
        pl.semaphore_signal(barrier, inc=1, device_id=where, device_id_type=MESH)

    def tile(q):
        return pl.ds(q * LANES, LANES)

    loads = []
    for q in range(tiles):
        loads.append(pltpu.make_async_copy(lev.at[:, tile(q)], lv.at[q], in_sem.at[0, q]))
        loads.append(pltpu.make_async_copy(obs.at[:, tile(q)], ov.at[q], in_sem.at[1, q]))
        loads.append(pltpu.make_async_copy(pert.at[:, :, tile(q)], pv.at[:, q], in_sem.at[2, q]))
        loads.append(pltpu.make_async_copy(ens.at[:, :, :, tile(q)], own.at[:, :, q, rows], in_sem.at[3, q]))
    for copy in loads:
        copy.start()

    pl.semaphore_wait(barrier, 4)

    def dom_copy(up, q):
        first, lands, to = (pd - CAP, 0, next_dom) if up else (0, CAP, prev_dom)
        return pltpu.make_async_remote_copy(
            src_ref=ens.at[first : first + CAP, :, :, tile(q)],
            dst_ref=ext.at[lands : lands + CAP, :, q, rows],
            send_sem=dom_out_sem.at[int(up), q],
            recv_sem=dom_in_sem.at[int(up), q],
            device_id=(to, me),
            device_id_type=MESH,
        )

    @pl.when(k < doms - 1)
    def _():
        for q in range(tiles):
            dom_copy(True, q).start()

    @pl.when(k > 0)
    def _():
        for q in range(tiles):
            dom_copy(False, q).start()

    def clear(ref, count):
        @pl.loop(0, count)
        def _(i):
            blank = jnp.zeros(ref.shape[1:-2] + (8, LANES), jnp.float32)
            ref[i, ..., TOP - 8 : TOP, :] = blank
            ref[i, ..., TOP + ny : TOP + ny + 8, :] = blank

    clear(own, pd)
    clear(ext, 2 * CAP)
    clear(h0, pd)
    for ref in (s1, s2, b0, b1, b2):
        clear(ref, ref.shape[0])

    for copy in loads:
        copy.wait()

    y_of = lax.broadcasted_iota(jnp.int32, (1, ny, LANES), 1).astype(jnp.float32)
    turn = 2.0 * (0.2 + 0.6 * y_of / ny)

    def ground(levels, observed, wet_ref, depth_ref, pull_ref):
        wet_ref[...] = jnp.where(levels > 0, 0.1, 0.0).astype(jnp.float32)
        depth_ref[0] = 1.25 * levels
        depth_ref[1] = 0.25 * levels
        pull_ref[0] = 0.5 * observed
        pull_ref[1] = 0.1 * observed

    ground(lv[...].astype(jnp.float32), ov[...], gw, gd, go)

    def from_own(j):
        return jnp.clip(anc[k * pd + j] - k * pd, 0, pd - 1)

    def from_ext(j, low):
        parent = anc[k * pd + j]
        if low:
            return jnp.where(k == 0, j, jnp.clip(parent - (k * pd - CAP), 0, CAP - 1))
        return jnp.where(
            k == doms - 1, j - (pd - 2 * CAP), jnp.clip(parent - (k + 1) * pd, 0, CAP - 1) + CAP
        )

    @pl.loop(CAP, pd - CAP)
    def _(j):
        h0[j, :, rows] = 5.0 * (own[from_own(j), H_, :, rows] + pv[j])

    def column(ref, i, j, q):
        return jnp.concatenate(
            [ref[i, E_ : N_ + 1, q, rows], h0[j, q, rows][None], ref[i, C_:, q, rows]], axis=0
        )

    lane = lane_of((1, 1, LANES))
    half = lax.rem(lane, 64)

    def packed(ref, i, j, at, to_left, to_right):
        chosen = (lane >= at) & (lane < at + EDGE)
        to_left = jnp.where(chosen, pltpu.roll(column(ref, i, j, 0), at, 2), to_left)
        to_right = jnp.where(chosen, pltpu.roll(column(ref, i, j, tiles - 1), at + EDGE, 2), to_right)
        return to_left, to_right

    def message(second, rightward):
        src, dst = (out2, in2) if second else (out1, in1)
        return pltpu.make_async_remote_copy(
            src_ref=src.at[int(rightward)],
            dst_ref=dst.at[int(rightward)],
            send_sem=msg_out_sem.at[int(second), int(rightward)],
            recv_sem=msg_in_sem.at[int(second), int(rightward)],
            device_id=(k, next_space if rightward else prev_space),
            device_id_type=MESH,
        )

    blank = jnp.zeros((4, ny, LANES), jnp.float32)
    for m, pairs in enumerate((8, (early - 16) // 2)):

        def pack(p, carry):
            for s in range(2):
                j = CAP + 16 * m + 2 * p + s
                carry = packed(own, from_own(j), j, 64 * s + 8 * p, *carry)
            return carry

        left, right = lax.fori_loop(0, pairs, pack, (blank, blank))
        out1[0, 4 * m : 4 * m + 4] = left
        out1[1, 4 * m : 4 * m + 4] = right
    for i, field in enumerate((lv[...].astype(jnp.float32), ov[...])):
        out1[0, 8 + i] = jnp.where(half < EDGE, jnp.where(lane < 64, field[:1], pltpu.roll(field[:1], 64, 2)), 0.0)[0]
        end = field[tiles - 1 :]
        out1[1, 8 + i] = jnp.where(
            half < EDGE, jnp.where(lane < 64, pltpu.roll(end, EDGE, 2), pltpu.roll(end, 64 + EDGE, 2)), 0.0
        )[0]
    message(False, False).start()
    message(False, True).start()

    def unit(slots, src, where):
        for step in range(STEPS):
            last = step == STEPS - 1
            old, new = (None, s1) if step == 0 else (s1, s2) if step == 1 else (s2, s1)
            now = pl.ds(TOP, ny)

            def reader(ref, s):
                return lambda field, up: ref[s, field, :, pl.ds(TOP + up, ny)]

            def first_reader(s):
                return lambda field, up: (
                    h0[slots[s], :, pl.ds(TOP + up, ny)]
                    if field == H_
                    else src[where[s], field, :, pl.ds(TOP + up, ny)]
                )

            read = [first_reader(s) if step == 0 else reader(old, s) for s in range(UNIT)]
            for s in range(UNIT):
                e, n = flow(read[s], gw[...], turn, True)
                new[s, E_, :, now] = e
                new[s, N_, :, now] = n
                if last:
                    out[slots[s], E_] = e
                    out[slots[s], N_] = n
            for s in range(UNIT):
                h, c = level(read[s], reader(new, s), gd[int(last)], go[int(last)], last, True)
                if last:
                    out[slots[s], H_] = h
                    out[slots[s], C_] = c
                else:
                    new[s, H_, :, now] = h
                    new[s, C_, :, now] = c

    @pl.loop(0, early // UNIT)
    def _(i):
        slots = [CAP + i * UNIT + s for s in range(UNIT)]
        unit(slots, own, [from_own(j) for j in slots])

    late = [0, 1, pd - 2, pd - 1]

    @pl.when(k > 0)
    def _():
        for q in range(tiles):
            dom_copy(True, q).wait_recv()

    @pl.when(k < doms - 1)
    def _():
        for q in range(tiles):
            dom_copy(False, q).wait_recv()

    @pl.when(k == 0)
    def _():
        for s in range(CAP):
            ext[s, :, :, rows] = own[from_own(late[s]), :, :, rows]

    @pl.when(k == doms - 1)
    def _():
        for s in range(CAP, 2 * CAP):
            ext[s, :, :, rows] = own[from_own(late[s]), :, :, rows]

    late_from = [from_ext(j, j < CAP) for j in late]
    left, right = blank, blank
    for t, j in enumerate(late):
        h0[j, :, rows] = 5.0 * (ext[late_from[t], H_, :, rows] + pv[j])
    for t, j in enumerate(late):
        left, right = packed(ext, late_from[t], j, 64 * (t % 2) + 8 * (t // 2), left, right)
    out2[0] = left
    out2[1] = right
    message(True, False).start()
    message(True, True).start()
    unit(late, ext, late_from)

    message(False, False).wait_recv()
    message(False, True).wait_recv()

    def ends(first, final, s, tile_so_far):
        base = 64 * s
        inner = (lane >= base + EDGE) & (lane < base + 3 * EDGE)
        tile_so_far = jnp.where(inner, pltpu.roll(first, base + EDGE, 2), tile_so_far)
        inner = (lane >= base + 32) & (lane < base + 32 + 2 * EDGE)
        return jnp.where(inner, pltpu.roll(final, (base + 32 + 2 * EDGE) % LANES, 2), tile_so_far)

    def beyond(from_left, from_right, p):
        shift_left = (LANES - 8 * p) % LANES if isinstance(p, int) else lax.rem(LANES - 8 * p, LANES)
        shift_right = (LANES + 44 - 8 * p) % LANES if isinstance(p, int) else lax.rem(LANES + 44 - 8 * p, LANES)
        got = jnp.where(half < EDGE, pltpu.roll(from_left, shift_left, 2), 0.0)
        return jnp.where((half >= 44) & (half < 44 + EDGE), pltpu.roll(from_right, shift_right, 2), got)

    fields = []
    for i, field in enumerate((lv[...].astype(jnp.float32), ov[...])):
        got = beyond(in1[1, 8 + i][None], in1[0, 8 + i][None], 0)
        for s in range(2):
            got = ends(field[:1], field[tiles - 1 :], s, got)
        fields.append(got[0])
    gs[0] = jnp.where(fields[0] > 0, 0.1, 0.0).astype(jnp.float32)
    gs[1] = 1.25 * fields[0]
    gs[2] = 0.25 * fields[0]
    gs[3] = 0.5 * fields[1]
    gs[4] = 0.1 * fields[1]

    def strips(chunk_pairs):
        now = pl.ds(TOP, ny)
        for p, (got, slots) in enumerate(chunk_pairs):
            for s, (src, where, j) in enumerate(slots):
                got = ends(column(src, where, j, 0), column(src, where, j, tiles - 1), s, got)
            b0[:, p, now] = got

        def reader(ref):
            return lambda field, up: ref[field, :, pl.ds(TOP + up, ny)]

        for step in range(STEPS):
            last = step == STEPS - 1
            old, new = ((b0, b1), (b1, b2), (b2, b0))[step]
            e, n = flow(reader(old), gs[0][None], turn, False)
            new[E_, :, now] = e
            new[N_, :, now] = n
            depth, pull = (gs[2], gs[4]) if last else (gs[1], gs[3])
            h, c = level(reader(old), reader(new), depth[None], pull[None], last, False)
            new[H_, :, now] = h
            new[C_, :, now] = c
        for p, (_, slots) in enumerate(chunk_pairs):
            done = b0[:, p, now]
            for s, (_, _, j) in enumerate(slots):
                base = 64 * s
                at_left = pltpu.roll(done, LANES - EDGE - base, 2)
                at_right = pltpu.roll(done, (LANES - EDGE - (base + 32 + EDGE)) % LANES, 2)
                on = jnp.broadcast_to(lane < EDGE, done.shape)
                pltpu.store(out.at[j, :, 0], at_left, mask=on)
                on = jnp.broadcast_to(lane >= LANES - EDGE, done.shape)
                pltpu.store(out.at[j, :, tiles - 1], at_right, mask=on)

    def early_pair(m, p_in_message, first_slot):
        got = beyond(in1[1, pl.ds(4 * m, 4)], in1[0, pl.ds(4 * m, 4)], p_in_message)
        return got, [(own, from_own(first_slot + s), first_slot + s) for s in range(2)]

    @pl.loop(0, early // 8)
    def _(c):
        strips([early_pair(c // 2, 4 * lax.rem(c, 2) + p, CAP + 8 * c + 2 * p) for p in range(4)])

    message(True, False).wait_recv()
    message(True, True).wait_recv()
    done = early // 8 * 8
    mixed = [early_pair(1, (done - 16) // 2 + p, CAP + done + 2 * p) for p in range(2)]
    for p in range(2):
        got = beyond(in2[1], in2[0], p)
        mixed.append((got, [(ext, late_from[2 * p + s], late[2 * p + s]) for s in range(2)]))
    strips(mixed)

    for second in (False, True):
        for rightward in (False, True):
            message(second, rightward).wait_send()

    @pl.when(k < doms - 1)
    def _():
        for q in range(tiles):
            dom_copy(True, q).wait_send()

    @pl.when(k > 0)
    def _():
        for q in range(tiles):
            dom_copy(False, q).wait_send()


def put_out(made, out, sem):
    copies = [
        pltpu.make_async_copy(made.at[:, :, q], out.at[:, :, :, pl.ds(q * LANES, LANES)], sem.at[q])
        for q in range(made.shape[2])
    ]
    for copy in copies:
        copy.start()
    for copy in copies:
        copy.wait()


def local(ensemble, ancestors, perturbation, levels, observed):
    pd, nf, ny, nx = ensemble.shape
    tiles = nx // LANES
    f32 = jnp.float32
    hbm = pl.BlockSpec(memory_space=pltpu.HBM)
    made = pl.pallas_call(
        kernel,
        out_shape=pltpu.VMEM((pd, nf, tiles, ny, LANES), f32),
        in_specs=[pl.BlockSpec(memory_space=pltpu.SMEM), hbm, hbm, hbm, hbm],
        out_specs=pl.BlockSpec(memory_space=pltpu.VMEM),
        scratch_shapes=[
            pltpu.VMEM((pd, nf, tiles, PITCH, LANES), f32),
            pltpu.VMEM((2 * CAP, nf, tiles, PITCH, LANES), f32),
            pltpu.VMEM((pd, tiles, PITCH, LANES), f32),
            pltpu.VMEM((pd, tiles, ny, LANES), f32),
            pltpu.VMEM((tiles, ny, LANES), jnp.int32),
            pltpu.VMEM((tiles, ny, LANES), f32),
            pltpu.VMEM((tiles, ny, LANES), f32),
            pltpu.VMEM((2, tiles, ny, LANES), f32),
            pltpu.VMEM((2, tiles, ny, LANES), f32),
            pltpu.VMEM((UNIT, nf, tiles, PITCH, LANES), f32),
            pltpu.VMEM((UNIT, nf, tiles, PITCH, LANES), f32),
            pltpu.VMEM((2, 10, ny, LANES), f32),
            pltpu.VMEM((2, nf, ny, LANES), f32),
            pltpu.VMEM((2, 10, ny, LANES), f32),
            pltpu.VMEM((2, nf, ny, LANES), f32),
            pltpu.VMEM((5, ny, LANES), f32),
            pltpu.VMEM((nf, 4, PITCH, LANES), f32),
            pltpu.VMEM((nf, 4, PITCH, LANES), f32),
            pltpu.VMEM((nf, 4, PITCH, LANES), f32),
            pltpu.SemaphoreType.DMA((4, tiles)),
            pltpu.SemaphoreType.DMA((2, tiles)),
            pltpu.SemaphoreType.DMA((2, tiles)),
            pltpu.SemaphoreType.DMA((2, 2)),
            pltpu.SemaphoreType.DMA((2, 2)),
        ],
        compiler_params=pltpu.CompilerParams(
            collective_id=0, has_side_effects=True, vmem_limit_bytes=40 * 1024 * 1024
        ),
        name="resample_and_step",
    )(*(pltpu.with_memory_space_constraint(x, pltpu.HBM) for x in (ancestors, ensemble, perturbation, levels, observed)))
    return pl.pallas_call(
        put_out,
        out_shape=jax.ShapeDtypeStruct((pd, nf, ny, nx), f32),
        in_specs=[pl.BlockSpec(memory_space=pltpu.VMEM)],
        out_specs=hbm,
        scratch_shapes=[pltpu.SemaphoreType.DMA((tiles,))],
        compiler_params=pltpu.CompilerParams(vmem_limit_bytes=16 * 1024 * 1024),
        name="put_out",
    )(made)


def solution(mesh):
    return jax.shard_map(
        local,
        mesh=mesh,
        in_specs=(
            P("dom", None, None, "space"),
            P(),
            P("dom", None, "space"),
            P(None, "space"),
            P(None, "space"),
        ),
        out_specs=P("dom", None, None, "space"),
        check_vma=False,
    )
```

```python
import functools

import jax
import jax.numpy as jnp
from jax import lax
from jax.experimental import pallas as pl
from jax.experimental.pallas import tpu as pltpu
from jax.sharding import PartitionSpec as P

MESH = pl.DeviceIdType.MESH
STEPS = 3
CAP = 2
EDGE = 2 * STEPS
LANES = 128
TOP = 8
PITCH = 32
UNIT = 4
HALF = 8
E_, N_, H_, C_ = range(4)


def lane_of(shape):
    return lax.broadcasted_iota(jnp.int32, shape, len(shape) - 1)


def east(cells, joined):
    turned = pltpu.roll(cells, LANES - 1, 2)
    if not joined:
        return turned
    following = jnp.concatenate([turned[1:], turned[:1]], axis=0)
    return jnp.where(lane_of(cells.shape) == LANES - 1, following, turned)


def west(cells, joined):
    turned = pltpu.roll(cells, 1, 2)
    if not joined:
        return turned
    preceding = jnp.concatenate([turned[-1:], turned[:-1]], axis=0)
    return jnp.where(lane_of(cells.shape) == 0, preceding, turned)


def flow(read, wet, turn, joined):
    e, n, h = read(E_, 0), read(N_, 0), read(H_, 0)
    e_new = wet * (
        (5.5 * e + turn * n)
        + (read(E_, 1) + read(E_, -1))
        + (east(e - h, joined) + west(e + h, joined))
    )
    n_new = wet * (
        (5.5 * n - turn * e)
        + (east(n, joined) + west(n, joined))
        + ((read(N_, 1) - read(H_, 1)) + (read(N_, -1) + read(H_, -1)))
    )
    return e_new, n_new


def level(read, read_new, depth, pull, last, joined):
    e, n = read_new(E_, 0), read_new(N_, 0)
    spread = (east(e, joined) - west(e, joined)) + (read_new(N_, 1) - read_new(N_, -1))
    h_new = ((0.18 if last else 0.9) * read(H_, 0) + pull) - depth * spread
    c = read(C_, 0)
    c_east, c_west = east(c, joined), west(c, joined)
    c_north, c_south = read(C_, 1), read(C_, -1)
    c_new = (
        (6.0 * c + ((c_east + c_west) + (c_north + c_south)))
        - e * (c_east - c_west)
        - n * (c_north - c_south)
    )
    if last:
        c_new = 0.001 * c_new
    return h_new, c_new


def level_of(levels, observed):
    return (
        jnp.where(levels > 0, 0.1, 0.0).astype(jnp.float32),
        1.25 * levels,
        0.25 * levels,
        0.5 * observed,
        0.1 * observed,
    )


def turn_of(ny, y0):
    y = lax.broadcasted_iota(jnp.int32, (1, HALF, LANES), 1).astype(jnp.float32) + float(y0)
    return 2.0 * (0.2 + 0.6 * y / ny)


def kernel(
    anc, ens, pert, lev, obs, out, b0, gs,
    own, ext, h0, pv, lv, ov, gw, gd, go, s1, s2, out1, in1, edge_out, edge_in,
    in_sem, dom_out_sem, dom_in_sem, msg_out_sem, msg_in_sem, edge_out_sem, edge_in_sem,
):
    pd = ens.shape[0]
    ny = ens.shape[2]
    tiles = ens.shape[3] // LANES
    doms, spaces = lax.axis_size("dom"), lax.axis_size("space")
    k, me = lax.axis_index("dom"), lax.axis_index("space")
    prev_space, next_space = lax.rem(me + spaces - 1, spaces), lax.rem(me + 1, spaces)
    early = pd - 2 * CAP
    rows = slice(TOP, TOP + ny)

    barrier = pltpu.get_barrier_semaphore()


    def greet(dom, *spaces_there):
        for space in spaces_there:
            pl.semaphore_signal(barrier, inc=1, device_id=(dom, space), device_id_type=MESH)

    greet(k, prev_space, next_space)

    @pl.when(k > 0)
    def _():
        greet(k - 1, me, prev_space, next_space)

    @pl.when(k < doms - 1)
    def _():
        greet(k + 1, me, prev_space, next_space)

    def tile(q):
        return pl.ds(q * LANES, LANES)

    loads = []
    for q in range(tiles):
        loads.append(pltpu.make_async_copy(lev.at[:, tile(q)], lv.at[q], in_sem.at[0, q]))
        loads.append(pltpu.make_async_copy(obs.at[:, tile(q)], ov.at[q], in_sem.at[1, q]))
        loads.append(pltpu.make_async_copy(pert.at[:, :, tile(q)], pv.at[:, q], in_sem.at[2, q]))
        loads.append(pltpu.make_async_copy(ens.at[:, :, :, tile(q)], own.at[:, :, q, rows], in_sem.at[3, q]))
    for copy in loads:
        copy.start()

    def clear(ref, count):
        @pl.loop(0, count)
        def _(i):
            blank = jnp.zeros(ref.shape[1:-2] + (8, LANES), jnp.float32)
            ref[i, ..., TOP - 8 : TOP, :] = blank
            ref[i, ..., TOP + ny : TOP + ny + 8, :] = blank

    for ref in (own, ext, h0, s1, s2, b0):
        clear(ref, ref.shape[0])

    for copy in loads:
        copy.wait()

    gw[...], gd[0], gd[1], go[0], go[1] = level_of(lv[...].astype(jnp.float32), ov[...])

    def from_own(j):
        return jnp.clip(anc[k * pd + j] - k * pd, 0, pd - 1)

    def from_ext(j, low):
        parent = anc[k * pd + j]
        if low:
            return jnp.where(k == 0, j, jnp.clip(parent - (k * pd - CAP), 0, CAP - 1))
        return jnp.where(
            k == doms - 1, j - (pd - 2 * CAP), jnp.clip(parent - (k + 1) * pd, 0, CAP - 1) + CAP
        )

    @pl.loop(0, early // UNIT)
    def _(i):
        for s in range(UNIT):
            j = CAP + i * UNIT + s
            h0[j, :, rows] = 5.0 * (own[from_own(j), H_, :, rows] + pv[j])

    def column(ref, i, j, q):
        return jnp.concatenate(
            [ref[i, E_ : N_ + 1, q, rows], h0[j, q, rows][None], ref[i, C_:, q, rows]], axis=0
        )

    lane = lane_of((1, 1, LANES))
    half = lax.rem(lane, 64)

    def packed(ref, i, j, at, to_left, to_right):
        chosen = (lane >= at) & (lane < at + EDGE)
        to_left = jnp.where(chosen, pltpu.roll(column(ref, i, j, 0), at, 2), to_left)
        to_right = jnp.where(chosen, pltpu.roll(column(ref, i, j, tiles - 1), at + EDGE, 2), to_right)
        return to_left, to_right

    def message(rightward):
        return pltpu.make_async_remote_copy(
            src_ref=out1.at[int(rightward)],
            dst_ref=in1.at[int(rightward)],
            send_sem=msg_out_sem.at[int(rightward)],
            recv_sem=msg_in_sem.at[int(rightward)],
            device_id=(k, next_space if rightward else prev_space),
            device_id_type=MESH,
        )

    edge_to = (jnp.where(k < doms - 1, k + 1, k), jnp.where(k > 0, k - 1, k))
    edge_side = (jnp.where(k < doms - 1, 0, 1), jnp.where(k > 0, 1, 0))

    def edge_particle(up, t):
        if up:
            return jnp.where(k < doms - 1, pd - CAP + t, from_own(pd - CAP + t))
        return jnp.where(k > 0, t, from_own(t))

    def edge_message(up, rightward):
        at = 0 if up else 1
        return pltpu.make_async_remote_copy(
            src_ref=edge_out.at[at, int(rightward)],
            dst_ref=edge_in.at[edge_side[at], int(rightward)],
            send_sem=edge_out_sem.at[at, int(rightward)],
            recv_sem=edge_in_sem.at[edge_side[at], int(rightward)],
            device_id=(edge_to[at], next_space if rightward else prev_space),
            device_id_type=MESH,
        )

    def edge_arrival(side, rightward):
        return pltpu.make_async_remote_copy(
            src_ref=edge_out.at[side, int(rightward)],
            dst_ref=edge_in.at[side, int(rightward)],
            send_sem=edge_out_sem.at[side, int(rightward)],
            recv_sem=edge_in_sem.at[side, int(rightward)],
            device_id=(k, next_space if rightward else prev_space),
            device_id_type=MESH,
        )

    blank = jnp.zeros((4, ny, LANES), jnp.float32)
    for m, pairs in enumerate((8, (early - 16) // 2)):

        def pack(i, carry):
            for p in (2 * i, 2 * i + 1):
                for s in range(2):
                    j = CAP + 16 * m + 2 * p + s
                    carry = packed(own, from_own(j), j, 64 * s + 8 * p, *carry)
            return carry

        left, right = lax.fori_loop(0, pairs // 2, pack, (blank, blank))
        out1[0, 4 * m : 4 * m + 4] = left
        out1[1, 4 * m : 4 * m + 4] = right
    late = [pd - 2, pd - 1, 0, 1]
    levels = lv[...].astype(jnp.float32)
    for rightward in range(2):
        q, end = (tiles - 1, EDGE) if rightward else (0, 0)
        got = jnp.zeros((ny, LANES), jnp.float32)
        parts = [(levels[q], at) for at in (0, 64)] + [(ov[q], at) for at in (8, 72)]
        parts += [(5.0 * pv[j, q], 64 * (t % 2) + 16 + 8 * (t // 2)) for t, j in enumerate(late)]
        for part, at in parts:
            got = jnp.where((lane[0] >= at) & (lane[0] < at + EDGE), pltpu.roll(part, at + end, 1), got)
        out1[rightward, 8] = got
        for up in (True, False):
            for t in range(CAP):
                i = edge_particle(up, t)
                got = jnp.zeros((ny, LANES), jnp.float32)
                for f in range(4):
                    part = own[i, f, q, rows]
                    if f == H_:
                        part = 5.0 * part
                    at = 8 * f
                    got = jnp.where((lane[0] >= at) & (lane[0] < at + EDGE), pltpu.roll(part, at + end, 1), got)
                edge_out[0 if up else 1, rightward, t] = got + pltpu.roll(got, 64, 1)

    def unit(slots, src, where):
        for step in range(STEPS):
            last = step == STEPS - 1
            old, new = (None, s1) if step == 0 else (s1, s2) if step == 1 else (s2, s1)

            def reader(ref, s, y0):
                return lambda field, up: ref[s, field, :, pl.ds(TOP + y0 + up, HALF)]

            def first_reader(s, y0):
                return lambda field, up: (
                    h0[slots[s], :, pl.ds(TOP + y0 + up, HALF)]
                    if field == H_
                    else src[where[s], field, :, pl.ds(TOP + y0 + up, HALF)]
                )

            def read(s, y0):
                return first_reader(s, y0) if step == 0 else reader(old, s, y0)

            for s in range(UNIT):
                for y0 in range(0, ny, HALF):
                    e, n = flow(read(s, y0), gw[:, pl.ds(y0, HALF)], turn_of(ny, y0), True)
                    now = pl.ds(TOP + y0, HALF)
                    new[s, E_, :, now] = e
                    new[s, N_, :, now] = n
                    if last:
                        out[slots[s], E_, :, pl.ds(y0, HALF)] = e
                        out[slots[s], N_, :, pl.ds(y0, HALF)] = n
            for s in range(UNIT):
                for y0 in range(0, ny, HALF):
                    there = pl.ds(y0, HALF)
                    h, c = level(
                        read(s, y0), reader(new, s, y0), gd[int(last), :, there], go[int(last), :, there], last, True
                    )
                    if last:
                        out[slots[s], H_, :, there] = h
                        out[slots[s], C_, :, there] = c
                    else:
                        now = pl.ds(TOP + y0, HALF)
                        new[s, H_, :, now] = h
                        new[s, C_, :, now] = c

    def early_unit(i):
        slots = [CAP + i * UNIT + s for s in range(UNIT)]
        unit(slots, own, [from_own(j) for j in slots])

    pl.semaphore_wait(barrier, 2 + jnp.where(k > 0, 3, 0) + jnp.where(k < doms - 1, 3, 0))

    def dom_copy(up, q):
        first, lands, to = (pd - CAP, 0, k + 1) if up else (0, CAP, k - 1)
        return pltpu.make_async_remote_copy(
            src_ref=ens.at[first : first + CAP, :, :, tile(q)],
            dst_ref=ext.at[lands : lands + CAP, :, q, rows],
            send_sem=dom_out_sem.at[int(up), q],
            recv_sem=dom_in_sem.at[int(up), q],
            device_id=(to, me),
            device_id_type=MESH,
        )

    def send_particles(up, on):
        @pl.when(on)
        def _():
            for q in range(tiles):
                dom_copy(up, q).start()

    odd = lax.rem(k, 2) == 1
    send_particles(True, odd & (k < doms - 1))
    send_particles(False, jnp.logical_not(odd) & (k > 0))
    for rightward in (False, True):
        message(rightward).start()
        for up in (False, True):
            edge_message(up, rightward).start()
    send_particles(True, jnp.logical_not(odd))
    send_particles(False, odd)

    pl.loop(0, early // UNIT)(early_unit)

    @pl.when(k > 0)
    def _():
        for q in range(tiles):
            dom_copy(True, q).wait_recv()

    @pl.when(k < doms - 1)
    def _():
        for q in range(tiles):
            dom_copy(False, q).wait_recv()

    @pl.when(k == 0)
    def _():
        for s in range(CAP):
            ext[s, :, :, rows] = own[from_own(s), :, :, rows]

    @pl.when(k == doms - 1)
    def _():
        for s in range(CAP, 2 * CAP):
            ext[s, :, :, rows] = own[from_own(pd - 2 * CAP + s), :, :, rows]

    late_from = [from_ext(j, j < CAP) for j in late]
    for t, j in enumerate(late):
        h0[j, :, rows] = 5.0 * (ext[late_from[t], H_, :, rows] + pv[j])
    unit(late, ext, late_from)

    for rightward in (False, True):
        message(rightward).wait_recv()

    def ends(first, final, s, tile_so_far):
        base = 64 * s
        inner = (lane >= base + EDGE) & (lane < base + 3 * EDGE)
        tile_so_far = jnp.where(inner, pltpu.roll(first, base + EDGE, 2), tile_so_far)
        inner = (lane >= base + 32) & (lane < base + 32 + 2 * EDGE)
        return jnp.where(inner, pltpu.roll(final, (base + 32 + 2 * EDGE) % LANES, 2), tile_so_far)

    def beyond(from_left, from_right, at):
        shift_left = (LANES - at) % LANES if isinstance(at, int) else lax.rem(LANES - at, LANES)
        shift_right = (LANES + 44 - at) % LANES if isinstance(at, int) else lax.rem(LANES + 44 - at, LANES)
        got = jnp.where(half < EDGE, pltpu.roll(from_left, shift_left, 2), 0.0)
        return jnp.where((half >= 44) & (half < 44 + EDGE), pltpu.roll(from_right, shift_right, 2), got)

    fields = []
    for i, field in enumerate((levels, ov[...])):
        got = beyond(in1[1, 8:9], in1[0, 8:9], 8 * i)
        for s in range(2):
            got = ends(field[:1], field[tiles - 1 :], s, got)
        fields.append(got[0])
    gs[0], gs[1], gs[2], gs[3], gs[4] = level_of(*fields)

    def strip(c, p, got, ref, slots):
        for s, (i, j) in enumerate(slots):
            got = ends(column(ref, i, j, 0), column(ref, i, j, tiles - 1), s, got)
        b0[c, :, p, rows] = got

    def early_strip(c, p, m, p_in_message):
        got = beyond(in1[1, pl.ds(4 * m, 4)], in1[0, pl.ds(4 * m, 4)], 8 * p_in_message)
        first = CAP + 8 * c + 2 * p
        strip(c, p, got, own, [(from_own(first + s), first + s) for s in range(2)])

    whole = early // 8

    @pl.loop(0, whole)
    def _(c):
        for p in range(4):
            early_strip(c, p, c // 2, 4 * lax.rem(c, 2) + p)

    for p in range(2):
        early_strip(whole, p, 1, 4 * (whole - 2) + p)
    for side in range(2):
        for rightward in (False, True):
            edge_arrival(side, rightward).wait_recv()
    for p in range(2):
        side = 1 - p
        where = [late_from[2 * p + s] - CAP * side for s in range(2)]
        ways = [jnp.where(lane < 64, *(edge_in[side, w, where[s]][None] for s in range(2))) for w in range(2)]
        got = [beyond(ways[1], ways[0], 8 * f) for f in range(4)]
        got[H_] = got[H_] + beyond(in1[1, 8:9], in1[0, 8:9], 16 + 8 * p)
        slots = [(late_from[2 * p + s], late[2 * p + s]) for s in range(2)]
        strip(whole, 2 + p, jnp.concatenate(got, axis=0), ext, slots)

    for rightward in (False, True):
        message(rightward).wait_send()
        for up in (False, True):
            edge_message(up, rightward).wait_send()

    @pl.when(k < doms - 1)
    def _():
        for q in range(tiles):
            dom_copy(True, q).wait_send()

    @pl.when(k > 0)
    def _():
        for q in range(tiles):
            dom_copy(False, q).wait_send()


def finish(made, b0, gs, out, b1, b2, b3, sides, inner_sem, side_sem):
    pd, nf, tiles, ny, _ = made.shape
    lane = lane_of((1, 1, LANES))
    inner = [
        pltpu.make_async_copy(made.at[:, :, q], out.at[:, :, :, pl.ds(q * LANES, LANES)], inner_sem.at[q])
        for q in range(1, tiles - 1)
    ]
    for copy in inner:
        copy.start()

    for ref in (b1, b2, b3):
        blank = jnp.zeros(ref.shape[:-2] + (8, LANES), jnp.float32)
        ref[..., TOP - 8 : TOP, :] = blank
        ref[..., TOP + ny : TOP + ny + 8, :] = blank

    def leave(c, side, part):
        first, count = (CAP + 8 * c, 6) if part == 0 else (lax.rem(CAP + 8 * c + 6, pd), 2)
        at = side * (tiles - 1) * LANES
        return pltpu.make_async_copy(
            sides.at[side, pl.ds(first, count)],
            out.at[pl.ds(first, count), :, :, pl.ds(at, LANES)],
            side_sem.at[c, side, part],
        )

    def chunk(c):
        def reader(ref, y0):
            if ref is b0:
                return lambda field, up: ref[c, field, :, pl.ds(TOP + y0 + up, HALF)]
            return lambda field, up: ref[field, :, pl.ds(TOP + y0 + up, HALF)]

        for step in range(STEPS):
            last = step == STEPS - 1
            old, new = ((b0, b1), (b1, b2), (b2, b3))[step]
            for y0 in range(0, ny, HALF):
                now = pl.ds(TOP + y0, HALF)
                e, n = flow(reader(old, y0), gs[0, pl.ds(y0, HALF)][None], turn_of(ny, y0), False)
                new[E_, :, now] = e
                new[N_, :, now] = n
            depth, pull = (gs[2], gs[4]) if last else (gs[1], gs[3])
            for y0 in range(0, ny, HALF):
                now = pl.ds(TOP + y0, HALF)
                h, c_new = level(
                    reader(old, y0), reader(new, y0), depth[None, y0 : y0 + HALF], pull[None, y0 : y0 + HALF], last, False
                )
                new[H_, :, now] = h
                new[C_, :, now] = c_new
        for p in range(4):
            done = b3[:, p, TOP : TOP + ny]
            for s in range(2):
                base = 64 * s
                j = lax.rem(CAP + 8 * c + 2 * p + s, pd)
                at_left = pltpu.roll(done, LANES - EDGE - base, 2)
                at_right = pltpu.roll(done, (LANES - EDGE - (base + 32 + EDGE)) % LANES, 2)
                sides[0, j] = jnp.where(lane < EDGE, at_left, made[j, :, 0])
                sides[1, j] = jnp.where(lane >= LANES - EDGE, at_right, made[j, :, tiles - 1])
        for side in range(2):
            for part in range(2):
                leave(c, side, part).start()

    pl.loop(0, pd // 8)(chunk)

    for copy in inner:
        copy.wait()

    @pl.loop(0, pd // 8)
    def _(c):
        for side in range(2):
            for part in range(2):
                leave(c, side, part).wait()


def local(ensemble, ancestors, perturbation, levels, observed):
    pd, nf, ny, nx = ensemble.shape
    tiles = nx // LANES
    f32 = jnp.float32
    hbm = pl.BlockSpec(memory_space=pl.ANY)
    vmem = pl.BlockSpec(memory_space=pltpu.VMEM)
    made, strips, ground = pl.pallas_call(
        kernel,
        out_shape=[
            pltpu.VMEM((pd, nf, tiles, ny, LANES), f32),
            pltpu.VMEM((pd // 8, nf, 4, PITCH, LANES), f32),
            pltpu.VMEM((5, ny, LANES), f32),
        ],
        in_specs=[pl.BlockSpec(memory_space=pltpu.SMEM), hbm, hbm, hbm, hbm],
        out_specs=[vmem, vmem, vmem],
        scratch_shapes=[
            pltpu.VMEM((pd, nf, tiles, PITCH, LANES), f32),
            pltpu.VMEM((2 * CAP, nf, tiles, PITCH, LANES), f32),
            pltpu.VMEM((pd, tiles, PITCH, LANES), f32),
            pltpu.VMEM((pd, tiles, ny, LANES), f32),
            pltpu.VMEM((tiles, ny, LANES), jnp.int32),
            pltpu.VMEM((tiles, ny, LANES), f32),
            pltpu.VMEM((tiles, ny, LANES), f32),
            pltpu.VMEM((2, tiles, ny, LANES), f32),
            pltpu.VMEM((2, tiles, ny, LANES), f32),
            pltpu.VMEM((UNIT, nf, tiles, PITCH, LANES), f32),
            pltpu.VMEM((UNIT, nf, tiles, PITCH, LANES), f32),
            pltpu.VMEM((2, 9, ny, LANES), f32),
            pltpu.VMEM((2, 9, ny, LANES), f32),
            pltpu.VMEM((2, 2, CAP, ny, LANES), f32),
            pltpu.VMEM((2, 2, CAP, ny, LANES), f32),
            pltpu.SemaphoreType.DMA((4, tiles)),
            pltpu.SemaphoreType.DMA((2, tiles)),
            pltpu.SemaphoreType.DMA((2, tiles)),
            pltpu.SemaphoreType.DMA((2,)),
            pltpu.SemaphoreType.DMA((2,)),
            pltpu.SemaphoreType.DMA((2, 2)),
            pltpu.SemaphoreType.DMA((2, 2)),
        ],
        compiler_params=pltpu.CompilerParams(
            collective_id=0, has_side_effects=True, vmem_limit_bytes=40 * 1024 * 1024
        ),
        name="resample_and_step",
    )(*(pltpu.with_memory_space_constraint(x, pltpu.HBM) for x in (ancestors, ensemble, perturbation, levels, observed)))
    return pl.pallas_call(
        finish,
        out_shape=jax.ShapeDtypeStruct((pd, nf, ny, nx), f32),
        in_specs=[vmem, vmem, vmem],
        out_specs=hbm,
        scratch_shapes=[
            pltpu.VMEM((nf, 4, PITCH, LANES), f32),
            pltpu.VMEM((nf, 4, PITCH, LANES), f32),
            pltpu.VMEM((nf, 4, PITCH, LANES), f32),
            pltpu.VMEM((2, pd, nf, ny, LANES), f32),
            pltpu.SemaphoreType.DMA((tiles,)),
            pltpu.SemaphoreType.DMA((pd // 8, 2, 2)),
        ],
        compiler_params=pltpu.CompilerParams(vmem_limit_bytes=24 * 1024 * 1024),
        name="finish",
    )(made, strips, ground)


def solution(mesh):
    return jax.shard_map(
        local,
        mesh=mesh,
        in_specs=(
            P("dom", None, None, "space"),
            P(),
            P("dom", None, "space"),
            P(None, "space"),
            P(None, "space"),
        ),
        out_specs=P("dom", None, None, "space"),
        check_vma=False,
    )
```

```python
import functools

import jax
import jax.numpy as jnp
from jax import lax
from jax.experimental import pallas as pl
from jax.experimental.pallas import tpu as pltpu
from jax.sharding import PartitionSpec as P

MESH = pl.DeviceIdType.MESH
STEPS = 3
CAP = 2
EDGE = 2 * STEPS
LANES = 128
TOP = 8
PITCH = 32
UNIT = 4
HALF = 8
PAIRS = 7
E_, N_, H_, C_ = range(4)


def lane_of(shape):
    return lax.broadcasted_iota(jnp.int32, shape, len(shape) - 1)


def east(cells, joined):
    turned = pltpu.roll(cells, LANES - 1, 2)
    if not joined:
        return turned
    following = jnp.concatenate([turned[1:], turned[:1]], axis=0)
    return jnp.where(lane_of(cells.shape) == LANES - 1, following, turned)


def west(cells, joined):
    turned = pltpu.roll(cells, 1, 2)
    if not joined:
        return turned
    preceding = jnp.concatenate([turned[-1:], turned[:-1]], axis=0)
    return jnp.where(lane_of(cells.shape) == 0, preceding, turned)


def flow(read, wet, turn, joined):
    e, n, h = read(E_, 0), read(N_, 0), read(H_, 0)
    e_new = wet * (
        (5.5 * e + turn * n)
        + (read(E_, 1) + read(E_, -1))
        + (east(e - h, joined) + west(e + h, joined))
    )
    n_new = wet * (
        (5.5 * n - turn * e)
        + (east(n, joined) + west(n, joined))
        + ((read(N_, 1) - read(H_, 1)) + (read(N_, -1) + read(H_, -1)))
    )
    return e_new, n_new


def level(read, read_new, depth, pull, last, joined):
    e, n = read_new(E_, 0), read_new(N_, 0)
    spread = (east(e, joined) - west(e, joined)) + (read_new(N_, 1) - read_new(N_, -1))
    h_new = ((0.18 if last else 0.9) * read(H_, 0) + pull) - depth * spread
    c = read(C_, 0)
    c_east, c_west = east(c, joined), west(c, joined)
    c_north, c_south = read(C_, 1), read(C_, -1)
    c_new = (
        (6.0 * c + ((c_east + c_west) + (c_north + c_south)))
        - e * (c_east - c_west)
        - n * (c_north - c_south)
    )
    if last:
        c_new = 0.001 * c_new
    return h_new, c_new


def level_of(levels, observed):
    return (
        jnp.where(levels > 0, 0.1, 0.0).astype(jnp.float32),
        1.25 * levels,
        0.25 * levels,
        0.5 * observed,
        0.1 * observed,
    )


def turn_of(ny, y0):
    y = lax.broadcasted_iota(jnp.int32, (1, HALF, LANES), 1).astype(jnp.float32) + float(y0)
    return 2.0 * (0.2 + 0.6 * y / ny)


def all_steps(first, s1, s2, ground, keep, joined, ny, parts):
    wet, depth, pull = ground
    count = len(parts)
    for step in range(STEPS):
        last = step == STEPS - 1
        old, new = (None, s1) if step == 0 else (s1, s2) if step == 1 else (s2, s1)

        def reader(ref, i, y0):
            return lambda field, up: parts[i](ref, field, pl.ds(TOP + y0 + up, HALF))[...]

        def read(i, y0):
            return (lambda field, up: first(i, field, y0, up)) if step == 0 else reader(old, i, y0)

        for i in range(count):
            for y0 in range(0, ny, HALF):
                e, n = flow(read(i, y0), wet(y0), turn_of(ny, y0), joined)
                now = pl.ds(TOP + y0, HALF)
                parts[i](new, E_, now)[...] = e
                parts[i](new, N_, now)[...] = n
                if last:
                    keep(i, E_, y0, e)
                    keep(i, N_, y0, n)
        for i in range(count):
            for y0 in range(0, ny, HALF):
                h, c = level(read(i, y0), reader(new, i, y0), depth(last, y0), pull(last, y0), last, joined)
                now = pl.ds(TOP + y0, HALF)
                if last:
                    keep(i, H_, y0, h)
                    keep(i, C_, y0, c)
                else:
                    parts[i](new, H_, now)[...] = h
                    parts[i](new, C_, now)[...] = c


def slot_parts():
    return [lambda ref, field, now, s=s: ref.at[s, field, :, now] for s in range(UNIT)]


def row_ground(gw, gd, go):
    return (
        lambda y0: gw[:, pl.ds(y0, HALF)],
        lambda last, y0: gd[int(last), :, pl.ds(y0, HALF)],
        lambda last, y0: go[int(last), :, pl.ds(y0, HALF)],
    )


def strip_ground(gs):
    return (
        lambda y0: gs[0, pl.ds(y0, HALF)][None],
        lambda last, y0: gs[2 if last else 1, pl.ds(y0, HALF)][None],
        lambda last, y0: gs[4 if last else 3, pl.ds(y0, HALF)][None],
    )


def step_strips(b0, b1, b2, b3, gs, groups, ny):
    parts = [lambda ref, field, now, g=g: ref.at[field, g, now] for g in groups]

    def keep(i, field, y0, value):
        b3[field, groups[i], pl.ds(y0, HALF)] = value

    all_steps(
        lambda i, field, y0, up: b0[field, groups[i], pl.ds(TOP + y0 + up, HALF)],
        b1, b2, strip_ground(gs), keep, False, ny, parts,
    )


def put_strips(b3, p, slots, out):
    done = b3[:, p]
    lane = lane_of(done.shape)
    final = out.shape[2] - 1
    for s, j in enumerate(slots):
        base = 64 * s
        at_left = pltpu.roll(done, LANES - EDGE - base, 2)
        at_right = pltpu.roll(done, (LANES - EDGE - (base + 32 + EDGE)) % LANES, 2)
        pltpu.store(out.at[j, :, 0], at_left, mask=lane < EDGE)
        pltpu.store(out.at[j, :, final], at_right, mask=lane >= LANES - EDGE)


def clear_rows(ref, ny):
    @pl.loop(0, ref.shape[0])
    def _(i):
        blank = jnp.zeros(ref.shape[1:-2] + (8, LANES), jnp.float32)
        ref[i, ..., TOP - 8 : TOP, :] = blank
        ref[i, ..., TOP + ny : TOP + ny + 8, :] = blank


def kernel(
    anc_in, ens, pert, lev, obs, out, late0, late_strips, gs, gw, gd, go,
    anc, ends_of, inner, ext, h0, pv, lv, ov, s1, s2, b0, b1, b2, b3, out1, in1, edge_out, edge_in,
    in_sem, dom_out_sem, dom_in_sem, msg_out_sem, msg_in_sem, edge_out_sem, edge_in_sem,
):
    pd = ens.shape[0]
    ny = ens.shape[2]
    tiles = ens.shape[3] // LANES
    doms, spaces = lax.axis_size("dom"), lax.axis_size("space")
    k, me = lax.axis_index("dom"), lax.axis_index("space")
    prev_space, next_space = lax.rem(me + spaces - 1, spaces), lax.rem(me + 1, spaces)
    early = pd - 2 * CAP
    rows = slice(TOP, TOP + ny)

    barrier = pltpu.get_barrier_semaphore()

    def greet(dom, *spaces_there):
        for space in spaces_there:
            pl.semaphore_signal(barrier, inc=1, device_id=(dom, space), device_id_type=MESH)

    greet(k, prev_space, next_space)

    @pl.when(k > 0)
    def _():
        greet(k - 1, me, prev_space, next_space)

    @pl.when(k < doms - 1)
    def _():
        greet(k + 1, me, prev_space, next_space)

    def tile(q):
        return pl.ds(q * LANES, LANES)

    needed_first, needed_next = [pltpu.make_async_copy(anc_in, anc, in_sem.at[4, 0])], []
    for q in (0, tiles - 1, *range(1, tiles - 1)):
        at_end = q in (0, tiles - 1)
        loads = needed_first if at_end else needed_next
        here = ends_of.at[:, :, int(q > 0), rows] if at_end else inner.at[:, :, q - 1, rows]
        loads.append(pltpu.make_async_copy(ens.at[:, :, :, tile(q)], here, in_sem.at[3, q]))
        loads.append(pltpu.make_async_copy(pert.at[:, :, tile(q)], pv.at[:, q], in_sem.at[2, q]))
        loads.append(pltpu.make_async_copy(lev.at[:, tile(q)], lv.at[q], in_sem.at[0, q]))
        loads.append(pltpu.make_async_copy(obs.at[:, tile(q)], ov.at[q], in_sem.at[1, q]))
    for copy in needed_first + needed_next:
        copy.start()

    for ref in (ends_of, inner, h0, late0, s1, s2, b0, b1, b2, late_strips):
        clear_rows(ref, ny)

    for copy in needed_first:
        copy.wait()

    def from_own(j):
        return jnp.clip(anc[k * pd + j] - k * pd, 0, pd - 1)

    def from_ext(j, low):
        parent = anc[k * pd + j]
        if low:
            return jnp.where(k == 0, j, jnp.clip(parent - (k * pd - CAP), 0, CAP - 1))
        return jnp.where(
            k == doms - 1, j - (pd - 2 * CAP), jnp.clip(parent - (k + 1) * pd, 0, CAP - 1) + CAP
        )

    def column(i, j, side):
        h = 5.0 * (ends_of[i, H_, side, rows] + pv[j, side * (tiles - 1)])
        return jnp.concatenate(
            [ends_of[i, E_ : N_ + 1, side, rows], h[None], ends_of[i, C_:, side, rows]], axis=0
        )

    full = lane_of((4, ny, LANES))
    flat = lane_of((ny, LANES))

    def message(rightward):
        return pltpu.make_async_remote_copy(
            src_ref=out1.at[int(rightward)],
            dst_ref=in1.at[int(rightward)],
            send_sem=msg_out_sem.at[int(rightward)],
            recv_sem=msg_in_sem.at[int(rightward)],
            device_id=(k, next_space if rightward else prev_space),
            device_id_type=MESH,
        )

    edge_to = (jnp.where(k < doms - 1, k + 1, k), jnp.where(k > 0, k - 1, k))
    edge_side = (jnp.where(k < doms - 1, 0, 1), jnp.where(k > 0, 1, 0))

    def edge_particle(up, t):
        if up:
            return jnp.where(k < doms - 1, pd - CAP + t, from_own(pd - CAP + t))
        return jnp.where(k > 0, t, from_own(t))

    def edge_message(up, rightward):
        at = 0 if up else 1
        return pltpu.make_async_remote_copy(
            src_ref=edge_out.at[at, int(rightward)],
            dst_ref=edge_in.at[edge_side[at], int(rightward)],
            send_sem=edge_out_sem.at[at, int(rightward)],
            recv_sem=edge_in_sem.at[edge_side[at], int(rightward)],
            device_id=(edge_to[at], next_space if rightward else prev_space),
            device_id_type=MESH,
        )

    def edge_arrival(side, rightward):
        return pltpu.make_async_remote_copy(
            src_ref=edge_out.at[side, int(rightward)],
            dst_ref=edge_in.at[side, int(rightward)],
            send_sem=edge_out_sem.at[side, int(rightward)],
            recv_sem=edge_in_sem.at[side, int(rightward)],
            device_id=(k, next_space if rightward else prev_space),
            device_id_type=MESH,
        )

    @pl.loop(0, early // (2 * PAIRS))
    def _(m):
        to_left = jnp.zeros((4, ny, LANES), jnp.float32)
        to_right = to_left
        for p in range(PAIRS):
            for s in range(2):
                at = 64 * s + 8 * p
                j = CAP + 2 * (PAIRS * m + p) + s
                i = from_own(j)
                chosen = (full >= at) & (full < at + EDGE)
                to_left = jnp.where(chosen, pltpu.roll(column(i, j, 0), at, 2), to_left)
                to_right = jnp.where(chosen, pltpu.roll(column(i, j, 1), at + EDGE, 2), to_right)
        out1[0, pl.ds(4 * m, 4)] = to_left
        out1[1, pl.ds(4 * m, 4)] = to_right

    late = [pd - 2, pd - 1, 0, 1]
    for rightward in range(2):
        q, end = (tiles - 1, EDGE) if rightward else (0, 0)
        got = jnp.zeros((ny, LANES), jnp.float32)
        parts = [(lv[q].astype(jnp.float32), at) for at in (0, 64)] + [(ov[q], at) for at in (8, 72)]
        parts += [(5.0 * pv[j, q], 64 * (t % 2) + 16 + 8 * (t // 2)) for t, j in enumerate(late)]
        for part, at in parts:
            got = jnp.where((flat >= at) & (flat < at + EDGE), pltpu.roll(part, at + end, 1), got)
        out1[rightward, 8] = got
        for up in (True, False):
            for t in range(CAP):
                i = edge_particle(up, t)
                got = jnp.zeros((ny, LANES), jnp.float32)
                for f in range(4):
                    part = ends_of[i, f, rightward, rows]
                    if f == H_:
                        part = 5.0 * part
                    at = 8 * f
                    got = jnp.where((flat >= at) & (flat < at + EDGE), pltpu.roll(part, at + end, 1), got)
                edge_out[0 if up else 1, rightward, t] = got + pltpu.roll(got, 64, 1)

    pl.semaphore_wait(barrier, 2 + jnp.where(k > 0, 3, 0) + jnp.where(k < doms - 1, 3, 0))

    def dom_copy(up, q):
        first, lands, to = (pd - CAP, 0, k + 1) if up else (0, CAP, k - 1)
        return pltpu.make_async_remote_copy(
            src_ref=ens.at[first : first + CAP, :, :, tile(q)],
            dst_ref=ext.at[lands : lands + CAP, :, q],
            send_sem=dom_out_sem.at[int(up), q],
            recv_sem=dom_in_sem.at[int(up), q],
            device_id=(to, me),
            device_id_type=MESH,
        )

    def send_particles(up, on):
        @pl.when(on)
        def _():
            for q in range(tiles):
                dom_copy(up, q).start()

    for rightward in (True, False):
        message(rightward).start()
        for up in (False, True):
            edge_message(up, rightward).start()
    odd = lax.rem(k, 2) == 1
    send_particles(True, odd & (k < doms - 1))
    send_particles(False, jnp.logical_not(odd) & (k > 0))
    send_particles(True, jnp.logical_not(odd))
    send_particles(False, odd)

    for copy in needed_next:
        copy.wait()

    levels = lv[...].astype(jnp.float32)
    gw[...], gd[0], gd[1], go[0], go[1] = level_of(levels, ov[...])

    def whole_rows(i, f, at):
        return jnp.concatenate([ends_of[i, f, :1, at], inner[i, f, :, at], ends_of[i, f, 1:, at]], axis=0)

    @pl.loop(0, early // UNIT)
    def _(u):
        for s in range(UNIT):
            j = CAP + u * UNIT + s
            h0[j, :, rows] = 5.0 * (whole_rows(from_own(j), H_, rows) + pv[j])

    @pl.loop(0, early // UNIT)
    def _(u):
        slots = [CAP + u * UNIT + s for s in range(UNIT)]
        where = [from_own(j) for j in slots]

        def first(i, field, y0, up):
            at = pl.ds(TOP + y0 + up, HALF)
            return h0[slots[i], :, at] if field == H_ else whole_rows(where[i], field, at)

        def keep(i, field, y0, value):
            out[slots[i], field, :, pl.ds(y0, HALF)] = value

        all_steps(first, s1, s2, row_ground(gw, gd, go), keep, True, ny, slot_parts())

    for rightward in (False, True):
        message(rightward).wait_recv()

    def ends(first, final, s, tile_so_far):
        base = 64 * s
        lane = lane_of(first.shape)
        chosen = (lane >= base + EDGE) & (lane < base + 3 * EDGE)
        tile_so_far = jnp.where(chosen, pltpu.roll(first, base + EDGE, 2), tile_so_far)
        chosen = (lane >= base + 32) & (lane < base + 32 + 2 * EDGE)
        return jnp.where(chosen, pltpu.roll(final, (base + 32 + 2 * EDGE) % LANES, 2), tile_so_far)

    def beyond(from_left, from_right, at):
        half = lax.rem(lane_of(from_left.shape), 64)
        got = jnp.where(half < EDGE, pltpu.roll(from_left, (LANES - at) % LANES, 2), 0.0)
        chosen = (half >= 44) & (half < 44 + EDGE)
        return jnp.where(chosen, pltpu.roll(from_right, (LANES + 44 - at) % LANES, 2), got)

    fields = []
    for i, field in enumerate((levels, ov[...])):
        got = beyond(in1[1, 8:9], in1[0, 8:9], 8 * i)
        for s in range(2):
            got = ends(field[:1], field[tiles - 1 :], s, got)
        fields.append(got[0])
    gs[0], gs[1], gs[2], gs[3], gs[4] = level_of(*fields)

    @pl.loop(0, early // (2 * PAIRS))
    def _(m):
        from_left, from_right = in1[1, pl.ds(4 * m, 4)], in1[0, pl.ds(4 * m, 4)]
        slots = [[CAP + 2 * (PAIRS * m + p) + s for s in range(2)] for p in range(PAIRS)]
        for p in range(PAIRS):
            got = beyond(from_left, from_right, 8 * p)
            for s, j in enumerate(slots[p]):
                i = from_own(j)
                got = ends(column(i, j, 0), column(i, j, 1), s, got)
            b0[:, p, rows] = got
        step_strips(b0, b1, b2, b3, gs, [slice(0, 4), slice(4, PAIRS)], ny)
        for p in range(PAIRS):
            put_strips(b3, p, slots[p], out)

    @pl.when(k > 0)
    def _():
        for q in range(tiles):
            dom_copy(True, q).wait_recv()

    @pl.when(k < doms - 1)
    def _():
        for q in range(tiles):
            dom_copy(False, q).wait_recv()

    def own_particle(lands, j):
        for f in range(4):
            ext[lands, f] = whole_rows(from_own(j), f, rows)

    @pl.when(k == 0)
    def _():
        for s in range(CAP):
            own_particle(s, s)

    @pl.when(k == doms - 1)
    def _():
        for s in range(CAP, 2 * CAP):
            own_particle(s, pd - 2 * CAP + s)

    late_from = [from_ext(j, j < CAP) for j in late]
    for t, j in enumerate(late):
        for f in range(4):
            state = ext[late_from[t], f]
            late0[t, f, :, rows] = 5.0 * (state + pv[j]) if f == H_ else state

    for side in range(2):
        for rightward in (False, True):
            edge_arrival(side, rightward).wait_recv()
    for p in range(2):
        side = 1 - p
        where = [late_from[2 * p + s] - CAP * side for s in range(2)]
        ways = [jnp.where(flat < 64, *(edge_in[side, w, where[s]] for s in range(2)))[None] for w in range(2)]
        got = [beyond(ways[1], ways[0], 8 * f) for f in range(4)]
        got[H_] = got[H_] + beyond(in1[1, 8:9], in1[0, 8:9], 16 + 8 * p)
        got = jnp.concatenate(got, axis=0)
        for s in range(2):
            got = ends(late0[2 * p + s, :, 0, rows], late0[2 * p + s, :, tiles - 1, rows], s, got)
        late_strips[:, p, rows] = got

    for rightward in (False, True):
        message(rightward).wait_send()
        for up in (False, True):
            edge_message(up, rightward).wait_send()

    @pl.when(k < doms - 1)
    def _():
        for q in range(tiles):
            dom_copy(True, q).wait_send()

    @pl.when(k > 0)
    def _():
        for q in range(tiles):
            dom_copy(False, q).wait_send()


def finish(made, late0, late_strips, gs, gw, gd, go, out, late_out, s1, s2, b1, b2, b3, sem):
    pd, nf, tiles, ny, _ = made.shape

    def tile(q):
        return pl.ds(q * LANES, LANES)

    copies = [
        pltpu.make_async_copy(made.at[CAP : pd - CAP, :, q], out.at[CAP : pd - CAP, :, :, tile(q)], sem.at[0, q])
        for q in range(tiles)
    ]
    for copy in copies:
        copy.start()
    for ref in (s1, s2, b1, b2):
        clear_rows(ref, ny)

    def keep(i, field, y0, value):
        late_out[i, field, :, pl.ds(y0, HALF)] = value

    all_steps(
        lambda i, field, y0, up: late0[i, field, :, pl.ds(TOP + y0 + up, HALF)],
        s1, s2, row_ground(gw, gd, go), keep, True, ny, slot_parts(),
    )
    step_strips(late_strips, b1, b2, b3, gs, [slice(0, CAP)], ny)
    for p in range(2):
        put_strips(b3, p, [2 * p, 2 * p + 1], late_out)
    for p, first in enumerate((pd - CAP, 0)):
        for q in range(tiles):
            copy = pltpu.make_async_copy(
                late_out.at[CAP * p : CAP * p + CAP, :, q], out.at[first : first + CAP, :, :, tile(q)], sem.at[1 + p, q]
            )
            copy.start()
            copies.append(copy)
    for copy in copies:
        copy.wait()


def local(ensemble, ancestors, perturbation, levels, observed):
    pd, nf, ny, nx = ensemble.shape
    tiles = nx // LANES
    f32 = jnp.float32
    hbm = pl.BlockSpec(memory_space=pl.ANY)
    vmem = pl.BlockSpec(memory_space=pltpu.VMEM)
    state = (UNIT, nf, tiles, PITCH, LANES)
    handed = [
        pltpu.VMEM((pd, nf, tiles, ny, LANES), f32),
        pltpu.VMEM(state, f32),
        pltpu.VMEM((nf, CAP, PITCH, LANES), f32),
        pltpu.VMEM((5, ny, LANES), f32),
        pltpu.VMEM((tiles, ny, LANES), f32),
        pltpu.VMEM((2, tiles, ny, LANES), f32),
        pltpu.VMEM((2, tiles, ny, LANES), f32),
    ]
    between = pl.pallas_call(
        kernel,
        out_shape=handed,
        in_specs=[hbm] * 5,
        out_specs=[vmem] * len(handed),
        scratch_shapes=[
            pltpu.SMEM(ancestors.shape, jnp.int32),
            pltpu.VMEM((pd, nf, 2, PITCH, LANES), f32),
            pltpu.VMEM((pd, nf, tiles - 2, PITCH, LANES), f32),
            pltpu.VMEM((2 * CAP, nf, tiles, ny, LANES), f32),
            pltpu.VMEM((pd, tiles, PITCH, LANES), f32),
            pltpu.VMEM((pd, tiles, ny, LANES), f32),
            pltpu.VMEM((tiles, ny, LANES), jnp.int32),
            pltpu.VMEM((tiles, ny, LANES), f32),
            pltpu.VMEM(state, f32),
            pltpu.VMEM(state, f32),
            pltpu.VMEM((nf, PAIRS, PITCH, LANES), f32),
            pltpu.VMEM((nf, PAIRS, PITCH, LANES), f32),
            pltpu.VMEM((nf, PAIRS, PITCH, LANES), f32),
            pltpu.VMEM((nf, PAIRS, ny, LANES), f32),
            pltpu.VMEM((2, 9, ny, LANES), f32),
            pltpu.VMEM((2, 9, ny, LANES), f32),
            pltpu.VMEM((2, 2, CAP, ny, LANES), f32),
            pltpu.VMEM((2, 2, CAP, ny, LANES), f32),
            pltpu.SemaphoreType.DMA((5, tiles)),
            pltpu.SemaphoreType.DMA((2, tiles)),
            pltpu.SemaphoreType.DMA((2, tiles)),
            pltpu.SemaphoreType.DMA((2,)),
            pltpu.SemaphoreType.DMA((2,)),
            pltpu.SemaphoreType.DMA((2, 2)),
            pltpu.SemaphoreType.DMA((2, 2)),
        ],
        compiler_params=pltpu.CompilerParams(
            collective_id=0, has_side_effects=True, vmem_limit_bytes=40 * 1024 * 1024
        ),
        name="resample_and_step",
    )(*(pltpu.with_memory_space_constraint(x, pltpu.HBM) for x in (ancestors, ensemble, perturbation, levels, observed)))
    return pl.pallas_call(
        finish,
        out_shape=jax.ShapeDtypeStruct((pd, nf, ny, nx), f32),
        in_specs=[vmem] * len(handed),
        out_specs=hbm,
        scratch_shapes=[
            pltpu.VMEM((UNIT, nf, tiles, ny, LANES), f32),
            pltpu.VMEM(state, f32),
            pltpu.VMEM(state, f32),
            pltpu.VMEM((nf, CAP, PITCH, LANES), f32),
            pltpu.VMEM((nf, CAP, PITCH, LANES), f32),
            pltpu.VMEM((nf, CAP, ny, LANES), f32),
            pltpu.SemaphoreType.DMA((3, tiles)),
        ],
        compiler_params=pltpu.CompilerParams(vmem_limit_bytes=24 * 1024 * 1024),
        name="finish",
    )(*between)


def solution(mesh):
    return jax.shard_map(
        local,
        mesh=mesh,
        in_specs=(
            P("dom", None, None, "space"),
            P(),
            P("dom", None, "space"),
            P(None, "space"),
            P(None, "space"),
        ),
        out_specs=P("dom", None, None, "space"),
        check_vma=False,
    )
```

```python
import functools

import jax
import jax.numpy as jnp
from jax import lax
from jax.experimental import pallas as pl
from jax.experimental.pallas import tpu as pltpu
from jax.sharding import PartitionSpec as P

MESH = pl.DeviceIdType.MESH
STEPS = 3
CAP = 2
EDGE = 2 * STEPS
LANES = 128
TOP = 8
PITCH = 32
UNIT = 4
HALF = 8
PAIRS = 7
RUN = 8
AHEAD = 4
NEED = (EDGE, EDGE - 1, EDGE, EDGE - 3)
SHELF = (0, 12, 6, 17)
SLOT_LANES = 20
TRIPLE = 3
E_, N_, H_, C_ = range(4)


def lane_of(shape):
    return lax.broadcasted_iota(jnp.int32, shape, len(shape) - 1)


def east(cells, joined):
    turned = pltpu.roll(cells, LANES - 1, 2)
    if not joined:
        return turned
    following = jnp.concatenate([turned[1:], turned[:1]], axis=0)
    return jnp.where(lane_of(cells.shape) == LANES - 1, following, turned)


def west(cells, joined):
    turned = pltpu.roll(cells, 1, 2)
    if not joined:
        return turned
    preceding = jnp.concatenate([turned[-1:], turned[:-1]], axis=0)
    return jnp.where(lane_of(cells.shape) == 0, preceding, turned)


def flow(read, wet, turn, joined):
    e, n, h = read(E_, 0), read(N_, 0), read(H_, 0)
    e_new = wet * (
        (5.5 * e + turn * n)
        + (read(E_, 1) + read(E_, -1))
        + (east(e - h, joined) + west(e + h, joined))
    )
    n_new = wet * (
        (5.5 * n - turn * e)
        + (east(n, joined) + west(n, joined))
        + ((read(N_, 1) - read(H_, 1)) + (read(N_, -1) + read(H_, -1)))
    )
    return e_new, n_new


def level(read, read_new, depth, pull, last, joined):
    e, n = read_new(E_, 0), read_new(N_, 0)
    spread = (east(e, joined) - west(e, joined)) + (read_new(N_, 1) - read_new(N_, -1))
    h_new = ((0.18 if last else 0.9) * read(H_, 0) + pull) - depth * spread
    c = read(C_, 0)
    c_east, c_west = east(c, joined), west(c, joined)
    c_north, c_south = read(C_, 1), read(C_, -1)
    c_new = (
        (6.0 * c + ((c_east + c_west) + (c_north + c_south)))
        - e * (c_east - c_west)
        - n * (c_north - c_south)
    )
    if last:
        c_new = 0.001 * c_new
    return h_new, c_new


def level_of(levels, observed):
    return (
        jnp.where(levels > 0, 0.1, 0.0).astype(jnp.float32),
        1.25 * levels,
        0.25 * levels,
        0.5 * observed,
        0.1 * observed,
    )


def turn_of(ny, y0):
    y = lax.broadcasted_iota(jnp.int32, (1, HALF, LANES), 1).astype(jnp.float32) + float(y0)
    return 2.0 * (0.2 + 0.6 * y / ny)


def all_steps(first, s1, s2, ground, keep, joined, ny, parts):
    wet, depth, pull = ground
    count = len(parts)
    for step in range(STEPS):
        last = step == STEPS - 1
        old, new = (None, s1) if step == 0 else (s1, s2) if step == 1 else (s2, s1)

        def reader(ref, i, y0):
            return lambda field, up: parts[i](ref, field, pl.ds(TOP + y0 + up, HALF))[...]

        def read(i, y0):
            return (lambda field, up: first(i, field, y0, up)) if step == 0 else reader(old, i, y0)

        for i in range(count):
            for y0 in range(0, ny, HALF):
                e, n = flow(read(i, y0), wet(y0), turn_of(ny, y0), joined)
                now = pl.ds(TOP + y0, HALF)
                parts[i](new, E_, now)[...] = e
                parts[i](new, N_, now)[...] = n
                if last:
                    keep(i, E_, y0, e)
                    keep(i, N_, y0, n)
        for i in range(count):
            for y0 in range(0, ny, HALF):
                h, c = level(read(i, y0), reader(new, i, y0), depth(last, y0), pull(last, y0), last, joined)
                now = pl.ds(TOP + y0, HALF)
                if last:
                    keep(i, H_, y0, h)
                    keep(i, C_, y0, c)
                else:
                    parts[i](new, H_, now)[...] = h
                    parts[i](new, C_, now)[...] = c


def slot_parts():
    return [lambda ref, field, now, s=s: ref.at[s, field, :, now] for s in range(UNIT)]


def row_ground(gw, gd, go):
    return (
        lambda y0: gw[:, pl.ds(y0, HALF)],
        lambda last, y0: gd[int(last), :, pl.ds(y0, HALF)],
        lambda last, y0: go[int(last), :, pl.ds(y0, HALF)],
    )


def strip_ground(gs):
    return (
        lambda y0: gs[0, pl.ds(y0, HALF)][None],
        lambda last, y0: gs[2 if last else 1, pl.ds(y0, HALF)][None],
        lambda last, y0: gs[4 if last else 3, pl.ds(y0, HALF)][None],
    )


def step_strips(b0, b1, b2, b3, gs, groups, ny):
    parts = [lambda ref, field, now, g=g: ref.at[field, g, now] for g in groups]

    def keep(i, field, y0, value):
        b3[field, groups[i], pl.ds(y0, HALF)] = value

    all_steps(
        lambda i, field, y0, up: b0[field, groups[i], pl.ds(TOP + y0 + up, HALF)],
        b1, b2, strip_ground(gs), keep, False, ny, parts,
    )


def put_strips(b3, p, slots, out):
    done = b3[:, p]
    lane = lane_of(done.shape)
    final = out.shape[2] - 1
    for s, j in enumerate(slots):
        base = 64 * s
        at_left = pltpu.roll(done, LANES - EDGE - base, 2)
        at_right = pltpu.roll(done, (LANES - EDGE - (base + 32 + EDGE)) % LANES, 2)
        pltpu.store(out.at[j, :, 0], at_left, mask=lane < EDGE)
        pltpu.store(out.at[j, :, final], at_right, mask=lane >= LANES - EDGE)


def clear_rows(ref, ny):
    @pl.loop(0, ref.shape[0])
    def _(i):
        blank = jnp.zeros(ref.shape[1:-2] + (8, LANES), jnp.float32)
        ref[i, ..., TOP - 8 : TOP, :] = blank
        ref[i, ..., TOP + ny : TOP + ny + 8, :] = blank


def kernel(
    anc_in, ens, pert, lev, obs, out, late0, late_strips, gs, gw, gd, go,
    anc, ends_of, inner, ext, h0, pv, lv, ov, s1, s2, b0, b1, b2, b3, out1, in1, edge_out, edge_in,
    in_sem, dom_out_sem, dom_in_sem, msg_out_sem, msg_in_sem, edge_out_sem, edge_in_sem,
):
    pd = ens.shape[0]
    ny = ens.shape[2]
    tiles = ens.shape[3] // LANES
    doms, spaces = lax.axis_size("dom"), lax.axis_size("space")
    k, me = lax.axis_index("dom"), lax.axis_index("space")
    prev_space, next_space = lax.rem(me + spaces - 1, spaces), lax.rem(me + 1, spaces)
    early = pd - 2 * CAP
    rows = slice(TOP, TOP + ny)

    barrier = pltpu.get_barrier_semaphore()

    def greet(dom, *spaces_there):
        for space in spaces_there:
            pl.semaphore_signal(barrier, inc=1, device_id=(dom, space), device_id_type=MESH)

    greet(k, prev_space, next_space)

    @pl.when(k > 0)
    def _():
        greet(k - 1, me, prev_space, next_space)

    @pl.when(k < doms - 1)
    def _():
        greet(k + 1, me, prev_space, next_space)

    def tile(q):
        return pl.ds(q * LANES, LANES)

    needed_first, needed_next = [pltpu.make_async_copy(anc_in, anc, in_sem.at[4, 0])], []
    for q in (0, tiles - 1, *range(1, tiles - 1)):
        at_end = q in (0, tiles - 1)
        loads = needed_first if at_end else needed_next
        here = ends_of.at[:, :, int(q > 0), rows] if at_end else inner.at[:, :, q - 1, rows]
        loads.append(pltpu.make_async_copy(ens.at[:, :, :, tile(q)], here, in_sem.at[3, q]))
        loads.append(pltpu.make_async_copy(pert.at[:, :, tile(q)], pv.at[:, q], in_sem.at[2, q]))
        loads.append(pltpu.make_async_copy(lev.at[:, tile(q)], lv.at[q], in_sem.at[0, q]))
        loads.append(pltpu.make_async_copy(obs.at[:, tile(q)], ov.at[q], in_sem.at[1, q]))
    for copy in needed_first + needed_next:
        copy.start()

    for ref in (ends_of, inner, h0, late0, s1, s2, b0, b1, b2, late_strips):
        clear_rows(ref, ny)

    for copy in needed_first:
        copy.wait()

    def from_own(j):
        return jnp.clip(anc[k * pd + j] - k * pd, 0, pd - 1)

    def from_ext(j, low):
        parent = anc[k * pd + j]
        if low:
            return jnp.where(k == 0, j, jnp.clip(parent - (k * pd - CAP), 0, CAP - 1))
        return jnp.where(
            k == doms - 1, j - (pd - 2 * CAP), jnp.clip(parent - (k + 1) * pd, 0, CAP - 1) + CAP
        )

    def column(i, j, side):
        h = 5.0 * (ends_of[i, H_, side, rows] + pv[j, side * (tiles - 1)])
        return jnp.concatenate(
            [ends_of[i, E_ : N_ + 1, side, rows], h[None], ends_of[i, C_:, side, rows]], axis=0
        )

    flat = lane_of((ny, LANES))

    def message(rightward):
        return pltpu.make_async_remote_copy(
            src_ref=out1.at[int(rightward)],
            dst_ref=in1.at[int(rightward)],
            send_sem=msg_out_sem.at[int(rightward)],
            recv_sem=msg_in_sem.at[int(rightward)],
            device_id=(k, next_space if rightward else prev_space),
            device_id_type=MESH,
        )

    edge_to = (jnp.where(k < doms - 1, k + 1, k), jnp.where(k > 0, k - 1, k))
    edge_side = (jnp.where(k < doms - 1, 0, 1), jnp.where(k > 0, 1, 0))

    def edge_particle(up, t):
        if up:
            return jnp.where(k < doms - 1, pd - CAP + t, from_own(pd - CAP + t))
        return jnp.where(k > 0, t, from_own(t))

    def edge_message(up, rightward):
        at = 0 if up else 1
        return pltpu.make_async_remote_copy(
            src_ref=edge_out.at[at, int(rightward)],
            dst_ref=edge_in.at[edge_side[at], int(rightward)],
            send_sem=edge_out_sem.at[at, int(rightward)],
            recv_sem=edge_in_sem.at[edge_side[at], int(rightward)],
            device_id=(edge_to[at], next_space if rightward else prev_space),
            device_id_type=MESH,
        )

    def edge_arrival(side, rightward):
        return pltpu.make_async_remote_copy(
            src_ref=edge_out.at[side, int(rightward)],
            dst_ref=edge_in.at[side, int(rightward)],
            send_sem=edge_out_sem.at[side, int(rightward)],
            recv_sem=edge_in_sem.at[side, int(rightward)],
            device_id=(k, next_space if rightward else prev_space),
            device_id_type=MESH,
        )

    def shelve(columns, side, at, tile_so_far):
        for f in range(4):
            first = LANES - NEED[f] if side else 0
            to = at + SHELF[f]
            chosen = (flat >= to) & (flat < to + NEED[f])
            tile_so_far = jnp.where(chosen, pltpu.roll(columns[f], (to - first) % LANES, 1), tile_so_far)
        return tile_so_far

    shelves = -(-PAIRS // TRIPLE)

    @pl.loop(0, early // (2 * PAIRS))
    def _(m):
        for r in range(shelves):
            packed = [jnp.zeros((ny, LANES), jnp.float32)] * 2
            for p in range(TRIPLE * r, min(PAIRS, TRIPLE * r + TRIPLE)):
                for s in range(2):
                    j = CAP + 2 * (PAIRS * m + p) + s
                    i = from_own(j)
                    for side in range(2):
                        at = 64 * s + SLOT_LANES * (p - TRIPLE * r)
                        packed[side] = shelve(column(i, j, side), side, at, packed[side])
            for side in range(2):
                out1[side, shelves * m + r] = packed[side]

    extra = shelves * (early // (2 * PAIRS))
    late = [pd - 2, pd - 1, 0, 1]
    for rightward in range(2):
        q, end = (tiles - 1, EDGE) if rightward else (0, 0)
        got = jnp.zeros((ny, LANES), jnp.float32)
        parts = [(lv[q].astype(jnp.float32), at) for at in (0, 64)] + [(ov[q], at) for at in (8, 72)]
        parts += [(5.0 * pv[j, q], 64 * (t % 2) + 16 + 8 * (t // 2)) for t, j in enumerate(late)]
        for part, at in parts:
            got = jnp.where((flat >= at) & (flat < at + EDGE), pltpu.roll(part, at + end, 1), got)
        out1[rightward, extra] = got
        for up in (True, False):
            got = jnp.zeros((ny, LANES), jnp.float32)
            for t in range(CAP):
                i = edge_particle(up, t)
                columns = [ends_of[i, f, rightward, rows] for f in range(4)]
                columns[H_] = 5.0 * columns[H_]
                got = shelve(columns, rightward, 64 * t, got)
            edge_out[0 if up else 1, rightward] = got

    def dom_copy(up, q):
        first, lands, to = (pd - CAP, 0, k + 1) if up else (0, CAP, k - 1)
        return pltpu.make_async_remote_copy(
            src_ref=ens.at[first : first + CAP, :, :, tile(q)],
            dst_ref=ext.at[lands : lands + CAP, :, q],
            send_sem=dom_out_sem.at[int(up), q],
            recv_sem=dom_in_sem.at[int(up), q],
            device_id=(to, me),
            device_id_type=MESH,
        )

    def send_particles(up, on):
        @pl.when(on)
        def _():
            for q in range(tiles):
                dom_copy(up, q).start()

    odd = lax.rem(k, 2) == 1

    def send():
        pl.semaphore_wait(barrier, 2 + jnp.where(k > 0, 3, 0) + jnp.where(k < doms - 1, 3, 0))
        for rightward in (True, False):
            message(rightward).start()
            for up in (False, True):
                edge_message(up, rightward).start()
        send_particles(True, odd & (k < doms - 1))
        send_particles(False, jnp.logical_not(odd) & (k > 0))
        send_particles(True, jnp.logical_not(odd))
        send_particles(False, odd)

    ahead = lax.rem(me, RUN) == 0
    pl.when(jnp.logical_not(ahead))(send)

    for copy in needed_next:
        copy.wait()

    levels = lv[...].astype(jnp.float32)
    gw[...], gd[0], gd[1], go[0], go[1] = level_of(levels, ov[...])

    def whole_rows(i, f, at):
        return jnp.concatenate([ends_of[i, f, :1, at], inner[i, f, :, at], ends_of[i, f, 1:, at]], axis=0)

    @pl.loop(0, early // UNIT)
    def _(u):
        for s in range(UNIT):
            j = CAP + u * UNIT + s
            h0[j, :, rows] = 5.0 * (whole_rows(from_own(j), H_, rows) + pv[j])

    @pl.loop(0, early // UNIT)
    def _(u):
        pl.when(ahead & (u == AHEAD))(send)
        slots = [CAP + u * UNIT + s for s in range(UNIT)]
        where = [from_own(j) for j in slots]

        def first(i, field, y0, up):
            at = pl.ds(TOP + y0 + up, HALF)
            return h0[slots[i], :, at] if field == H_ else whole_rows(where[i], field, at)

        def keep(i, field, y0, value):
            out[slots[i], field, :, pl.ds(y0, HALF)] = value

        all_steps(first, s1, s2, row_ground(gw, gd, go), keep, True, ny, slot_parts())

    for rightward in (False, True):
        message(rightward).wait_recv()

    def ends(first, final, s, tile_so_far):
        base = 64 * s
        lane = lane_of(first.shape)
        chosen = (lane >= base + EDGE) & (lane < base + 3 * EDGE)
        tile_so_far = jnp.where(chosen, pltpu.roll(first, base + EDGE, 2), tile_so_far)
        chosen = (lane >= base + 32) & (lane < base + 32 + 2 * EDGE)
        return jnp.where(chosen, pltpu.roll(final, (base + 32 + 2 * EDGE) % LANES, 2), tile_so_far)

    def beyond(from_left, from_right, at, width=EDGE):
        half = lax.rem(lane_of(from_left.shape), 64)
        chosen = (half >= EDGE - width) & (half < EDGE)
        got = jnp.where(chosen, pltpu.roll(from_left, (LANES + EDGE - width - at) % LANES, 1), 0.0)
        chosen = (half >= 44) & (half < 44 + width)
        return jnp.where(chosen, pltpu.roll(from_right, (LANES + 44 - at) % LANES, 1), got)

    def unshelved(from_left, from_right, at):
        return [beyond(from_left, from_right, at + SHELF[f], NEED[f]) for f in range(4)]

    fields = []
    for i, field in enumerate((levels, ov[...])):
        got = beyond(in1[1, extra], in1[0, extra], 8 * i)[None]
        for s in range(2):
            got = ends(field[:1], field[tiles - 1 :], s, got)
        fields.append(got[0])
    gs[0], gs[1], gs[2], gs[3], gs[4] = level_of(*fields)

    @pl.loop(0, early // (2 * PAIRS))
    def _(m):
        slots = [[CAP + 2 * (PAIRS * m + p) + s for s in range(2)] for p in range(PAIRS)]
        for p in range(PAIRS):
            r = shelves * m + p // TRIPLE
            got = jnp.stack(unshelved(in1[1, r], in1[0, r], SLOT_LANES * (p % TRIPLE)))
            for s, j in enumerate(slots[p]):
                i = from_own(j)
                got = ends(column(i, j, 0), column(i, j, 1), s, got)
            b0[:, p, rows] = got
        step_strips(b0, b1, b2, b3, gs, [slice(0, 4), slice(4, PAIRS)], ny)
        for p in range(PAIRS):
            put_strips(b3, p, slots[p], out)

    @pl.when(k > 0)
    def _():
        for q in range(tiles):
            dom_copy(True, q).wait_recv()

    @pl.when(k < doms - 1)
    def _():
        for q in range(tiles):
            dom_copy(False, q).wait_recv()

    def own_particle(lands, j):
        for f in range(4):
            ext[lands, f] = whole_rows(from_own(j), f, rows)

    @pl.when(k == 0)
    def _():
        for s in range(CAP):
            own_particle(s, s)

    @pl.when(k == doms - 1)
    def _():
        for s in range(CAP, 2 * CAP):
            own_particle(s, pd - 2 * CAP + s)

    late_from = [from_ext(j, j < CAP) for j in late]
    for t, j in enumerate(late):
        for f in range(4):
            state = ext[late_from[t], f]
            late0[t, f, :, rows] = 5.0 * (state + pv[j]) if f == H_ else state

    for side in range(2):
        for rightward in (False, True):
            edge_arrival(side, rightward).wait_recv()
    for p in range(2):
        side = 1 - p
        where = [late_from[2 * p + s] - CAP * side for s in range(2)]
        ways = []
        for w in range(2):
            came = edge_in[side, w]
            turned = pltpu.roll(came, 64, 1)
            ways.append(jnp.where(flat < 64, *(jnp.where(where[s] == s, came, turned) for s in range(2))))
        got = unshelved(ways[1], ways[0], 0)
        got[H_] = got[H_] + beyond(in1[1, extra], in1[0, extra], 16 + 8 * p)
        got = jnp.stack(got)
        for s in range(2):
            got = ends(late0[2 * p + s, :, 0, rows], late0[2 * p + s, :, tiles - 1, rows], s, got)
        late_strips[:, p, rows] = got

    for rightward in (False, True):
        message(rightward).wait_send()
        for up in (False, True):
            edge_message(up, rightward).wait_send()

    @pl.when(k < doms - 1)
    def _():
        for q in range(tiles):
            dom_copy(True, q).wait_send()

    @pl.when(k > 0)
    def _():
        for q in range(tiles):
            dom_copy(False, q).wait_send()


def finish(made, late0, late_strips, gs, gw, gd, go, out, late_out, s1, s2, b1, b2, b3, sem):
    pd, nf, tiles, ny, _ = made.shape

    def tile(q):
        return pl.ds(q * LANES, LANES)

    copies = [
        pltpu.make_async_copy(made.at[CAP : pd - CAP, :, q], out.at[CAP : pd - CAP, :, :, tile(q)], sem.at[0, q])
        for q in range(tiles)
    ]
    for copy in copies:
        copy.start()
    for ref in (s1, s2, b1, b2):
        clear_rows(ref, ny)

    def keep(i, field, y0, value):
        late_out[i, field, :, pl.ds(y0, HALF)] = value

    all_steps(
        lambda i, field, y0, up: late0[i, field, :, pl.ds(TOP + y0 + up, HALF)],
        s1, s2, row_ground(gw, gd, go), keep, True, ny, slot_parts(),
    )
    step_strips(late_strips, b1, b2, b3, gs, [slice(0, CAP)], ny)
    for p in range(2):
        put_strips(b3, p, [2 * p, 2 * p + 1], late_out)
    for p, first in enumerate((pd - CAP, 0)):
        for q in range(tiles):
            copy = pltpu.make_async_copy(
                late_out.at[CAP * p : CAP * p + CAP, :, q], out.at[first : first + CAP, :, :, tile(q)], sem.at[1 + p, q]
            )
            copy.start()
            copies.append(copy)
    for copy in copies:
        copy.wait()


def local(ensemble, ancestors, perturbation, levels, observed):
    pd, nf, ny, nx = ensemble.shape
    tiles = nx // LANES
    f32 = jnp.float32
    hbm = pl.BlockSpec(memory_space=pl.ANY)
    vmem = pl.BlockSpec(memory_space=pltpu.VMEM)
    state = (UNIT, nf, tiles, PITCH, LANES)
    handed = [
        pltpu.VMEM((pd, nf, tiles, ny, LANES), f32),
        pltpu.VMEM(state, f32),
        pltpu.VMEM((nf, CAP, PITCH, LANES), f32),
        pltpu.VMEM((5, ny, LANES), f32),
        pltpu.VMEM((tiles, ny, LANES), f32),
        pltpu.VMEM((2, tiles, ny, LANES), f32),
        pltpu.VMEM((2, tiles, ny, LANES), f32),
    ]
    between = pl.pallas_call(
        kernel,
        out_shape=handed,
        in_specs=[hbm] * 5,
        out_specs=[vmem] * len(handed),
        scratch_shapes=[
            pltpu.SMEM(ancestors.shape, jnp.int32),
            pltpu.VMEM((pd, nf, 2, PITCH, LANES), f32),
            pltpu.VMEM((pd, nf, tiles - 2, PITCH, LANES), f32),
            pltpu.VMEM((2 * CAP, nf, tiles, ny, LANES), f32),
            pltpu.VMEM((pd, tiles, PITCH, LANES), f32),
            pltpu.VMEM((pd, tiles, ny, LANES), f32),
            pltpu.VMEM((tiles, ny, LANES), jnp.int32),
            pltpu.VMEM((tiles, ny, LANES), f32),
            pltpu.VMEM(state, f32),
            pltpu.VMEM(state, f32),
            pltpu.VMEM((nf, PAIRS, PITCH, LANES), f32),
            pltpu.VMEM((nf, PAIRS, PITCH, LANES), f32),
            pltpu.VMEM((nf, PAIRS, PITCH, LANES), f32),
            pltpu.VMEM((nf, PAIRS, ny, LANES), f32),
            pltpu.VMEM((2, 7, ny, LANES), f32),
            pltpu.VMEM((2, 7, ny, LANES), f32),
            pltpu.VMEM((2, 2, ny, LANES), f32),
            pltpu.VMEM((2, 2, ny, LANES), f32),
            pltpu.SemaphoreType.DMA((5, tiles)),
            pltpu.SemaphoreType.DMA((2, tiles)),
            pltpu.SemaphoreType.DMA((2, tiles)),
            pltpu.SemaphoreType.DMA((2,)),
            pltpu.SemaphoreType.DMA((2,)),
            pltpu.SemaphoreType.DMA((2, 2)),
            pltpu.SemaphoreType.DMA((2, 2)),
        ],
        compiler_params=pltpu.CompilerParams(
            collective_id=0, has_side_effects=True, vmem_limit_bytes=40 * 1024 * 1024
        ),
        name="resample_and_step",
    )(*(pltpu.with_memory_space_constraint(x, pltpu.HBM) for x in (ancestors, ensemble, perturbation, levels, observed)))
    return pl.pallas_call(
        finish,
        out_shape=jax.ShapeDtypeStruct((pd, nf, ny, nx), f32),
        in_specs=[vmem] * len(handed),
        out_specs=hbm,
        scratch_shapes=[
            pltpu.VMEM((UNIT, nf, tiles, ny, LANES), f32),
            pltpu.VMEM(state, f32),
            pltpu.VMEM(state, f32),
            pltpu.VMEM((nf, CAP, PITCH, LANES), f32),
            pltpu.VMEM((nf, CAP, PITCH, LANES), f32),
            pltpu.VMEM((nf, CAP, ny, LANES), f32),
            pltpu.SemaphoreType.DMA((3, tiles)),
        ],
        compiler_params=pltpu.CompilerParams(vmem_limit_bytes=24 * 1024 * 1024),
        name="finish",
    )(*between)


def solution(mesh):
    return jax.shard_map(
        local,
        mesh=mesh,
        in_specs=(
            P("dom", None, None, "space"),
            P(),
            P("dom", None, "space"),
            P(None, "space"),
            P(None, "space"),
        ),
        out_specs=P("dom", None, None, "space"),
        check_vma=False,
    )
```

```python
import functools

import jax
import jax.numpy as jnp
from jax import lax
from jax.experimental import pallas as pl
from jax.experimental.pallas import tpu as pltpu
from jax.sharding import PartitionSpec as P

MESH = pl.DeviceIdType.MESH
STEPS = 3
CAP = 2
EDGE = 2 * STEPS
LANES = 128
TOP = 8
PITCH = 32
UNIT = 4
HALF = 8
PAIRS = 7
RUN = 8
ROW = 8
AHEAD = 3
NEED = (EDGE, EDGE - 1, EDGE, EDGE - 3)
SHELF = (0, 12, 6, 17)
SLOT_LANES = 20
TRIPLE = 3
E_, N_, H_, C_ = range(4)


def lane_of(shape):
    return lax.broadcasted_iota(jnp.int32, shape, len(shape) - 1)


def east(cells, joined):
    turned = pltpu.roll(cells, LANES - 1, 2)
    if not joined:
        return turned
    following = jnp.concatenate([turned[1:], turned[:1]], axis=0)
    return jnp.where(lane_of(cells.shape) == LANES - 1, following, turned)


def west(cells, joined):
    turned = pltpu.roll(cells, 1, 2)
    if not joined:
        return turned
    preceding = jnp.concatenate([turned[-1:], turned[:-1]], axis=0)
    return jnp.where(lane_of(cells.shape) == 0, preceding, turned)


def flow(read, wet, turn, joined):
    e, n, h = read(E_, 0), read(N_, 0), read(H_, 0)
    e_new = wet * (
        (5.5 * e + turn * n)
        + (read(E_, 1) + read(E_, -1))
        + (east(e - h, joined) + west(e + h, joined))
    )
    n_new = wet * (
        (5.5 * n - turn * e)
        + (east(n, joined) + west(n, joined))
        + ((read(N_, 1) - read(H_, 1)) + (read(N_, -1) + read(H_, -1)))
    )
    return e_new, n_new


def level(read, read_new, depth, pull, last, joined):
    e, n = read_new(E_, 0), read_new(N_, 0)
    spread = (east(e, joined) - west(e, joined)) + (read_new(N_, 1) - read_new(N_, -1))
    h_new = ((0.18 if last else 0.9) * read(H_, 0) + pull) - depth * spread
    c = read(C_, 0)
    c_east, c_west = east(c, joined), west(c, joined)
    c_north, c_south = read(C_, 1), read(C_, -1)
    c_new = (
        (6.0 * c + ((c_east + c_west) + (c_north + c_south)))
        - e * (c_east - c_west)
        - n * (c_north - c_south)
    )
    if last:
        c_new = 0.001 * c_new
    return h_new, c_new


def level_of(levels, observed):
    return (
        jnp.where(levels > 0, 0.1, 0.0).astype(jnp.float32),
        1.25 * levels,
        0.25 * levels,
        0.5 * observed,
        0.1 * observed,
    )


def turn_of(ny, y0):
    y = lax.broadcasted_iota(jnp.int32, (1, HALF, LANES), 1).astype(jnp.float32) + float(y0)
    return 2.0 * (0.2 + 0.6 * y / ny)


def all_steps(first, s1, s2, ground, keep, joined, ny, parts):
    wet, depth, pull = ground
    count = len(parts)
    for step in range(STEPS):
        last = step == STEPS - 1
        old, new = (None, s1) if step == 0 else (s1, s2) if step == 1 else (s2, s1)

        def reader(ref, i, y0):
            return lambda field, up: parts[i](ref, field, pl.ds(TOP + y0 + up, HALF))[...]

        def read(i, y0):
            return (lambda field, up: first(i, field, y0, up)) if step == 0 else reader(old, i, y0)

        for i in range(count):
            for y0 in range(0, ny, HALF):
                e, n = flow(read(i, y0), wet(y0), turn_of(ny, y0), joined)
                now = pl.ds(TOP + y0, HALF)
                parts[i](new, E_, now)[...] = e
                parts[i](new, N_, now)[...] = n
                if last:
                    keep(i, E_, y0, e)
                    keep(i, N_, y0, n)
        for i in range(count):
            for y0 in range(0, ny, HALF):
                h, c = level(read(i, y0), reader(new, i, y0), depth(last, y0), pull(last, y0), last, joined)
                now = pl.ds(TOP + y0, HALF)
                if last:
                    keep(i, H_, y0, h)
                    keep(i, C_, y0, c)
                else:
                    parts[i](new, H_, now)[...] = h
                    parts[i](new, C_, now)[...] = c


def slot_parts():
    return [lambda ref, field, now, s=s: ref.at[s, field, :, now] for s in range(UNIT)]


def row_ground(gw, gd, go):
    return (
        lambda y0: gw[:, pl.ds(y0, HALF)],
        lambda last, y0: gd[int(last), :, pl.ds(y0, HALF)],
        lambda last, y0: go[int(last), :, pl.ds(y0, HALF)],
    )


def strip_ground(gs):
    return (
        lambda y0: gs[0, pl.ds(y0, HALF)][None],
        lambda last, y0: gs[2 if last else 1, pl.ds(y0, HALF)][None],
        lambda last, y0: gs[4 if last else 3, pl.ds(y0, HALF)][None],
    )


def step_strips(b0, b1, b2, b3, gs, groups, ny):
    parts = [lambda ref, field, now, g=g: ref.at[field, g, now] for g in groups]

    def keep(i, field, y0, value):
        b3[field, groups[i], pl.ds(y0, HALF)] = value

    all_steps(
        lambda i, field, y0, up: b0[field, groups[i], pl.ds(TOP + y0 + up, HALF)],
        b1, b2, strip_ground(gs), keep, False, ny, parts,
    )


def put_strips(b3, p, slots, out):
    done = b3[:, p]
    lane = lane_of(done.shape)
    final = out.shape[2] - 1
    for s, j in enumerate(slots):
        base = 64 * s
        at_left = pltpu.roll(done, LANES - EDGE - base, 2)
        at_right = pltpu.roll(done, (LANES - EDGE - (base + 32 + EDGE)) % LANES, 2)
        pltpu.store(out.at[j, :, 0], at_left, mask=lane < EDGE)
        pltpu.store(out.at[j, :, final], at_right, mask=lane >= LANES - EDGE)


def clear_rows(ref, ny):
    @pl.loop(0, ref.shape[0])
    def _(i):
        blank = jnp.zeros(ref.shape[1:-2] + (8, LANES), jnp.float32)
        ref[i, ..., TOP - 8 : TOP, :] = blank
        ref[i, ..., TOP + ny : TOP + ny + 8, :] = blank


def kernel(
    anc_in, ens, pert, lev, obs, out, late0, late_strips, gs, gw, gd, go,
    anc, ends_of, inner, ext, h0, pv, lv, ov, s1, s2, b0, b1, b2, b3, out1, in1, edge_out, edge_in,
    in_sem, dom_out_sem, dom_in_sem, msg_out_sem, msg_in_sem, edge_out_sem, edge_in_sem,
):
    pd = ens.shape[0]
    ny = ens.shape[2]
    tiles = ens.shape[3] // LANES
    doms, spaces = lax.axis_size("dom"), lax.axis_size("space")
    k, me = lax.axis_index("dom"), lax.axis_index("space")
    prev_space, next_space = lax.rem(me + spaces - 1, spaces), lax.rem(me + 1, spaces)
    early = pd - 2 * CAP
    rows = slice(TOP, TOP + ny)

    barrier = pltpu.get_barrier_semaphore()

    def greet(dom, *spaces_there):
        for space in spaces_there:
            pl.semaphore_signal(barrier, inc=1, device_id=(dom, space), device_id_type=MESH)

    greet(k, prev_space, next_space)

    @pl.when(k > 0)
    def _():
        greet(k - 1, me, prev_space, next_space)

    @pl.when(k < doms - 1)
    def _():
        greet(k + 1, me, prev_space, next_space)

    def tile(q):
        return pl.ds(q * LANES, LANES)

    needed_first, needed_next = [pltpu.make_async_copy(anc_in, anc, in_sem.at[4, 0])], []
    for q in (0, tiles - 1, *range(1, tiles - 1)):
        at_end = q in (0, tiles - 1)
        loads = needed_first if at_end else needed_next
        here = ends_of.at[:, :, int(q > 0), rows] if at_end else inner.at[:, :, q - 1, rows]
        loads.append(pltpu.make_async_copy(ens.at[:, :, :, tile(q)], here, in_sem.at[3, q]))
        loads.append(pltpu.make_async_copy(pert.at[:, :, tile(q)], pv.at[:, q], in_sem.at[2, q]))
        loads.append(pltpu.make_async_copy(lev.at[:, tile(q)], lv.at[q], in_sem.at[0, q]))
        loads.append(pltpu.make_async_copy(obs.at[:, tile(q)], ov.at[q], in_sem.at[1, q]))
    for copy in needed_first + needed_next:
        copy.start()

    for ref in (ends_of, inner, h0, late0, s1, s2, b0, b1, b2, late_strips):
        clear_rows(ref, ny)

    for copy in needed_first:
        copy.wait()

    def from_own(j):
        return jnp.clip(anc[k * pd + j] - k * pd, 0, pd - 1)

    def from_ext(j, low):
        parent = anc[k * pd + j]
        if low:
            return jnp.where(k == 0, j, jnp.clip(parent - (k * pd - CAP), 0, CAP - 1))
        return jnp.where(
            k == doms - 1, j - (pd - 2 * CAP), jnp.clip(parent - (k + 1) * pd, 0, CAP - 1) + CAP
        )

    def column(i, j, side):
        h = 5.0 * (ends_of[i, H_, side, rows] + pv[j, side * (tiles - 1)])
        return jnp.concatenate(
            [ends_of[i, E_ : N_ + 1, side, rows], h[None], ends_of[i, C_:, side, rows]], axis=0
        )

    flat = lane_of((ny, LANES))

    def message(rightward):
        return pltpu.make_async_remote_copy(
            src_ref=out1.at[int(rightward)],
            dst_ref=in1.at[int(rightward)],
            send_sem=msg_out_sem.at[int(rightward)],
            recv_sem=msg_in_sem.at[int(rightward)],
            device_id=(k, next_space if rightward else prev_space),
            device_id_type=MESH,
        )

    edge_to = (jnp.where(k < doms - 1, k + 1, k), jnp.where(k > 0, k - 1, k))
    edge_side = (jnp.where(k < doms - 1, 0, 1), jnp.where(k > 0, 1, 0))

    def edge_particle(up, t):
        if up:
            return jnp.where(k < doms - 1, pd - CAP + t, from_own(pd - CAP + t))
        return jnp.where(k > 0, t, from_own(t))

    def edge_message(up, rightward):
        at = 0 if up else 1
        return pltpu.make_async_remote_copy(
            src_ref=edge_out.at[at, int(rightward)],
            dst_ref=edge_in.at[edge_side[at], int(rightward)],
            send_sem=edge_out_sem.at[at, int(rightward)],
            recv_sem=edge_in_sem.at[edge_side[at], int(rightward)],
            device_id=(edge_to[at], next_space if rightward else prev_space),
            device_id_type=MESH,
        )

    def edge_arrival(side, rightward):
        return pltpu.make_async_remote_copy(
            src_ref=edge_out.at[side, int(rightward)],
            dst_ref=edge_in.at[side, int(rightward)],
            send_sem=edge_out_sem.at[side, int(rightward)],
            recv_sem=edge_in_sem.at[side, int(rightward)],
            device_id=(k, next_space if rightward else prev_space),
            device_id_type=MESH,
        )

    def shelve(columns, side, at, tile_so_far):
        for f in range(4):
            first = LANES - NEED[f] if side else 0
            to = at + SHELF[f]
            chosen = (flat >= to) & (flat < to + NEED[f])
            tile_so_far = jnp.where(chosen, pltpu.roll(columns[f], (to - first) % LANES, 1), tile_so_far)
        return tile_so_far

    shelves = -(-PAIRS // TRIPLE)

    @pl.loop(0, early // (2 * PAIRS))
    def _(m):
        for r in range(shelves):
            packed = [jnp.zeros((ny, LANES), jnp.float32)] * 2
            for p in range(TRIPLE * r, min(PAIRS, TRIPLE * r + TRIPLE)):
                for s in range(2):
                    j = CAP + 2 * (PAIRS * m + p) + s
                    i = from_own(j)
                    for side in range(2):
                        at = 64 * s + SLOT_LANES * (p - TRIPLE * r)
                        packed[side] = shelve(column(i, j, side), side, at, packed[side])
            for side in range(2):
                out1[side, shelves * m + r] = packed[side]

    extra = shelves * (early // (2 * PAIRS))
    late = [pd - 2, pd - 1, 0, 1]
    for rightward in range(2):
        q, end = (tiles - 1, EDGE) if rightward else (0, 0)
        got = jnp.zeros((ny, LANES), jnp.float32)
        parts = [(lv[q].astype(jnp.float32), at) for at in (0, 64)] + [(ov[q], at) for at in (8, 72)]
        parts += [(5.0 * pv[j, q], 64 * (t % 2) + 16 + 8 * (t // 2)) for t, j in enumerate(late)]
        for part, at in parts:
            got = jnp.where((flat >= at) & (flat < at + EDGE), pltpu.roll(part, at + end, 1), got)
        out1[rightward, extra] = got
        for up in (True, False):
            got = jnp.zeros((ny, LANES), jnp.float32)
            for t in range(CAP):
                i = edge_particle(up, t)
                columns = [ends_of[i, f, rightward, rows] for f in range(4)]
                columns[H_] = 5.0 * columns[H_]
                got = shelve(columns, rightward, 64 * t, got)
            edge_out[0 if up else 1, rightward] = got

    def dom_copy(up, q):
        first, lands, to = (pd - CAP, 0, k + 1) if up else (0, CAP, k - 1)
        return pltpu.make_async_remote_copy(
            src_ref=ens.at[first : first + CAP, :, :, tile(q)],
            dst_ref=ext.at[lands : lands + CAP, :, q],
            send_sem=dom_out_sem.at[int(up), q],
            recv_sem=dom_in_sem.at[int(up), q],
            device_id=(to, me),
            device_id_type=MESH,
        )

    def send_particles(up, on):
        @pl.when(on)
        def _():
            for q in range(tiles):
                dom_copy(up, q).start()

    odd = lax.rem(k, 2) == 1

    def send():
        pl.semaphore_wait(barrier, 2 + jnp.where(k > 0, 3, 0) + jnp.where(k < doms - 1, 3, 0))
        in_hurry = lax.rem(me, RUN) < RUN - 1
        far_up = in_hurry & (lax.rem(k, ROW) == ROW - 1) & (k < doms - 1)
        far_down = in_hurry & (lax.rem(k, ROW) == 0) & (k > 0)
        send_particles(True, far_up)
        send_particles(False, far_down)
        for rightward in (True, False):
            message(rightward).start()
            for up in (False, True):
                edge_message(up, rightward).start()
        send_particles(True, odd & (k < doms - 1) & jnp.logical_not(far_up))
        send_particles(False, jnp.logical_not(odd) & (k > 0) & jnp.logical_not(far_down))
        send_particles(True, jnp.logical_not(odd))
        send_particles(False, odd)

    ahead = lax.rem(me, RUN) == 0
    pl.when(jnp.logical_not(ahead))(send)

    for copy in needed_next:
        copy.wait()

    levels = lv[...].astype(jnp.float32)
    gw[...], gd[0], gd[1], go[0], go[1] = level_of(levels, ov[...])

    def whole_rows(i, f, at):
        return jnp.concatenate([ends_of[i, f, :1, at], inner[i, f, :, at], ends_of[i, f, 1:, at]], axis=0)

    @pl.loop(0, early // UNIT)
    def _(u):
        for s in range(UNIT):
            j = CAP + u * UNIT + s
            h0[j, :, rows] = 5.0 * (whole_rows(from_own(j), H_, rows) + pv[j])

    @pl.loop(0, early // UNIT)
    def _(u):
        pl.when(ahead & (u == AHEAD))(send)
        slots = [CAP + u * UNIT + s for s in range(UNIT)]
        where = [from_own(j) for j in slots]

        def first(i, field, y0, up):
            at = pl.ds(TOP + y0 + up, HALF)
            return h0[slots[i], :, at] if field == H_ else whole_rows(where[i], field, at)

        def keep(i, field, y0, value):
            out[slots[i], field, :, pl.ds(y0, HALF)] = value

        all_steps(first, s1, s2, row_ground(gw, gd, go), keep, True, ny, slot_parts())

    for rightward in (False, True):
        message(rightward).wait_recv()

    def ends(first, final, s, tile_so_far):
        base = 64 * s
        lane = lane_of(first.shape)
        chosen = (lane >= base + EDGE) & (lane < base + 3 * EDGE)
        tile_so_far = jnp.where(chosen, pltpu.roll(first, base + EDGE, 2), tile_so_far)
        chosen = (lane >= base + 32) & (lane < base + 32 + 2 * EDGE)
        return jnp.where(chosen, pltpu.roll(final, (base + 32 + 2 * EDGE) % LANES, 2), tile_so_far)

    def beyond(from_left, from_right, at, width=EDGE):
        half = lax.rem(lane_of(from_left.shape), 64)
        chosen = (half >= EDGE - width) & (half < EDGE)
        got = jnp.where(chosen, pltpu.roll(from_left, (LANES + EDGE - width - at) % LANES, 1), 0.0)
        chosen = (half >= 44) & (half < 44 + width)
        return jnp.where(chosen, pltpu.roll(from_right, (LANES + 44 - at) % LANES, 1), got)

    def unshelved(from_left, from_right, at):
        return [beyond(from_left, from_right, at + SHELF[f], NEED[f]) for f in range(4)]

    fields = []
    for i, field in enumerate((levels, ov[...])):
        got = beyond(in1[1, extra], in1[0, extra], 8 * i)[None]
        for s in range(2):
            got = ends(field[:1], field[tiles - 1 :], s, got)
        fields.append(got[0])
    gs[0], gs[1], gs[2], gs[3], gs[4] = level_of(*fields)

    @pl.loop(0, early // (2 * PAIRS))
    def _(m):
        slots = [[CAP + 2 * (PAIRS * m + p) + s for s in range(2)] for p in range(PAIRS)]
        for p in range(PAIRS):
            r = shelves * m + p // TRIPLE
            got = jnp.stack(unshelved(in1[1, r], in1[0, r], SLOT_LANES * (p % TRIPLE)))
            for s, j in enumerate(slots[p]):
                i = from_own(j)
                got = ends(column(i, j, 0), column(i, j, 1), s, got)
            b0[:, p, rows] = got
        step_strips(b0, b1, b2, b3, gs, [slice(0, 4), slice(4, PAIRS)], ny)
        for p in range(PAIRS):
            put_strips(b3, p, slots[p], out)

    @pl.when(k > 0)
    def _():
        for q in range(tiles):
            dom_copy(True, q).wait_recv()

    @pl.when(k < doms - 1)
    def _():
        for q in range(tiles):
            dom_copy(False, q).wait_recv()

    def own_particle(lands, j):
        for f in range(4):
            ext[lands, f] = whole_rows(from_own(j), f, rows)

    @pl.when(k == 0)
    def _():
        for s in range(CAP):
            own_particle(s, s)

    @pl.when(k == doms - 1)
    def _():
        for s in range(CAP, 2 * CAP):
            own_particle(s, pd - 2 * CAP + s)

    late_from = [from_ext(j, j < CAP) for j in late]
    for t, j in enumerate(late):
        for f in range(4):
            state = ext[late_from[t], f]
            late0[t, f, :, rows] = 5.0 * (state + pv[j]) if f == H_ else state

    for side in range(2):
        for rightward in (False, True):
            edge_arrival(side, rightward).wait_recv()
    for p in range(2):
        side = 1 - p
        where = [late_from[2 * p + s] - CAP * side for s in range(2)]
        ways = []
        for w in range(2):
            came = edge_in[side, w]
            turned = pltpu.roll(came, 64, 1)
            ways.append(jnp.where(flat < 64, *(jnp.where(where[s] == s, came, turned) for s in range(2))))
        got = unshelved(ways[1], ways[0], 0)
        got[H_] = got[H_] + beyond(in1[1, extra], in1[0, extra], 16 + 8 * p)
        got = jnp.stack(got)
        for s in range(2):
            got = ends(late0[2 * p + s, :, 0, rows], late0[2 * p + s, :, tiles - 1, rows], s, got)
        late_strips[:, p, rows] = got

    for rightward in (False, True):
        message(rightward).wait_send()
        for up in (False, True):
            edge_message(up, rightward).wait_send()

    @pl.when(k < doms - 1)
    def _():
        for q in range(tiles):
            dom_copy(True, q).wait_send()

    @pl.when(k > 0)
    def _():
        for q in range(tiles):
            dom_copy(False, q).wait_send()


def finish(made, late0, late_strips, gs, gw, gd, go, out, late_out, s1, s2, b1, b2, b3, sem):
    pd, nf, tiles, ny, _ = made.shape

    def tile(q):
        return pl.ds(q * LANES, LANES)

    copies = [
        pltpu.make_async_copy(made.at[CAP : pd - CAP, :, q], out.at[CAP : pd - CAP, :, :, tile(q)], sem.at[0, q])
        for q in range(tiles)
    ]
    for copy in copies:
        copy.start()
    for ref in (s1, s2, b1, b2):
        clear_rows(ref, ny)

    def keep(i, field, y0, value):
        late_out[i, field, :, pl.ds(y0, HALF)] = value

    all_steps(
        lambda i, field, y0, up: late0[i, field, :, pl.ds(TOP + y0 + up, HALF)],
        s1, s2, row_ground(gw, gd, go), keep, True, ny, slot_parts(),
    )
    step_strips(late_strips, b1, b2, b3, gs, [slice(0, CAP)], ny)
    for p in range(2):
        put_strips(b3, p, [2 * p, 2 * p + 1], late_out)
    for p, first in enumerate((pd - CAP, 0)):
        for q in range(tiles):
            copy = pltpu.make_async_copy(
                late_out.at[CAP * p : CAP * p + CAP, :, q], out.at[first : first + CAP, :, :, tile(q)], sem.at[1 + p, q]
            )
            copy.start()
            copies.append(copy)
    for copy in copies:
        copy.wait()


def local(ensemble, ancestors, perturbation, levels, observed):
    pd, nf, ny, nx = ensemble.shape
    tiles = nx // LANES
    f32 = jnp.float32
    hbm = pl.BlockSpec(memory_space=pl.ANY)
    vmem = pl.BlockSpec(memory_space=pltpu.VMEM)
    state = (UNIT, nf, tiles, PITCH, LANES)
    handed = [
        pltpu.VMEM((pd, nf, tiles, ny, LANES), f32),
        pltpu.VMEM(state, f32),
        pltpu.VMEM((nf, CAP, PITCH, LANES), f32),
        pltpu.VMEM((5, ny, LANES), f32),
        pltpu.VMEM((tiles, ny, LANES), f32),
        pltpu.VMEM((2, tiles, ny, LANES), f32),
        pltpu.VMEM((2, tiles, ny, LANES), f32),
    ]
    between = pl.pallas_call(
        kernel,
        out_shape=handed,
        in_specs=[hbm] * 5,
        out_specs=[vmem] * len(handed),
        scratch_shapes=[
            pltpu.SMEM(ancestors.shape, jnp.int32),
            pltpu.VMEM((pd, nf, 2, PITCH, LANES), f32),
            pltpu.VMEM((pd, nf, tiles - 2, PITCH, LANES), f32),
            pltpu.VMEM((2 * CAP, nf, tiles, ny, LANES), f32),
            pltpu.VMEM((pd, tiles, PITCH, LANES), f32),
            pltpu.VMEM((pd, tiles, ny, LANES), f32),
            pltpu.VMEM((tiles, ny, LANES), jnp.int32),
            pltpu.VMEM((tiles, ny, LANES), f32),
            pltpu.VMEM(state, f32),
            pltpu.VMEM(state, f32),
            pltpu.VMEM((nf, PAIRS, PITCH, LANES), f32),
            pltpu.VMEM((nf, PAIRS, PITCH, LANES), f32),
            pltpu.VMEM((nf, PAIRS, PITCH, LANES), f32),
            pltpu.VMEM((nf, PAIRS, ny, LANES), f32),
            pltpu.VMEM((2, 7, ny, LANES), f32),
            pltpu.VMEM((2, 7, ny, LANES), f32),
            pltpu.VMEM((2, 2, ny, LANES), f32),
            pltpu.VMEM((2, 2, ny, LANES), f32),
            pltpu.SemaphoreType.DMA((5, tiles)),
            pltpu.SemaphoreType.DMA((2, tiles)),
            pltpu.SemaphoreType.DMA((2, tiles)),
            pltpu.SemaphoreType.DMA((2,)),
            pltpu.SemaphoreType.DMA((2,)),
            pltpu.SemaphoreType.DMA((2, 2)),
            pltpu.SemaphoreType.DMA((2, 2)),
        ],
        compiler_params=pltpu.CompilerParams(
            collective_id=0, has_side_effects=True, vmem_limit_bytes=40 * 1024 * 1024
        ),
        name="resample_and_step",
    )(*(pltpu.with_memory_space_constraint(x, pltpu.HBM) for x in (ancestors, ensemble, perturbation, levels, observed)))
    return pl.pallas_call(
        finish,
        out_shape=jax.ShapeDtypeStruct((pd, nf, ny, nx), f32),
        in_specs=[vmem] * len(handed),
        out_specs=hbm,
        scratch_shapes=[
            pltpu.VMEM((UNIT, nf, tiles, ny, LANES), f32),
            pltpu.VMEM(state, f32),
            pltpu.VMEM(state, f32),
            pltpu.VMEM((nf, CAP, PITCH, LANES), f32),
            pltpu.VMEM((nf, CAP, PITCH, LANES), f32),
            pltpu.VMEM((nf, CAP, ny, LANES), f32),
            pltpu.SemaphoreType.DMA((3, tiles)),
        ],
        compiler_params=pltpu.CompilerParams(vmem_limit_bytes=24 * 1024 * 1024),
        name="finish",
    )(*between)


def solution(mesh):
    return jax.shard_map(
        local,
        mesh=mesh,
        in_specs=(
            P("dom", None, None, "space"),
            P(),
            P("dom", None, "space"),
            P(None, "space"),
            P(None, "space"),
        ),
        out_specs=P("dom", None, None, "space"),
        check_vma=False,
    )
```

```python
import functools

import jax
import jax.numpy as jnp
from jax import lax
from jax.experimental import pallas as pl
from jax.experimental.pallas import tpu as pltpu
from jax.sharding import PartitionSpec as P

MESH = pl.DeviceIdType.MESH
STEPS = 3
CAP = 2
EDGE = 2 * STEPS
LANES = 128
TOP = 8
PITCH = 32
UNIT = 4
HALF = 8
PAIRS = 7
RUN = 8
AHEAD = 4
NEED = (EDGE, EDGE - 1, EDGE, EDGE - 3)
SHELF = (0, 12, 6, 17)
SLOT_LANES = 20
TRIPLE = 3
E_, N_, H_, C_ = range(4)


def lane_of(shape):
    return lax.broadcasted_iota(jnp.int32, shape, len(shape) - 1)


def east(cells, joined):
    turned = pltpu.roll(cells, LANES - 1, 2)
    if not joined:
        return turned
    following = jnp.concatenate([turned[1:], turned[:1]], axis=0)
    return jnp.where(lane_of(cells.shape) == LANES - 1, following, turned)


def west(cells, joined):
    turned = pltpu.roll(cells, 1, 2)
    if not joined:
        return turned
    preceding = jnp.concatenate([turned[-1:], turned[:-1]], axis=0)
    return jnp.where(lane_of(cells.shape) == 0, preceding, turned)


def flow(read, wet, turn, joined):
    e, n, h = read(E_, 0), read(N_, 0), read(H_, 0)
    e_new = wet * (
        (5.5 * e + turn * n)
        + (read(E_, 1) + read(E_, -1))
        + (east(e - h, joined) + west(e + h, joined))
    )
    n_new = wet * (
        (5.5 * n - turn * e)
        + (east(n, joined) + west(n, joined))
        + ((read(N_, 1) - read(H_, 1)) + (read(N_, -1) + read(H_, -1)))
    )
    return e_new, n_new


def level(read, read_new, depth, pull, last, joined):
    e, n = read_new(E_, 0), read_new(N_, 0)
    spread = (east(e, joined) - west(e, joined)) + (read_new(N_, 1) - read_new(N_, -1))
    h_new = ((0.18 if last else 0.9) * read(H_, 0) + pull) - depth * spread
    c = read(C_, 0)
    c_east, c_west = east(c, joined), west(c, joined)
    c_north, c_south = read(C_, 1), read(C_, -1)
    c_new = (
        (6.0 * c + ((c_east + c_west) + (c_north + c_south)))
        - e * (c_east - c_west)
        - n * (c_north - c_south)
    )
    if last:
        c_new = 0.001 * c_new
    return h_new, c_new


def level_of(levels, observed):
    return (
        jnp.where(levels > 0, 0.1, 0.0).astype(jnp.float32),
        1.25 * levels,
        0.25 * levels,
        0.5 * observed,
        0.1 * observed,
    )


def turn_of(ny, y0):
    y = lax.broadcasted_iota(jnp.int32, (1, HALF, LANES), 1).astype(jnp.float32) + float(y0)
    return 2.0 * (0.2 + 0.6 * y / ny)


def all_steps(first, s1, s2, ground, keep, joined, ny, parts):
    wet, depth, pull = ground
    count = len(parts)
    for step in range(STEPS):
        last = step == STEPS - 1
        old, new = (None, s1) if step == 0 else (s1, s2) if step == 1 else (s2, s1)

        def reader(ref, i, y0):
            return lambda field, up: parts[i](ref, field, pl.ds(TOP + y0 + up, HALF))[...]

        def read(i, y0):
            return (lambda field, up: first(i, field, y0, up)) if step == 0 else reader(old, i, y0)

        for i in range(count):
            for y0 in range(0, ny, HALF):
                e, n = flow(read(i, y0), wet(y0), turn_of(ny, y0), joined)
                now = pl.ds(TOP + y0, HALF)
                parts[i](new, E_, now)[...] = e
                parts[i](new, N_, now)[...] = n
                if last:
                    keep(i, E_, y0, e)
                    keep(i, N_, y0, n)
        for i in range(count):
            for y0 in range(0, ny, HALF):
                h, c = level(read(i, y0), reader(new, i, y0), depth(last, y0), pull(last, y0), last, joined)
                now = pl.ds(TOP + y0, HALF)
                if last:
                    keep(i, H_, y0, h)
                    keep(i, C_, y0, c)
                else:
                    parts[i](new, H_, now)[...] = h
                    parts[i](new, C_, now)[...] = c


def slot_parts():
    return [lambda ref, field, now, s=s: ref.at[s, field, :, now] for s in range(UNIT)]


def row_ground(gw, gd, go):
    return (
        lambda y0: gw[:, pl.ds(y0, HALF)],
        lambda last, y0: gd[int(last), :, pl.ds(y0, HALF)],
        lambda last, y0: go[int(last), :, pl.ds(y0, HALF)],
    )


def strip_ground(gs):
    return (
        lambda y0: gs[0, pl.ds(y0, HALF)][None],
        lambda last, y0: gs[2 if last else 1, pl.ds(y0, HALF)][None],
        lambda last, y0: gs[4 if last else 3, pl.ds(y0, HALF)][None],
    )


def step_strips(b0, b1, b2, b3, gs, groups, ny):
    parts = [lambda ref, field, now, g=g: ref.at[field, g, now] for g in groups]

    def keep(i, field, y0, value):
        b3[field, groups[i], pl.ds(y0, HALF)] = value

    all_steps(
        lambda i, field, y0, up: b0[field, groups[i], pl.ds(TOP + y0 + up, HALF)],
        b1, b2, strip_ground(gs), keep, False, ny, parts,
    )


def put_strips(b3, p, slots, out):
    done = b3[:, p]
    lane = lane_of(done.shape)
    final = out.shape[2] - 1
    for s, j in enumerate(slots):
        base = 64 * s
        at_left = pltpu.roll(done, LANES - EDGE - base, 2)
        at_right = pltpu.roll(done, (LANES - EDGE - (base + 32 + EDGE)) % LANES, 2)
        pltpu.store(out.at[j, :, 0], at_left, mask=lane < EDGE)
        pltpu.store(out.at[j, :, final], at_right, mask=lane >= LANES - EDGE)


def clear_rows(ref, ny):
    @pl.loop(0, ref.shape[0])
    def _(i):
        blank = jnp.zeros(ref.shape[1:-2] + (8, LANES), jnp.float32)
        ref[i, ..., TOP - 8 : TOP, :] = blank
        ref[i, ..., TOP + ny : TOP + ny + 8, :] = blank


def kernel(
    anc_in, ens, pert, lev, obs, out, late0, late_strips, gs, gw, gd, go,
    anc, ends_of, inner, ext, h0, pv, lv, ov, s1, s2, b0, b1, b2, b3, out1, in1, edge_out, edge_in,
    in_sem, dom_out_sem, dom_in_sem, msg_out_sem, msg_in_sem, edge_out_sem, edge_in_sem,
):
    pd = ens.shape[0]
    ny = ens.shape[2]
    tiles = ens.shape[3] // LANES
    doms, spaces = lax.axis_size("dom"), lax.axis_size("space")
    k, me = lax.axis_index("dom"), lax.axis_index("space")
    prev_space, next_space = lax.rem(me + spaces - 1, spaces), lax.rem(me + 1, spaces)
    early = pd - 2 * CAP
    rows = slice(TOP, TOP + ny)

    barrier = pltpu.get_barrier_semaphore()

    def greet(dom, *spaces_there):
        for space in spaces_there:
            pl.semaphore_signal(barrier, inc=1, device_id=(dom, space), device_id_type=MESH)

    greet(k, prev_space, next_space)

    @pl.when(k > 0)
    def _():
        greet(k - 1, me, prev_space, next_space)

    @pl.when(k < doms - 1)
    def _():
        greet(k + 1, me, prev_space, next_space)

    def tile(q):
        return pl.ds(q * LANES, LANES)

    needed_first, needed_next = [pltpu.make_async_copy(anc_in, anc, in_sem.at[4, 0])], []
    for q in (0, tiles - 1, *range(1, tiles - 1)):
        at_end = q in (0, tiles - 1)
        loads = needed_first if at_end else needed_next
        here = ends_of.at[:, :, int(q > 0), rows] if at_end else inner.at[:, :, q - 1, rows]
        loads.append(pltpu.make_async_copy(ens.at[:, :, :, tile(q)], here, in_sem.at[3, q]))
        loads.append(pltpu.make_async_copy(pert.at[:, :, tile(q)], pv.at[:, q], in_sem.at[2, q]))
        loads.append(pltpu.make_async_copy(lev.at[:, tile(q)], lv.at[q], in_sem.at[0, q]))
        loads.append(pltpu.make_async_copy(obs.at[:, tile(q)], ov.at[q], in_sem.at[1, q]))
    for copy in needed_first + needed_next:
        copy.start()

    for ref in (ends_of, inner, h0, late0, s1, s2, b0, b1, b2, late_strips):
        clear_rows(ref, ny)

    for copy in needed_first:
        copy.wait()

    def from_own(j):
        return jnp.clip(anc[k * pd + j] - k * pd, 0, pd - 1)

    def from_ext(j, low):
        parent = anc[k * pd + j]
        if low:
            return jnp.where(k == 0, j, jnp.clip(parent - (k * pd - CAP), 0, CAP - 1))
        return jnp.where(
            k == doms - 1, j - (pd - 2 * CAP), jnp.clip(parent - (k + 1) * pd, 0, CAP - 1) + CAP
        )

    def column(i, j, side):
        h = 5.0 * (ends_of[i, H_, side, rows] + pv[j, side * (tiles - 1)])
        return jnp.concatenate(
            [ends_of[i, E_ : N_ + 1, side, rows], h[None], ends_of[i, C_:, side, rows]], axis=0
        )

    flat = lane_of((ny, LANES))

    def message(rightward):
        return pltpu.make_async_remote_copy(
            src_ref=out1.at[int(rightward)],
            dst_ref=in1.at[int(rightward)],
            send_sem=msg_out_sem.at[int(rightward)],
            recv_sem=msg_in_sem.at[int(rightward)],
            device_id=(k, next_space if rightward else prev_space),
            device_id_type=MESH,
        )

    edge_to = (jnp.where(k < doms - 1, k + 1, k), jnp.where(k > 0, k - 1, k))
    edge_side = (jnp.where(k < doms - 1, 0, 1), jnp.where(k > 0, 1, 0))

    def edge_particle(up, t):
        if up:
            return jnp.where(k < doms - 1, pd - CAP + t, from_own(pd - CAP + t))
        return jnp.where(k > 0, t, from_own(t))

    def edge_message(up, rightward):
        at = 0 if up else 1
        return pltpu.make_async_remote_copy(
            src_ref=edge_out.at[at, int(rightward)],
            dst_ref=edge_in.at[edge_side[at], int(rightward)],
            send_sem=edge_out_sem.at[at, int(rightward)],
            recv_sem=edge_in_sem.at[edge_side[at], int(rightward)],
            device_id=(edge_to[at], next_space if rightward else prev_space),
            device_id_type=MESH,
        )

    def edge_arrival(side, rightward):
        return pltpu.make_async_remote_copy(
            src_ref=edge_out.at[side, int(rightward)],
            dst_ref=edge_in.at[side, int(rightward)],
            send_sem=edge_out_sem.at[side, int(rightward)],
            recv_sem=edge_in_sem.at[side, int(rightward)],
            device_id=(k, next_space if rightward else prev_space),
            device_id_type=MESH,
        )

    def shelve(columns, side, at, tile_so_far):
        for f in range(4):
            first = LANES - NEED[f] if side else 0
            to = at + SHELF[f]
            chosen = (flat >= to) & (flat < to + NEED[f])
            tile_so_far = jnp.where(chosen, pltpu.roll(columns[f], (to - first) % LANES, 1), tile_so_far)
        return tile_so_far

    shelves = -(-PAIRS // TRIPLE)

    @pl.loop(0, early // (2 * PAIRS))
    def _(m):
        for r in range(shelves):
            packed = [jnp.zeros((ny, LANES), jnp.float32)] * 2
            for p in range(TRIPLE * r, min(PAIRS, TRIPLE * r + TRIPLE)):
                for s in range(2):
                    j = CAP + 2 * (PAIRS * m + p) + s
                    i = from_own(j)
                    for side in range(2):
                        at = 64 * s + SLOT_LANES * (p - TRIPLE * r)
                        packed[side] = shelve(column(i, j, side), side, at, packed[side])
            for side in range(2):
                out1[side, shelves * m + r] = packed[side]

    extra = shelves * (early // (2 * PAIRS))
    late = [pd - 2, pd - 1, 0, 1]
    for rightward in range(2):
        q, end = (tiles - 1, EDGE) if rightward else (0, 0)
        got = jnp.zeros((ny, LANES), jnp.float32)
        parts = [(lv[q].astype(jnp.float32), at) for at in (0, 64)] + [(ov[q], at) for at in (8, 72)]
        parts += [(5.0 * pv[j, q], 64 * (t % 2) + 16 + 8 * (t // 2)) for t, j in enumerate(late)]
        for part, at in parts:
            got = jnp.where((flat >= at) & (flat < at + EDGE), pltpu.roll(part, at + end, 1), got)
        out1[rightward, extra] = got
        for up in (True, False):
            got = jnp.zeros((ny, LANES), jnp.float32)
            for t in range(CAP):
                i = edge_particle(up, t)
                columns = [ends_of[i, f, rightward, rows] for f in range(4)]
                columns[H_] = 5.0 * columns[H_]
                got = shelve(columns, rightward, 64 * t, got)
            edge_out[0 if up else 1, rightward] = got

    def dom_copy(up, t):
        first, lands, to = (pd - CAP, 0, k + 1) if up else (0, CAP, k - 1)
        return pltpu.make_async_remote_copy(
            src_ref=ens.at[first + t],
            dst_ref=ext.at[lands + t],
            send_sem=dom_out_sem.at[int(up), t],
            recv_sem=dom_in_sem.at[int(up), t],
            device_id=(to, me),
            device_id_type=MESH,
        )

    def send_particles(up, on):
        @pl.when(on)
        def _():
            for t in range(CAP):
                dom_copy(up, t).start()

    odd = lax.rem(k, 2) == 1

    def send():
        pl.semaphore_wait(barrier, 2 + jnp.where(k > 0, 3, 0) + jnp.where(k < doms - 1, 3, 0))
        for rightward in (True, False):
            message(rightward).start()
            for up in (False, True):
                edge_message(up, rightward).start()
        send_particles(True, odd & (k < doms - 1))
        send_particles(False, jnp.logical_not(odd) & (k > 0))
        send_particles(True, jnp.logical_not(odd))
        send_particles(False, odd)

    ahead = lax.rem(me, RUN) == 0
    pl.when(jnp.logical_not(ahead))(send)

    for copy in needed_next:
        copy.wait()

    levels = lv[...].astype(jnp.float32)
    gw[...], gd[0], gd[1], go[0], go[1] = level_of(levels, ov[...])

    def whole_rows(i, f, at):
        return jnp.concatenate([ends_of[i, f, :1, at], inner[i, f, :, at], ends_of[i, f, 1:, at]], axis=0)

    @pl.loop(0, early // UNIT)
    def _(u):
        for s in range(UNIT):
            j = CAP + u * UNIT + s
            h0[j, :, rows] = 5.0 * (whole_rows(from_own(j), H_, rows) + pv[j])

    @pl.loop(0, early // UNIT)
    def _(u):
        pl.when(ahead & (u == AHEAD))(send)
        slots = [CAP + u * UNIT + s for s in range(UNIT)]
        where = [from_own(j) for j in slots]

        def first(i, field, y0, up):
            at = pl.ds(TOP + y0 + up, HALF)
            return h0[slots[i], :, at] if field == H_ else whole_rows(where[i], field, at)

        def keep(i, field, y0, value):
            out[slots[i], field, :, pl.ds(y0, HALF)] = value

        all_steps(first, s1, s2, row_ground(gw, gd, go), keep, True, ny, slot_parts())

    for rightward in (False, True):
        message(rightward).wait_recv()

    def ends(first, final, s, tile_so_far):
        base = 64 * s
        lane = lane_of(first.shape)
        chosen = (lane >= base + EDGE) & (lane < base + 3 * EDGE)
        tile_so_far = jnp.where(chosen, pltpu.roll(first, base + EDGE, 2), tile_so_far)
        chosen = (lane >= base + 32) & (lane < base + 32 + 2 * EDGE)
        return jnp.where(chosen, pltpu.roll(final, (base + 32 + 2 * EDGE) % LANES, 2), tile_so_far)

    def beyond(from_left, from_right, at, width=EDGE):
        half = lax.rem(lane_of(from_left.shape), 64)
        chosen = (half >= EDGE - width) & (half < EDGE)
        got = jnp.where(chosen, pltpu.roll(from_left, (LANES + EDGE - width - at) % LANES, 1), 0.0)
        chosen = (half >= 44) & (half < 44 + width)
        return jnp.where(chosen, pltpu.roll(from_right, (LANES + 44 - at) % LANES, 1), got)

    def unshelved(from_left, from_right, at):
        return [beyond(from_left, from_right, at + SHELF[f], NEED[f]) for f in range(4)]

    fields = []
    for i, field in enumerate((levels, ov[...])):
        got = beyond(in1[1, extra], in1[0, extra], 8 * i)[None]
        for s in range(2):
            got = ends(field[:1], field[tiles - 1 :], s, got)
        fields.append(got[0])
    gs[0], gs[1], gs[2], gs[3], gs[4] = level_of(*fields)

    @pl.loop(0, early // (2 * PAIRS))
    def _(m):
        slots = [[CAP + 2 * (PAIRS * m + p) + s for s in range(2)] for p in range(PAIRS)]
        for p in range(PAIRS):
            r = shelves * m + p // TRIPLE
            got = jnp.stack(unshelved(in1[1, r], in1[0, r], SLOT_LANES * (p % TRIPLE)))
            for s, j in enumerate(slots[p]):
                i = from_own(j)
                got = ends(column(i, j, 0), column(i, j, 1), s, got)
            b0[:, p, rows] = got
        step_strips(b0, b1, b2, b3, gs, [slice(0, 4), slice(4, PAIRS)], ny)
        for p in range(PAIRS):
            put_strips(b3, p, slots[p], out)

    @pl.when(k > 0)
    def _():
        for t in range(CAP):
            dom_copy(True, t).wait_recv()

    @pl.when(k < doms - 1)
    def _():
        for t in range(CAP):
            dom_copy(False, t).wait_recv()

    def own_particle(lands, j):
        for f in range(4):
            state = whole_rows(from_own(j), f, rows)
            for q in range(tiles):
                ext[lands, f, :, tile(q)] = state[q]

    @pl.when(k == 0)
    def _():
        for s in range(CAP):
            own_particle(s, s)

    @pl.when(k == doms - 1)
    def _():
        for s in range(CAP, 2 * CAP):
            own_particle(s, pd - 2 * CAP + s)

    late_from = [from_ext(j, j < CAP) for j in late]
    for t, j in enumerate(late):
        for f in range(4):
            state = jnp.stack([ext[late_from[t], f, :, tile(q)] for q in range(tiles)])
            late0[t, f, :, rows] = 5.0 * (state + pv[j]) if f == H_ else state

    for side in range(2):
        for rightward in (False, True):
            edge_arrival(side, rightward).wait_recv()
    for p in range(2):
        side = 1 - p
        where = [late_from[2 * p + s] - CAP * side for s in range(2)]
        ways = []
        for w in range(2):
            came = edge_in[side, w]
            turned = pltpu.roll(came, 64, 1)
            ways.append(jnp.where(flat < 64, *(jnp.where(where[s] == s, came, turned) for s in range(2))))
        got = unshelved(ways[1], ways[0], 0)
        got[H_] = got[H_] + beyond(in1[1, extra], in1[0, extra], 16 + 8 * p)
        got = jnp.stack(got)
        for s in range(2):
            got = ends(late0[2 * p + s, :, 0, rows], late0[2 * p + s, :, tiles - 1, rows], s, got)
        late_strips[:, p, rows] = got

    for rightward in (False, True):
        message(rightward).wait_send()
        for up in (False, True):
            edge_message(up, rightward).wait_send()

    @pl.when(k < doms - 1)
    def _():
        for t in range(CAP):
            dom_copy(True, t).wait_send()

    @pl.when(k > 0)
    def _():
        for t in range(CAP):
            dom_copy(False, t).wait_send()


def finish(made, late0, late_strips, gs, gw, gd, go, out, late_out, s1, s2, b1, b2, b3, sem):
    pd, nf, tiles, ny, _ = made.shape

    def tile(q):
        return pl.ds(q * LANES, LANES)

    copies = [
        pltpu.make_async_copy(made.at[CAP : pd - CAP, :, q], out.at[CAP : pd - CAP, :, :, tile(q)], sem.at[0, q])
        for q in range(tiles)
    ]
    for copy in copies:
        copy.start()
    for ref in (s1, s2, b1, b2):
        clear_rows(ref, ny)

    def keep(i, field, y0, value):
        late_out[i, field, :, pl.ds(y0, HALF)] = value

    all_steps(
        lambda i, field, y0, up: late0[i, field, :, pl.ds(TOP + y0 + up, HALF)],
        s1, s2, row_ground(gw, gd, go), keep, True, ny, slot_parts(),
    )
    step_strips(late_strips, b1, b2, b3, gs, [slice(0, CAP)], ny)
    for p in range(2):
        put_strips(b3, p, [2 * p, 2 * p + 1], late_out)
    for p, first in enumerate((pd - CAP, 0)):
        for q in range(tiles):
            copy = pltpu.make_async_copy(
                late_out.at[CAP * p : CAP * p + CAP, :, q], out.at[first : first + CAP, :, :, tile(q)], sem.at[1 + p, q]
            )
            copy.start()
            copies.append(copy)
    for copy in copies:
        copy.wait()


def local(ensemble, ancestors, perturbation, levels, observed):
    pd, nf, ny, nx = ensemble.shape
    tiles = nx // LANES
    f32 = jnp.float32
    hbm = pl.BlockSpec(memory_space=pl.ANY)
    vmem = pl.BlockSpec(memory_space=pltpu.VMEM)
    state = (UNIT, nf, tiles, PITCH, LANES)
    handed = [
        pltpu.VMEM((pd, nf, tiles, ny, LANES), f32),
        pltpu.VMEM(state, f32),
        pltpu.VMEM((nf, CAP, PITCH, LANES), f32),
        pltpu.VMEM((5, ny, LANES), f32),
        pltpu.VMEM((tiles, ny, LANES), f32),
        pltpu.VMEM((2, tiles, ny, LANES), f32),
        pltpu.VMEM((2, tiles, ny, LANES), f32),
    ]
    between = pl.pallas_call(
        kernel,
        out_shape=handed,
        in_specs=[hbm] * 5,
        out_specs=[vmem] * len(handed),
        scratch_shapes=[
            pltpu.SMEM(ancestors.shape, jnp.int32),
            pltpu.VMEM((pd, nf, 2, PITCH, LANES), f32),
            pltpu.VMEM((pd, nf, tiles - 2, PITCH, LANES), f32),
            pltpu.VMEM((2 * CAP, nf, ny, nx), f32),
            pltpu.VMEM((pd, tiles, PITCH, LANES), f32),
            pltpu.VMEM((pd, tiles, ny, LANES), f32),
            pltpu.VMEM((tiles, ny, LANES), jnp.int32),
            pltpu.VMEM((tiles, ny, LANES), f32),
            pltpu.VMEM(state, f32),
            pltpu.VMEM(state, f32),
            pltpu.VMEM((nf, PAIRS, PITCH, LANES), f32),
            pltpu.VMEM((nf, PAIRS, PITCH, LANES), f32),
            pltpu.VMEM((nf, PAIRS, PITCH, LANES), f32),
            pltpu.VMEM((nf, PAIRS, ny, LANES), f32),
            pltpu.VMEM((2, 7, ny, LANES), f32),
            pltpu.VMEM((2, 7, ny, LANES), f32),
            pltpu.VMEM((2, 2, ny, LANES), f32),
            pltpu.VMEM((2, 2, ny, LANES), f32),
            pltpu.SemaphoreType.DMA((5, tiles)),
            pltpu.SemaphoreType.DMA((2, CAP)),
            pltpu.SemaphoreType.DMA((2, CAP)),
            pltpu.SemaphoreType.DMA((2,)),
            pltpu.SemaphoreType.DMA((2,)),
            pltpu.SemaphoreType.DMA((2, 2)),
            pltpu.SemaphoreType.DMA((2, 2)),
        ],
        compiler_params=pltpu.CompilerParams(
            collective_id=0, has_side_effects=True, vmem_limit_bytes=40 * 1024 * 1024
        ),
        name="resample_and_step",
    )(*(pltpu.with_memory_space_constraint(x, pltpu.HBM) for x in (ancestors, ensemble, perturbation, levels, observed)))
    return pl.pallas_call(
        finish,
        out_shape=jax.ShapeDtypeStruct((pd, nf, ny, nx), f32),
        in_specs=[vmem] * len(handed),
        out_specs=hbm,
        scratch_shapes=[
            pltpu.VMEM((UNIT, nf, tiles, ny, LANES), f32),
            pltpu.VMEM(state, f32),
            pltpu.VMEM(state, f32),
            pltpu.VMEM((nf, CAP, PITCH, LANES), f32),
            pltpu.VMEM((nf, CAP, PITCH, LANES), f32),
            pltpu.VMEM((nf, CAP, ny, LANES), f32),
            pltpu.SemaphoreType.DMA((3, tiles)),
        ],
        compiler_params=pltpu.CompilerParams(vmem_limit_bytes=24 * 1024 * 1024),
        name="finish",
    )(*between)


def solution(mesh):
    return jax.shard_map(
        local,
        mesh=mesh,
        in_specs=(
            P("dom", None, None, "space"),
            P(),
            P("dom", None, "space"),
            P(None, "space"),
            P(None, "space"),
        ),
        out_specs=P("dom", None, None, "space"),
        check_vma=False,
    )
```

```python
import functools

import jax
import jax.numpy as jnp
from jax import lax
from jax.experimental import pallas as pl
from jax.experimental.pallas import tpu as pltpu
from jax.sharding import PartitionSpec as P

MESH = pl.DeviceIdType.MESH
STEPS = 3
CAP = 2
EDGE = 2 * STEPS
LANES = 128
TOP = 8
PITCH = 32
UNIT = 4
HALF = 8
PAIRS = 7
RUN = 8
LAGS = 4
AHEAD = (6, 3)
NEED = (EDGE, EDGE - 1, EDGE, EDGE - 3)
SHELF = (0, 12, 6, 17)
SLOT_LANES = 20
TRIPLE = 3
E_, N_, H_, C_ = range(4)


def lane_of(shape):
    return lax.broadcasted_iota(jnp.int32, shape, len(shape) - 1)


def east(cells, joined):
    turned = pltpu.roll(cells, LANES - 1, 2)
    if not joined:
        return turned
    following = jnp.concatenate([turned[1:], turned[:1]], axis=0)
    return jnp.where(lane_of(cells.shape) == LANES - 1, following, turned)


def west(cells, joined):
    turned = pltpu.roll(cells, 1, 2)
    if not joined:
        return turned
    preceding = jnp.concatenate([turned[-1:], turned[:-1]], axis=0)
    return jnp.where(lane_of(cells.shape) == 0, preceding, turned)


def flow(read, wet, turn, joined):
    e, n, h = read(E_, 0), read(N_, 0), read(H_, 0)
    e_new = wet * (
        (5.5 * e + turn * n)
        + (read(E_, 1) + read(E_, -1))
        + (east(e - h, joined) + west(e + h, joined))
    )
    n_new = wet * (
        (5.5 * n - turn * e)
        + (east(n, joined) + west(n, joined))
        + ((read(N_, 1) - read(H_, 1)) + (read(N_, -1) + read(H_, -1)))
    )
    return e_new, n_new


def level(read, read_new, depth, pull, last, joined):
    e, n = read_new(E_, 0), read_new(N_, 0)
    spread = (east(e, joined) - west(e, joined)) + (read_new(N_, 1) - read_new(N_, -1))
    h_new = ((0.18 if last else 0.9) * read(H_, 0) + pull) - depth * spread
    c = read(C_, 0)
    c_east, c_west = east(c, joined), west(c, joined)
    c_north, c_south = read(C_, 1), read(C_, -1)
    c_new = (
        (6.0 * c + ((c_east + c_west) + (c_north + c_south)))
        - e * (c_east - c_west)
        - n * (c_north - c_south)
    )
    if last:
        c_new = 0.001 * c_new
    return h_new, c_new


def level_of(levels, observed):
    return (
        jnp.where(levels > 0, 0.1, 0.0).astype(jnp.float32),
        1.25 * levels,
        0.25 * levels,
        0.5 * observed,
        0.1 * observed,
    )


def turn_of(ny, y0):
    y = lax.broadcasted_iota(jnp.int32, (1, HALF, LANES), 1).astype(jnp.float32) + float(y0)
    return 2.0 * (0.2 + 0.6 * y / ny)


def all_steps(first, s1, s2, ground, keep, joined, ny, parts):
    wet, depth, pull = ground
    count = len(parts)
    for step in range(STEPS):
        last = step == STEPS - 1
        old, new = (None, s1) if step == 0 else (s1, s2) if step == 1 else (s2, s1)

        def reader(ref, i, y0):
            return lambda field, up: parts[i](ref, field, pl.ds(TOP + y0 + up, HALF))[...]

        def read(i, y0):
            return (lambda field, up: first(i, field, y0, up)) if step == 0 else reader(old, i, y0)

        for i in range(count):
            for y0 in range(0, ny, HALF):
                e, n = flow(read(i, y0), wet(y0), turn_of(ny, y0), joined)
                now = pl.ds(TOP + y0, HALF)
                parts[i](new, E_, now)[...] = e
                parts[i](new, N_, now)[...] = n
                if last:
                    keep(i, E_, y0, e)
                    keep(i, N_, y0, n)
        for i in range(count):
            for y0 in range(0, ny, HALF):
                h, c = level(read(i, y0), reader(new, i, y0), depth(last, y0), pull(last, y0), last, joined)
                now = pl.ds(TOP + y0, HALF)
                if last:
                    keep(i, H_, y0, h)
                    keep(i, C_, y0, c)
                else:
                    parts[i](new, H_, now)[...] = h
                    parts[i](new, C_, now)[...] = c


def slot_parts():
    return [lambda ref, field, now, s=s: ref.at[s, field, :, now] for s in range(UNIT)]


def row_ground(gw, gd, go):
    return (
        lambda y0: gw[:, pl.ds(y0, HALF)],
        lambda last, y0: gd[int(last), :, pl.ds(y0, HALF)],
        lambda last, y0: go[int(last), :, pl.ds(y0, HALF)],
    )


def strip_ground(gs):
    return (
        lambda y0: gs[0, pl.ds(y0, HALF)][None],
        lambda last, y0: gs[2 if last else 1, pl.ds(y0, HALF)][None],
        lambda last, y0: gs[4 if last else 3, pl.ds(y0, HALF)][None],
    )


def step_strips(b0, b1, b2, b3, gs, groups, ny):
    parts = [lambda ref, field, now, g=g: ref.at[field, g, now] for g in groups]

    def keep(i, field, y0, value):
        b3[field, groups[i], pl.ds(y0, HALF)] = value

    all_steps(
        lambda i, field, y0, up: b0[field, groups[i], pl.ds(TOP + y0 + up, HALF)],
        b1, b2, strip_ground(gs), keep, False, ny, parts,
    )


def put_strips(b3, p, slots, out):
    done = b3[:, p]
    lane = lane_of(done.shape)
    final = out.shape[2] - 1
    for s, j in enumerate(slots):
        base = 64 * s
        at_left = pltpu.roll(done, LANES - EDGE - base, 2)
        at_right = pltpu.roll(done, (LANES - EDGE - (base + 32 + EDGE)) % LANES, 2)
        pltpu.store(out.at[j, :, 0], at_left, mask=lane < EDGE)
        pltpu.store(out.at[j, :, final], at_right, mask=lane >= LANES - EDGE)


def clear_rows(ref, ny):
    @pl.loop(0, ref.shape[0])
    def _(i):
        blank = jnp.zeros(ref.shape[1:-2] + (8, LANES), jnp.float32)
        ref[i, ..., TOP - 8 : TOP, :] = blank
        ref[i, ..., TOP + ny : TOP + ny + 8, :] = blank


def kernel(
    anc_in, ens, pert, lev, obs, out, late0, late_strips, gs, gw, gd, go,
    anc, ends_of, inner, ext, h0, pv, lv, ov, s1, s2, b0, b1, b2, b3, out1, in1, edge_out, edge_in,
    in_sem, dom_out_sem, dom_in_sem, msg_out_sem, msg_in_sem, edge_out_sem, edge_in_sem, entered,
):
    pd = ens.shape[0]
    ny = ens.shape[2]
    tiles = ens.shape[3] // LANES
    doms, spaces = lax.axis_size("dom"), lax.axis_size("space")
    k, me = lax.axis_index("dom"), lax.axis_index("space")
    prev_space, next_space = lax.rem(me + spaces - 1, spaces), lax.rem(me + 1, spaces)
    early = pd - 2 * CAP
    rows = slice(TOP, TOP + ny)

    barrier = pltpu.get_barrier_semaphore()

    def signal(semaphore, dom, space):
        pl.semaphore_signal(semaphore, inc=1, device_id=(dom, space), device_id_type=MESH)

    def signal_side(semaphore, rightward):
        space = next_space if rightward else prev_space
        signal(semaphore, k, space)

        @pl.when(k > 0)
        def _():
            signal(semaphore, k - 1, space)

        @pl.when(k < doms - 1)
        def _():
            signal(semaphore, k + 1, space)

    place = lax.rem(me, RUN)
    late_side = (place == 0, place < LAGS)
    ahead_side = ((place > 0) & (place <= LAGS), place == RUN - 1)
    dom_peers = jnp.where(k > 0, 1, 0) + jnp.where(k < doms - 1, 1, 0)
    side_peers = 1 + dom_peers

    @pl.when(k > 0)
    def _():
        signal(barrier, k - 1, me)

    @pl.when(k < doms - 1)
    def _():
        signal(barrier, k + 1, me)

    for side in range(2):
        pl.when(jnp.logical_not(ahead_side[side]))(functools.partial(signal_side, barrier, side))

    def tile(q):
        return pl.ds(q * LANES, LANES)

    needed_first, needed_next = [pltpu.make_async_copy(anc_in, anc, in_sem.at[4, 0])], []
    for q in (0, tiles - 1, *range(1, tiles - 1)):
        at_end = q in (0, tiles - 1)
        loads = needed_first if at_end else needed_next
        here = ends_of.at[:, :, int(q > 0), rows] if at_end else inner.at[:, :, q - 1, rows]
        loads.append(pltpu.make_async_copy(ens.at[:, :, :, tile(q)], here, in_sem.at[3, q]))
        loads.append(pltpu.make_async_copy(pert.at[:, :, tile(q)], pv.at[:, q], in_sem.at[2, q]))
        loads.append(pltpu.make_async_copy(lev.at[:, tile(q)], lv.at[q], in_sem.at[0, q]))
        loads.append(pltpu.make_async_copy(obs.at[:, tile(q)], ov.at[q], in_sem.at[1, q]))
    for copy in needed_first + needed_next:
        copy.start()

    for ref in (ends_of, inner, h0, late0, s1, s2, b0, b1, b2, late_strips):
        clear_rows(ref, ny)

    for copy in needed_first:
        copy.wait()

    def from_own(j):
        return jnp.clip(anc[k * pd + j] - k * pd, 0, pd - 1)

    def from_ext(j, low):
        parent = anc[k * pd + j]
        if low:
            return jnp.where(k == 0, j, jnp.clip(parent - (k * pd - CAP), 0, CAP - 1))
        return jnp.where(
            k == doms - 1, j - (pd - 2 * CAP), jnp.clip(parent - (k + 1) * pd, 0, CAP - 1) + CAP
        )

    def column(i, j, side):
        h = 5.0 * (ends_of[i, H_, side, rows] + pv[j, side * (tiles - 1)])
        return jnp.concatenate(
            [ends_of[i, E_ : N_ + 1, side, rows], h[None], ends_of[i, C_:, side, rows]], axis=0
        )

    flat = lane_of((ny, LANES))

    def message(rightward):
        return pltpu.make_async_remote_copy(
            src_ref=out1.at[int(rightward)],
            dst_ref=in1.at[int(rightward)],
            send_sem=msg_out_sem.at[int(rightward)],
            recv_sem=msg_in_sem.at[int(rightward)],
            device_id=(k, next_space if rightward else prev_space),
            device_id_type=MESH,
        )

    edge_to = (jnp.where(k < doms - 1, k + 1, k), jnp.where(k > 0, k - 1, k))
    edge_side = (jnp.where(k < doms - 1, 0, 1), jnp.where(k > 0, 1, 0))

    def edge_particle(up, t):
        if up:
            return jnp.where(k < doms - 1, pd - CAP + t, from_own(pd - CAP + t))
        return jnp.where(k > 0, t, from_own(t))

    def edge_message(up, rightward):
        at = 0 if up else 1
        return pltpu.make_async_remote_copy(
            src_ref=edge_out.at[at, int(rightward)],
            dst_ref=edge_in.at[edge_side[at], int(rightward)],
            send_sem=edge_out_sem.at[at, int(rightward)],
            recv_sem=edge_in_sem.at[edge_side[at], int(rightward)],
            device_id=(edge_to[at], next_space if rightward else prev_space),
            device_id_type=MESH,
        )

    def edge_arrival(side, rightward):
        return pltpu.make_async_remote_copy(
            src_ref=edge_out.at[side, int(rightward)],
            dst_ref=edge_in.at[side, int(rightward)],
            send_sem=edge_out_sem.at[side, int(rightward)],
            recv_sem=edge_in_sem.at[side, int(rightward)],
            device_id=(k, next_space if rightward else prev_space),
            device_id_type=MESH,
        )

    def shelve(columns, side, at, tile_so_far):
        for f in range(4):
            first = LANES - NEED[f] if side else 0
            to = at + SHELF[f]
            chosen = (flat >= to) & (flat < to + NEED[f])
            tile_so_far = jnp.where(chosen, pltpu.roll(columns[f], (to - first) % LANES, 1), tile_so_far)
        return tile_so_far

    shelves = -(-PAIRS // TRIPLE)

    @pl.loop(0, early // (2 * PAIRS))
    def _(m):
        for r in range(shelves):
            packed = [jnp.zeros((ny, LANES), jnp.float32)] * 2
            for p in range(TRIPLE * r, min(PAIRS, TRIPLE * r + TRIPLE)):
                for s in range(2):
                    j = CAP + 2 * (PAIRS * m + p) + s
                    i = from_own(j)
                    for side in range(2):
                        at = 64 * s + SLOT_LANES * (p - TRIPLE * r)
                        packed[side] = shelve(column(i, j, side), side, at, packed[side])
            for side in range(2):
                out1[side, shelves * m + r] = packed[side]

    extra = shelves * (early // (2 * PAIRS))
    late = [pd - 2, pd - 1, 0, 1]
    for rightward in range(2):
        q, end = (tiles - 1, EDGE) if rightward else (0, 0)
        got = jnp.zeros((ny, LANES), jnp.float32)
        parts = [(lv[q].astype(jnp.float32), at) for at in (0, 64)] + [(ov[q], at) for at in (8, 72)]
        parts += [(5.0 * pv[j, q], 64 * (t % 2) + 16 + 8 * (t // 2)) for t, j in enumerate(late)]
        for part, at in parts:
            got = jnp.where((flat >= at) & (flat < at + EDGE), pltpu.roll(part, at + end, 1), got)
        out1[rightward, extra] = got
        for up in (True, False):
            got = jnp.zeros((ny, LANES), jnp.float32)
            for t in range(CAP):
                i = edge_particle(up, t)
                columns = [ends_of[i, f, rightward, rows] for f in range(4)]
                columns[H_] = 5.0 * columns[H_]
                got = shelve(columns, rightward, 64 * t, got)
            edge_out[0 if up else 1, rightward] = got

    def dom_copy(up, t):
        first, lands, to = (pd - CAP, 0, k + 1) if up else (0, CAP, k - 1)
        return pltpu.make_async_remote_copy(
            src_ref=ens.at[first + t],
            dst_ref=ext.at[lands + t],
            send_sem=dom_out_sem.at[int(up), t],
            recv_sem=dom_in_sem.at[int(up), t],
            device_id=(to, me),
            device_id_type=MESH,
        )

    def send_particles(up, on):
        @pl.when(on)
        def _():
            for t in range(CAP):
                dom_copy(up, t).start()

    odd = lax.rem(k, 2) == 1

    def send_side(rightward):
        message(rightward).start()
        for up in (False, True):
            edge_message(up, rightward).start()

    pl.semaphore_wait(
        barrier, dom_peers + sum(jnp.where(late_side[side], 0, side_peers) for side in range(2))
    )
    for side in (1, 0):
        pl.when(ahead_side[side])(functools.partial(signal_side, entered.at[1 - side], side))
    for side in (1, 0):
        pl.when(jnp.logical_not(late_side[side]))(functools.partial(send_side, side))
    send_particles(True, odd & (k < doms - 1))
    send_particles(False, jnp.logical_not(odd) & (k > 0))
    send_particles(True, jnp.logical_not(odd))
    send_particles(False, odd)

    def send_late(side):
        pl.semaphore_wait(entered.at[side], side_peers)
        send_side(side)

    for copy in needed_next:
        copy.wait()

    levels = lv[...].astype(jnp.float32)
    gw[...], gd[0], gd[1], go[0], go[1] = level_of(levels, ov[...])

    def whole_rows(i, f, at):
        return jnp.concatenate([ends_of[i, f, :1, at], inner[i, f, :, at], ends_of[i, f, 1:, at]], axis=0)

    @pl.loop(0, early // UNIT)
    def _(u):
        for s in range(UNIT):
            j = CAP + u * UNIT + s
            h0[j, :, rows] = 5.0 * (whole_rows(from_own(j), H_, rows) + pv[j])

    @pl.loop(0, early // UNIT)
    def _(u):
        for side in range(2):
            pl.when(late_side[side] & (u == AHEAD[side]))(functools.partial(send_late, side))
        slots = [CAP + u * UNIT + s for s in range(UNIT)]
        where = [from_own(j) for j in slots]

        def first(i, field, y0, up):
            at = pl.ds(TOP + y0 + up, HALF)
            return h0[slots[i], :, at] if field == H_ else whole_rows(where[i], field, at)

        def keep(i, field, y0, value):
            out[slots[i], field, :, pl.ds(y0, HALF)] = value

        all_steps(first, s1, s2, row_ground(gw, gd, go), keep, True, ny, slot_parts())

    for rightward in (False, True):
        message(rightward).wait_recv()

    def ends(first, final, s, tile_so_far):
        base = 64 * s
        lane = lane_of(first.shape)
        chosen = (lane >= base + EDGE) & (lane < base + 3 * EDGE)
        tile_so_far = jnp.where(chosen, pltpu.roll(first, base + EDGE, 2), tile_so_far)
        chosen = (lane >= base + 32) & (lane < base + 32 + 2 * EDGE)
        return jnp.where(chosen, pltpu.roll(final, (base + 32 + 2 * EDGE) % LANES, 2), tile_so_far)

    def beyond(from_left, from_right, at, width=EDGE):
        half = lax.rem(lane_of(from_left.shape), 64)
        chosen = (half >= EDGE - width) & (half < EDGE)
        got = jnp.where(chosen, pltpu.roll(from_left, (LANES + EDGE - width - at) % LANES, 1), 0.0)
        chosen = (half >= 44) & (half < 44 + width)
        return jnp.where(chosen, pltpu.roll(from_right, (LANES + 44 - at) % LANES, 1), got)

    def unshelved(from_left, from_right, at):
        return [beyond(from_left, from_right, at + SHELF[f], NEED[f]) for f in range(4)]

    fields = []
    for i, field in enumerate((levels, ov[...])):
        got = beyond(in1[1, extra], in1[0, extra], 8 * i)[None]
        for s in range(2):
            got = ends(field[:1], field[tiles - 1 :], s, got)
        fields.append(got[0])
    gs[0], gs[1], gs[2], gs[3], gs[4] = level_of(*fields)

    @pl.loop(0, early // (2 * PAIRS))
    def _(m):
        slots = [[CAP + 2 * (PAIRS * m + p) + s for s in range(2)] for p in range(PAIRS)]
        for p in range(PAIRS):
            r = shelves * m + p // TRIPLE
            got = jnp.stack(unshelved(in1[1, r], in1[0, r], SLOT_LANES * (p % TRIPLE)))
            for s, j in enumerate(slots[p]):
                i = from_own(j)
                got = ends(column(i, j, 0), column(i, j, 1), s, got)
            b0[:, p, rows] = got
        step_strips(b0, b1, b2, b3, gs, [slice(0, 4), slice(4, PAIRS)], ny)
        for p in range(PAIRS):
            put_strips(b3, p, slots[p], out)

    @pl.when(k > 0)
    def _():
        for t in range(CAP):
            dom_copy(True, t).wait_recv()

    @pl.when(k < doms - 1)
    def _():
        for t in range(CAP):
            dom_copy(False, t).wait_recv()

    def own_particle(lands, j):
        for f in range(4):
            state = whole_rows(from_own(j), f, rows)
            for q in range(tiles):
                ext[lands, f, :, tile(q)] = state[q]

    @pl.when(k == 0)
    def _():
        for s in range(CAP):
            own_particle(s, s)

    @pl.when(k == doms - 1)
    def _():
        for s in range(CAP, 2 * CAP):
            own_particle(s, pd - 2 * CAP + s)

    late_from = [from_ext(j, j < CAP) for j in late]
    for t, j in enumerate(late):
        for f in range(4):
            state = jnp.stack([ext[late_from[t], f, :, tile(q)] for q in range(tiles)])
            late0[t, f, :, rows] = 5.0 * (state + pv[j]) if f == H_ else state

    for side in range(2):
        for rightward in (False, True):
            edge_arrival(side, rightward).wait_recv()
    for p in range(2):
        side = 1 - p
        where = [late_from[2 * p + s] - CAP * side for s in range(2)]
        ways = []
        for w in range(2):
            came = edge_in[side, w]
            turned = pltpu.roll(came, 64, 1)
            ways.append(jnp.where(flat < 64, *(jnp.where(where[s] == s, came, turned) for s in range(2))))
        got = unshelved(ways[1], ways[0], 0)
        got[H_] = got[H_] + beyond(in1[1, extra], in1[0, extra], 16 + 8 * p)
        got = jnp.stack(got)
        for s in range(2):
            got = ends(late0[2 * p + s, :, 0, rows], late0[2 * p + s, :, tiles - 1, rows], s, got)
        late_strips[:, p, rows] = got

    for rightward in (False, True):
        message(rightward).wait_send()
        for up in (False, True):
            edge_message(up, rightward).wait_send()

    @pl.when(k < doms - 1)
    def _():
        for t in range(CAP):
            dom_copy(True, t).wait_send()

    @pl.when(k > 0)
    def _():
        for t in range(CAP):
            dom_copy(False, t).wait_send()


def finish(made, late0, late_strips, gs, gw, gd, go, out, late_out, s1, s2, b1, b2, b3, sem):
    pd, nf, tiles, ny, _ = made.shape

    def tile(q):
        return pl.ds(q * LANES, LANES)

    copies = [
        pltpu.make_async_copy(made.at[CAP : pd - CAP, :, q], out.at[CAP : pd - CAP, :, :, tile(q)], sem.at[0, q])
        for q in range(tiles)
    ]
    for copy in copies:
        copy.start()
    for ref in (s1, s2, b1, b2):
        clear_rows(ref, ny)

    def keep(i, field, y0, value):
        late_out[i, field, :, pl.ds(y0, HALF)] = value

    all_steps(
        lambda i, field, y0, up: late0[i, field, :, pl.ds(TOP + y0 + up, HALF)],
        s1, s2, row_ground(gw, gd, go), keep, True, ny, slot_parts(),
    )
    step_strips(late_strips, b1, b2, b3, gs, [slice(0, CAP)], ny)
    for p in range(2):
        put_strips(b3, p, [2 * p, 2 * p + 1], late_out)
    for p, first in enumerate((pd - CAP, 0)):
        for q in range(tiles):
            copy = pltpu.make_async_copy(
                late_out.at[CAP * p : CAP * p + CAP, :, q], out.at[first : first + CAP, :, :, tile(q)], sem.at[1 + p, q]
            )
            copy.start()
            copies.append(copy)
    for copy in copies:
        copy.wait()


def local(ensemble, ancestors, perturbation, levels, observed):
    pd, nf, ny, nx = ensemble.shape
    tiles = nx // LANES
    f32 = jnp.float32
    hbm = pl.BlockSpec(memory_space=pl.ANY)
    vmem = pl.BlockSpec(memory_space=pltpu.VMEM)
    state = (UNIT, nf, tiles, PITCH, LANES)
    handed = [
        pltpu.VMEM((pd, nf, tiles, ny, LANES), f32),
        pltpu.VMEM(state, f32),
        pltpu.VMEM((nf, CAP, PITCH, LANES), f32),
        pltpu.VMEM((5, ny, LANES), f32),
        pltpu.VMEM((tiles, ny, LANES), f32),
        pltpu.VMEM((2, tiles, ny, LANES), f32),
        pltpu.VMEM((2, tiles, ny, LANES), f32),
    ]
    between = pl.pallas_call(
        kernel,
        out_shape=handed,
        in_specs=[hbm] * 5,
        out_specs=[vmem] * len(handed),
        scratch_shapes=[
            pltpu.SMEM(ancestors.shape, jnp.int32),
            pltpu.VMEM((pd, nf, 2, PITCH, LANES), f32),
            pltpu.VMEM((pd, nf, tiles - 2, PITCH, LANES), f32),
            pltpu.VMEM((2 * CAP, nf, ny, nx), f32),
            pltpu.VMEM((pd, tiles, PITCH, LANES), f32),
            pltpu.VMEM((pd, tiles, ny, LANES), f32),
            pltpu.VMEM((tiles, ny, LANES), jnp.int32),
            pltpu.VMEM((tiles, ny, LANES), f32),
            pltpu.VMEM(state, f32),
            pltpu.VMEM(state, f32),
            pltpu.VMEM((nf, PAIRS, PITCH, LANES), f32),
            pltpu.VMEM((nf, PAIRS, PITCH, LANES), f32),
            pltpu.VMEM((nf, PAIRS, PITCH, LANES), f32),
            pltpu.VMEM((nf, PAIRS, ny, LANES), f32),
            pltpu.VMEM((2, 7, ny, LANES), f32),
            pltpu.VMEM((2, 7, ny, LANES), f32),
            pltpu.VMEM((2, 2, ny, LANES), f32),
            pltpu.VMEM((2, 2, ny, LANES), f32),
            pltpu.SemaphoreType.DMA((5, tiles)),
            pltpu.SemaphoreType.DMA((2, CAP)),
            pltpu.SemaphoreType.DMA((2, CAP)),
            pltpu.SemaphoreType.DMA((2,)),
            pltpu.SemaphoreType.DMA((2,)),
            pltpu.SemaphoreType.DMA((2, 2)),
            pltpu.SemaphoreType.DMA((2, 2)),
            pltpu.SemaphoreType.REGULAR((2,)),
        ],
        compiler_params=pltpu.CompilerParams(
            collective_id=0, has_side_effects=True, vmem_limit_bytes=40 * 1024 * 1024
        ),
        name="resample_and_step",
    )(*(pltpu.with_memory_space_constraint(x, pltpu.HBM) for x in (ancestors, ensemble, perturbation, levels, observed)))
    return pl.pallas_call(
        finish,
        out_shape=jax.ShapeDtypeStruct((pd, nf, ny, nx), f32),
        in_specs=[vmem] * len(handed),
        out_specs=hbm,
        scratch_shapes=[
            pltpu.VMEM((UNIT, nf, tiles, ny, LANES), f32),
            pltpu.VMEM(state, f32),
            pltpu.VMEM(state, f32),
            pltpu.VMEM((nf, CAP, PITCH, LANES), f32),
            pltpu.VMEM((nf, CAP, PITCH, LANES), f32),
            pltpu.VMEM((nf, CAP, ny, LANES), f32),
            pltpu.SemaphoreType.DMA((3, tiles)),
        ],
        compiler_params=pltpu.CompilerParams(vmem_limit_bytes=24 * 1024 * 1024),
        name="finish",
    )(*between)


def solution(mesh):
    return jax.shard_map(
        local,
        mesh=mesh,
        in_specs=(
            P("dom", None, None, "space"),
            P(),
            P("dom", None, "space"),
            P(None, "space"),
            P(None, "space"),
        ),
        out_specs=P("dom", None, None, "space"),
        check_vma=False,
    )
```

```python
import functools

import jax
import jax.numpy as jnp
from jax import lax
from jax.experimental import pallas as pl
from jax.experimental.pallas import tpu as pltpu
from jax.sharding import PartitionSpec as P

MESH = pl.DeviceIdType.MESH
STEPS = 3
CAP = 2
EDGE = 2 * STEPS
LANES = 128
TOP = 8
PITCH = 32
UNIT = 4
HALF = 8
ROW = 8
PAIRS = 7
RUN = 8
LAGS = 4
AHEAD = (6, 3)
NEED = (EDGE, EDGE - 1, EDGE, EDGE - 3)
SHELF = (0, 12, 6, 17)
SLOT_LANES = 20
TRIPLE = 3
E_, N_, H_, C_ = range(4)


def lane_of(shape):
    return lax.broadcasted_iota(jnp.int32, shape, len(shape) - 1)


def east(cells, joined):
    turned = pltpu.roll(cells, LANES - 1, 2)
    if not joined:
        return turned
    following = jnp.concatenate([turned[1:], turned[:1]], axis=0)
    return jnp.where(lane_of(cells.shape) == LANES - 1, following, turned)


def west(cells, joined):
    turned = pltpu.roll(cells, 1, 2)
    if not joined:
        return turned
    preceding = jnp.concatenate([turned[-1:], turned[:-1]], axis=0)
    return jnp.where(lane_of(cells.shape) == 0, preceding, turned)


def flow(read, wet, turn, joined):
    e, n, h = read(E_, 0), read(N_, 0), read(H_, 0)
    e_new = wet * (
        (5.5 * e + turn * n)
        + (read(E_, 1) + read(E_, -1))
        + (east(e - h, joined) + west(e + h, joined))
    )
    n_new = wet * (
        (5.5 * n - turn * e)
        + (east(n, joined) + west(n, joined))
        + ((read(N_, 1) - read(H_, 1)) + (read(N_, -1) + read(H_, -1)))
    )
    return e_new, n_new


def level(read, read_new, depth, pull, last, joined):
    e, n = read_new(E_, 0), read_new(N_, 0)
    spread = (east(e, joined) - west(e, joined)) + (read_new(N_, 1) - read_new(N_, -1))
    h_new = ((0.18 if last else 0.9) * read(H_, 0) + pull) - depth * spread
    c = read(C_, 0)
    c_east, c_west = east(c, joined), west(c, joined)
    c_north, c_south = read(C_, 1), read(C_, -1)
    c_new = (
        (6.0 * c + ((c_east + c_west) + (c_north + c_south)))
        - e * (c_east - c_west)
        - n * (c_north - c_south)
    )
    if last:
        c_new = 0.001 * c_new
    return h_new, c_new


def level_of(levels, observed):
    return (
        jnp.where(levels > 0, 0.1, 0.0).astype(jnp.float32),
        1.25 * levels,
        0.25 * levels,
        0.5 * observed,
        0.1 * observed,
    )


def turn_of(ny, y0):
    y = lax.broadcasted_iota(jnp.int32, (1, HALF, LANES), 1).astype(jnp.float32) + float(y0)
    return 2.0 * (0.2 + 0.6 * y / ny)


def all_steps(first, s1, s2, ground, keep, joined, ny, parts):
    wet, depth, pull = ground
    count = len(parts)
    for step in range(STEPS):
        last = step == STEPS - 1
        old, new = (None, s1) if step == 0 else (s1, s2) if step == 1 else (s2, s1)

        def reader(ref, i, y0):
            return lambda field, up: parts[i](ref, field, pl.ds(TOP + y0 + up, HALF))[...]

        def read(i, y0):
            return (lambda field, up: first(i, field, y0, up)) if step == 0 else reader(old, i, y0)

        for i in range(count):
            for y0 in range(0, ny, HALF):
                e, n = flow(read(i, y0), wet(y0), turn_of(ny, y0), joined)
                now = pl.ds(TOP + y0, HALF)
                parts[i](new, E_, now)[...] = e
                parts[i](new, N_, now)[...] = n
                if last:
                    keep(i, E_, y0, e)
                    keep(i, N_, y0, n)
        for i in range(count):
            for y0 in range(0, ny, HALF):
                h, c = level(read(i, y0), reader(new, i, y0), depth(last, y0), pull(last, y0), last, joined)
                now = pl.ds(TOP + y0, HALF)
                if last:
                    keep(i, H_, y0, h)
                    keep(i, C_, y0, c)
                else:
                    parts[i](new, H_, now)[...] = h
                    parts[i](new, C_, now)[...] = c


def slot_parts():
    return [lambda ref, field, now, s=s: ref.at[s, field, :, now] for s in range(UNIT)]


def row_ground(gw, gd, go):
    return (
        lambda y0: gw[:, pl.ds(y0, HALF)],
        lambda last, y0: gd[int(last), :, pl.ds(y0, HALF)],
        lambda last, y0: go[int(last), :, pl.ds(y0, HALF)],
    )


def strip_ground(gs):
    return (
        lambda y0: gs[0, pl.ds(y0, HALF)][None],
        lambda last, y0: gs[2 if last else 1, pl.ds(y0, HALF)][None],
        lambda last, y0: gs[4 if last else 3, pl.ds(y0, HALF)][None],
    )


def step_strips(b0, b1, b2, b3, gs, groups, ny):
    parts = [lambda ref, field, now, g=g: ref.at[field, g, now] for g in groups]

    def keep(i, field, y0, value):
        b3[field, groups[i], pl.ds(y0, HALF)] = value

    all_steps(
        lambda i, field, y0, up: b0[field, groups[i], pl.ds(TOP + y0 + up, HALF)],
        b1, b2, strip_ground(gs), keep, False, ny, parts,
    )


def put_strips(b3, p, slots, out):
    done = b3[:, p]
    lane = lane_of(done.shape)
    final = out.shape[2] - 1
    for s, j in enumerate(slots):
        base = 64 * s
        at_left = pltpu.roll(done, LANES - EDGE - base, 2)
        at_right = pltpu.roll(done, (LANES - EDGE - (base + 32 + EDGE)) % LANES, 2)
        pltpu.store(out.at[j, :, 0], at_left, mask=lane < EDGE)
        pltpu.store(out.at[j, :, final], at_right, mask=lane >= LANES - EDGE)


def late_soon(k, me, doms):
    inner_end = (lax.rem(k, ROW) == ROW - 1) & (k < doms - 1)
    inner_start = (lax.rem(k, ROW) == 0) & (k > 0)
    return (lax.rem(me, RUN) == 0) & jnp.logical_not(inner_end | inner_start)


def clear_rows(ref, ny):
    @pl.loop(0, ref.shape[0])
    def _(i):
        blank = jnp.zeros(ref.shape[1:-2] + (8, LANES), jnp.float32)
        ref[i, ..., TOP - 8 : TOP, :] = blank
        ref[i, ..., TOP + ny : TOP + ny + 8, :] = blank


def kernel(
    anc_in, ens, pert, lev, obs, out, late_made, late0, late_strips, gs, gw, gd, go,
    anc, ends_of, inner, ext, h0, pv, lv, ov, s1, s2, b0, b1, b2, b3, out1, in1, edge_out, edge_in,
    in_sem, dom_out_sem, dom_in_sem, msg_out_sem, msg_in_sem, edge_out_sem, edge_in_sem, entered,
):
    pd = ens.shape[0]
    ny = ens.shape[2]
    tiles = ens.shape[3] // LANES
    doms, spaces = lax.axis_size("dom"), lax.axis_size("space")
    k, me = lax.axis_index("dom"), lax.axis_index("space")
    prev_space, next_space = lax.rem(me + spaces - 1, spaces), lax.rem(me + 1, spaces)
    early = pd - 2 * CAP
    rows = slice(TOP, TOP + ny)

    barrier = pltpu.get_barrier_semaphore()

    def signal(semaphore, dom, space):
        pl.semaphore_signal(semaphore, inc=1, device_id=(dom, space), device_id_type=MESH)

    def signal_side(semaphore, rightward):
        space = next_space if rightward else prev_space
        signal(semaphore, k, space)

        @pl.when(k > 0)
        def _():
            signal(semaphore, k - 1, space)

        @pl.when(k < doms - 1)
        def _():
            signal(semaphore, k + 1, space)

    place = lax.rem(me, RUN)
    late_side = (place == 0, place < LAGS)
    ahead_side = ((place > 0) & (place <= LAGS), place == RUN - 1)
    dom_peers = jnp.where(k > 0, 1, 0) + jnp.where(k < doms - 1, 1, 0)
    side_peers = 1 + dom_peers

    @pl.when(k > 0)
    def _():
        signal(barrier, k - 1, me)

    @pl.when(k < doms - 1)
    def _():
        signal(barrier, k + 1, me)

    for side in range(2):
        pl.when(jnp.logical_not(ahead_side[side]))(functools.partial(signal_side, barrier, side))

    def tile(q):
        return pl.ds(q * LANES, LANES)

    needed_first, needed_next = [pltpu.make_async_copy(anc_in, anc, in_sem.at[4, 0])], []
    for q in (0, tiles - 1, *range(1, tiles - 1)):
        at_end = q in (0, tiles - 1)
        loads = needed_first if at_end else needed_next
        here = ends_of.at[:, :, int(q > 0), rows] if at_end else inner.at[:, :, q - 1, rows]
        loads.append(pltpu.make_async_copy(ens.at[:, :, :, tile(q)], here, in_sem.at[3, q]))
        loads.append(pltpu.make_async_copy(pert.at[:, :, tile(q)], pv.at[:, q], in_sem.at[2, q]))
        loads.append(pltpu.make_async_copy(lev.at[:, tile(q)], lv.at[q], in_sem.at[0, q]))
        loads.append(pltpu.make_async_copy(obs.at[:, tile(q)], ov.at[q], in_sem.at[1, q]))
    for copy in needed_first + needed_next:
        copy.start()

    for ref in (ends_of, inner, h0, late0, s1, s2, b0, b1, b2, late_strips):
        clear_rows(ref, ny)

    def dom_copy(up, t):
        first, lands, to = (pd - CAP, 0, k + 1) if up else (0, CAP, k - 1)
        return pltpu.make_async_remote_copy(
            src_ref=ens.at[first + t],
            dst_ref=ext.at[lands + t],
            send_sem=dom_out_sem.at[int(up), t],
            recv_sem=dom_in_sem.at[int(up), t],
            device_id=(to, me),
            device_id_type=MESH,
        )

    def send_particles(up, on):
        @pl.when(on)
        def _():
            for t in range(CAP):
                dom_copy(up, t).start()

    pl.semaphore_wait(
        barrier, dom_peers + sum(jnp.where(late_side[side], 0, side_peers) for side in range(2))
    )
    for side in (1, 0):
        pl.when(ahead_side[side])(functools.partial(signal_side, entered.at[1 - side], side))
    odd = lax.rem(k, 2) == 1
    row_end, row_start = lax.rem(k, ROW) == ROW - 1, lax.rem(k, ROW) == 0
    far_up = row_end & (k < doms - 1) & (place < RUN - 1)
    far_down = row_start & (k > 0) & (place < RUN - 1)
    send_particles(True, far_up)
    send_particles(False, far_down)

    for copy in needed_first:
        copy.wait()

    def from_own(j):
        return jnp.clip(anc[k * pd + j] - k * pd, 0, pd - 1)

    def from_ext(j, low):
        parent = anc[k * pd + j]
        if low:
            return jnp.where(k == 0, j, jnp.clip(parent - (k * pd - CAP), 0, CAP - 1))
        return jnp.where(
            k == doms - 1, j - (pd - 2 * CAP), jnp.clip(parent - (k + 1) * pd, 0, CAP - 1) + CAP
        )

    def column(i, j, side):
        h = 5.0 * (ends_of[i, H_, side, rows] + pv[j, side * (tiles - 1)])
        return jnp.concatenate(
            [ends_of[i, E_ : N_ + 1, side, rows], h[None], ends_of[i, C_:, side, rows]], axis=0
        )

    flat = lane_of((ny, LANES))

    def message(rightward):
        return pltpu.make_async_remote_copy(
            src_ref=out1.at[int(rightward)],
            dst_ref=in1.at[int(rightward)],
            send_sem=msg_out_sem.at[int(rightward)],
            recv_sem=msg_in_sem.at[int(rightward)],
            device_id=(k, next_space if rightward else prev_space),
            device_id_type=MESH,
        )

    edge_to = (jnp.where(k < doms - 1, k + 1, k), jnp.where(k > 0, k - 1, k))
    edge_side = (jnp.where(k < doms - 1, 0, 1), jnp.where(k > 0, 1, 0))

    def edge_particle(up, t):
        if up:
            return jnp.where(k < doms - 1, pd - CAP + t, from_own(pd - CAP + t))
        return jnp.where(k > 0, t, from_own(t))

    def edge_message(up, rightward):
        at = 0 if up else 1
        return pltpu.make_async_remote_copy(
            src_ref=edge_out.at[at, int(rightward)],
            dst_ref=edge_in.at[edge_side[at], int(rightward)],
            send_sem=edge_out_sem.at[at, int(rightward)],
            recv_sem=edge_in_sem.at[edge_side[at], int(rightward)],
            device_id=(edge_to[at], next_space if rightward else prev_space),
            device_id_type=MESH,
        )

    def edge_arrival(side, rightward):
        return pltpu.make_async_remote_copy(
            src_ref=edge_out.at[side, int(rightward)],
            dst_ref=edge_in.at[side, int(rightward)],
            send_sem=edge_out_sem.at[side, int(rightward)],
            recv_sem=edge_in_sem.at[side, int(rightward)],
            device_id=(k, next_space if rightward else prev_space),
            device_id_type=MESH,
        )

    def shelve(columns, side, at, tile_so_far):
        for f in range(4):
            first = LANES - NEED[f] if side else 0
            to = at + SHELF[f]
            chosen = (flat >= to) & (flat < to + NEED[f])
            tile_so_far = jnp.where(chosen, pltpu.roll(columns[f], (to - first) % LANES, 1), tile_so_far)
        return tile_so_far

    shelves = -(-PAIRS // TRIPLE)

    @pl.loop(0, early // (2 * PAIRS))
    def _(m):
        for r in range(shelves):
            packed = [jnp.zeros((ny, LANES), jnp.float32)] * 2
            for p in range(TRIPLE * r, min(PAIRS, TRIPLE * r + TRIPLE)):
                for s in range(2):
                    j = CAP + 2 * (PAIRS * m + p) + s
                    i = from_own(j)
                    for side in range(2):
                        at = 64 * s + SLOT_LANES * (p - TRIPLE * r)
                        packed[side] = shelve(column(i, j, side), side, at, packed[side])
            for side in range(2):
                out1[side, shelves * m + r] = packed[side]

    extra = shelves * (early // (2 * PAIRS))
    late = [pd - 2, pd - 1, 0, 1]
    for rightward in range(2):
        q, end = (tiles - 1, EDGE) if rightward else (0, 0)
        got = jnp.zeros((ny, LANES), jnp.float32)
        parts = [(lv[q].astype(jnp.float32), at) for at in (0, 64)] + [(ov[q], at) for at in (8, 72)]
        parts += [(5.0 * pv[j, q], 64 * (t % 2) + 16 + 8 * (t // 2)) for t, j in enumerate(late)]
        for part, at in parts:
            got = jnp.where((flat >= at) & (flat < at + EDGE), pltpu.roll(part, at + end, 1), got)
        out1[rightward, extra] = got
        for up in (True, False):
            got = jnp.zeros((ny, LANES), jnp.float32)
            for t in range(CAP):
                i = edge_particle(up, t)
                columns = [ends_of[i, f, rightward, rows] for f in range(4)]
                columns[H_] = 5.0 * columns[H_]
                got = shelve(columns, rightward, 64 * t, got)
            edge_out[0 if up else 1, rightward] = got

    def send_side(rightward):
        message(rightward).start()
        for up in (False, True):
            edge_message(up, rightward).start()

    for side in (1, 0):
        pl.when(jnp.logical_not(late_side[side]))(functools.partial(send_side, side))
    send_particles(True, odd & (k < doms - 1) & jnp.logical_not(far_up))
    send_particles(False, jnp.logical_not(odd) & (k > 0) & jnp.logical_not(far_down))
    send_particles(True, jnp.logical_not(odd))
    send_particles(False, odd)

    def send_late(side):
        pl.semaphore_wait(entered.at[side], side_peers)
        send_side(side)

    for copy in needed_next:
        copy.wait()

    levels = lv[...].astype(jnp.float32)
    gw[...], gd[0], gd[1], go[0], go[1] = level_of(levels, ov[...])

    def whole_rows(i, f, at):
        return jnp.concatenate([ends_of[i, f, :1, at], inner[i, f, :, at], ends_of[i, f, 1:, at]], axis=0)

    @pl.loop(0, early // UNIT)
    def _(u):
        for s in range(UNIT):
            j = CAP + u * UNIT + s
            h0[j, :, rows] = 5.0 * (whole_rows(from_own(j), H_, rows) + pv[j])

    @pl.loop(0, early // UNIT)
    def _(u):
        for side in range(2):
            pl.when(late_side[side] & (u == AHEAD[side]))(functools.partial(send_late, side))
        slots = [CAP + u * UNIT + s for s in range(UNIT)]
        where = [from_own(j) for j in slots]

        def first(i, field, y0, up):
            at = pl.ds(TOP + y0 + up, HALF)
            return h0[slots[i], :, at] if field == H_ else whole_rows(where[i], field, at)

        def keep(i, field, y0, value):
            out[slots[i], field, :, pl.ds(y0, HALF)] = value

        all_steps(first, s1, s2, row_ground(gw, gd, go), keep, True, ny, slot_parts())

    late_from = [from_ext(j, j < CAP) for j in late]
    soon = late_soon(k, me, doms)

    def take_late():
        @pl.when(k > 0)
        def _():
            for t in range(CAP):
                dom_copy(True, t).wait_recv()

        @pl.when(k < doms - 1)
        def _():
            for t in range(CAP):
                dom_copy(False, t).wait_recv()

        def own_particle(lands, j):
            for f in range(4):
                state = whole_rows(from_own(j), f, rows)
                for q in range(tiles):
                    ext[lands, f, :, tile(q)] = state[q]

        @pl.when(k == 0)
        def _():
            for s in range(CAP):
                own_particle(s, s)

        @pl.when(k == doms - 1)
        def _():
            for s in range(CAP, 2 * CAP):
                own_particle(s, pd - 2 * CAP + s)

        for t, j in enumerate(late):
            for f in range(4):
                state = jnp.stack([ext[late_from[t], f, :, tile(q)] for q in range(tiles)])
                late0[t, f, :, rows] = 5.0 * (state + pv[j]) if f == H_ else state

    @pl.when(soon)
    def _():
        take_late()

        def keep(i, field, y0, value):
            late_made[i, field, :, pl.ds(y0, HALF)] = value

        all_steps(
            lambda i, field, y0, up: late0[i, field, :, pl.ds(TOP + y0 + up, HALF)],
            s1, s2, row_ground(gw, gd, go), keep, True, ny, slot_parts(),
        )

    for rightward in (False, True):
        message(rightward).wait_recv()

    def ends(first, final, s, tile_so_far):
        base = 64 * s
        lane = lane_of(first.shape)
        chosen = (lane >= base + EDGE) & (lane < base + 3 * EDGE)
        tile_so_far = jnp.where(chosen, pltpu.roll(first, base + EDGE, 2), tile_so_far)
        chosen = (lane >= base + 32) & (lane < base + 32 + 2 * EDGE)
        return jnp.where(chosen, pltpu.roll(final, (base + 32 + 2 * EDGE) % LANES, 2), tile_so_far)

    def beyond(from_left, from_right, at, width=EDGE):
        half = lax.rem(lane_of(from_left.shape), 64)
        chosen = (half >= EDGE - width) & (half < EDGE)
        got = jnp.where(chosen, pltpu.roll(from_left, (LANES + EDGE - width - at) % LANES, 1), 0.0)
        chosen = (half >= 44) & (half < 44 + width)
        return jnp.where(chosen, pltpu.roll(from_right, (LANES + 44 - at) % LANES, 1), got)

    def unshelved(from_left, from_right, at):
        return [beyond(from_left, from_right, at + SHELF[f], NEED[f]) for f in range(4)]

    fields = []
    for i, field in enumerate((levels, ov[...])):
        got = beyond(in1[1, extra], in1[0, extra], 8 * i)[None]
        for s in range(2):
            got = ends(field[:1], field[tiles - 1 :], s, got)
        fields.append(got[0])
    gs[0], gs[1], gs[2], gs[3], gs[4] = level_of(*fields)

    @pl.loop(0, early // (2 * PAIRS))
    def _(m):
        slots = [[CAP + 2 * (PAIRS * m + p) + s for s in range(2)] for p in range(PAIRS)]
        for p in range(PAIRS):
            r = shelves * m + p // TRIPLE
            got = jnp.stack(unshelved(in1[1, r], in1[0, r], SLOT_LANES * (p % TRIPLE)))
            for s, j in enumerate(slots[p]):
                i = from_own(j)
                got = ends(column(i, j, 0), column(i, j, 1), s, got)
            b0[:, p, rows] = got
        step_strips(b0, b1, b2, b3, gs, [slice(0, 4), slice(4, PAIRS)], ny)
        for p in range(PAIRS):
            put_strips(b3, p, slots[p], out)

    pl.when(jnp.logical_not(soon))(take_late)

    for side in range(2):
        for rightward in (False, True):
            edge_arrival(side, rightward).wait_recv()
    for p in range(2):
        side = 1 - p
        where = [late_from[2 * p + s] - CAP * side for s in range(2)]
        ways = []
        for w in range(2):
            came = edge_in[side, w]
            turned = pltpu.roll(came, 64, 1)
            ways.append(jnp.where(flat < 64, *(jnp.where(where[s] == s, came, turned) for s in range(2))))
        got = unshelved(ways[1], ways[0], 0)
        got[H_] = got[H_] + beyond(in1[1, extra], in1[0, extra], 16 + 8 * p)
        got = jnp.stack(got)
        for s in range(2):
            got = ends(late0[2 * p + s, :, 0, rows], late0[2 * p + s, :, tiles - 1, rows], s, got)
        late_strips[:, p, rows] = got

    for rightward in (False, True):
        message(rightward).wait_send()
        for up in (False, True):
            edge_message(up, rightward).wait_send()

    @pl.when(k < doms - 1)
    def _():
        for t in range(CAP):
            dom_copy(True, t).wait_send()

    @pl.when(k > 0)
    def _():
        for t in range(CAP):
            dom_copy(False, t).wait_send()


def finish(made, late_made, late0, late_strips, gs, gw, gd, go, out, late_out, s1, s2, b1, b2, b3, sem):
    pd, nf, tiles, ny, _ = made.shape

    def tile(q):
        return pl.ds(q * LANES, LANES)

    copies = [
        pltpu.make_async_copy(made.at[CAP : pd - CAP, :, q], out.at[CAP : pd - CAP, :, :, tile(q)], sem.at[0, q])
        for q in range(tiles)
    ]
    for copy in copies:
        copy.start()
    for ref in (s1, s2, b1, b2):
        clear_rows(ref, ny)

    soon = late_soon(lax.axis_index("dom"), lax.axis_index("space"), lax.axis_size("dom"))

    @pl.when(soon)
    def _():
        late_out[...] = late_made[...]

    @pl.when(jnp.logical_not(soon))
    def _():
        def keep(i, field, y0, value):
            late_out[i, field, :, pl.ds(y0, HALF)] = value

        all_steps(
            lambda i, field, y0, up: late0[i, field, :, pl.ds(TOP + y0 + up, HALF)],
            s1, s2, row_ground(gw, gd, go), keep, True, ny, slot_parts(),
        )

    step_strips(late_strips, b1, b2, b3, gs, [slice(0, CAP)], ny)
    for p in range(2):
        put_strips(b3, p, [2 * p, 2 * p + 1], late_out)
    for p, first in enumerate((pd - CAP, 0)):
        for q in range(tiles):
            copy = pltpu.make_async_copy(
                late_out.at[CAP * p : CAP * p + CAP, :, q], out.at[first : first + CAP, :, :, tile(q)], sem.at[1 + p, q]
            )
            copy.start()
            copies.append(copy)
    for copy in copies:
        copy.wait()


def local(ensemble, ancestors, perturbation, levels, observed):
    pd, nf, ny, nx = ensemble.shape
    tiles = nx // LANES
    f32 = jnp.float32
    hbm = pl.BlockSpec(memory_space=pl.ANY)
    vmem = pl.BlockSpec(memory_space=pltpu.VMEM)
    state = (UNIT, nf, tiles, PITCH, LANES)
    handed = [
        pltpu.VMEM((pd, nf, tiles, ny, LANES), f32),
        pltpu.VMEM((UNIT, nf, tiles, ny, LANES), f32),
        pltpu.VMEM(state, f32),
        pltpu.VMEM((nf, CAP, PITCH, LANES), f32),
        pltpu.VMEM((5, ny, LANES), f32),
        pltpu.VMEM((tiles, ny, LANES), f32),
        pltpu.VMEM((2, tiles, ny, LANES), f32),
        pltpu.VMEM((2, tiles, ny, LANES), f32),
    ]
    between = pl.pallas_call(
        kernel,
        out_shape=handed,
        in_specs=[hbm] * 5,
        out_specs=[vmem] * len(handed),
        scratch_shapes=[
            pltpu.SMEM(ancestors.shape, jnp.int32),
            pltpu.VMEM((pd, nf, 2, PITCH, LANES), f32),
            pltpu.VMEM((pd, nf, tiles - 2, PITCH, LANES), f32),
            pltpu.VMEM((2 * CAP, nf, ny, nx), f32),
            pltpu.VMEM((pd, tiles, PITCH, LANES), f32),
            pltpu.VMEM((pd, tiles, ny, LANES), f32),
            pltpu.VMEM((tiles, ny, LANES), jnp.int32),
            pltpu.VMEM((tiles, ny, LANES), f32),
            pltpu.VMEM(state, f32),
            pltpu.VMEM(state, f32),
            pltpu.VMEM((nf, PAIRS, PITCH, LANES), f32),
            pltpu.VMEM((nf, PAIRS, PITCH, LANES), f32),
            pltpu.VMEM((nf, PAIRS, PITCH, LANES), f32),
            pltpu.VMEM((nf, PAIRS, ny, LANES), f32),
            pltpu.VMEM((2, 7, ny, LANES), f32),
            pltpu.VMEM((2, 7, ny, LANES), f32),
            pltpu.VMEM((2, 2, ny, LANES), f32),
            pltpu.VMEM((2, 2, ny, LANES), f32),
            pltpu.SemaphoreType.DMA((5, tiles)),
            pltpu.SemaphoreType.DMA((2, CAP)),
            pltpu.SemaphoreType.DMA((2, CAP)),
            pltpu.SemaphoreType.DMA((2,)),
            pltpu.SemaphoreType.DMA((2,)),
            pltpu.SemaphoreType.DMA((2, 2)),
            pltpu.SemaphoreType.DMA((2, 2)),
            pltpu.SemaphoreType.REGULAR((2,)),
        ],
        compiler_params=pltpu.CompilerParams(
            collective_id=0, has_side_effects=True, vmem_limit_bytes=40 * 1024 * 1024
        ),
        name="resample_and_step",
    )(*(pltpu.with_memory_space_constraint(x, pltpu.HBM) for x in (ancestors, ensemble, perturbation, levels, observed)))
    return pl.pallas_call(
        finish,
        out_shape=jax.ShapeDtypeStruct((pd, nf, ny, nx), f32),
        in_specs=[vmem] * len(handed),
        out_specs=hbm,
        scratch_shapes=[
            pltpu.VMEM((UNIT, nf, tiles, ny, LANES), f32),
            pltpu.VMEM(state, f32),
            pltpu.VMEM(state, f32),
            pltpu.VMEM((nf, CAP, PITCH, LANES), f32),
            pltpu.VMEM((nf, CAP, PITCH, LANES), f32),
            pltpu.VMEM((nf, CAP, ny, LANES), f32),
            pltpu.SemaphoreType.DMA((3, tiles)),
        ],
        compiler_params=pltpu.CompilerParams(vmem_limit_bytes=24 * 1024 * 1024),
        name="finish",
    )(*between)


def solution(mesh):
    return jax.shard_map(
        local,
        mesh=mesh,
        in_specs=(
            P("dom", None, None, "space"),
            P(),
            P("dom", None, "space"),
            P(None, "space"),
            P(None, "space"),
        ),
        out_specs=P("dom", None, None, "space"),
        check_vma=False,
    )
```

```python
import functools

import jax
import jax.numpy as jnp
from jax import lax
from jax.experimental import pallas as pl
from jax.experimental.pallas import tpu as pltpu
from jax.sharding import PartitionSpec as P

MESH = pl.DeviceIdType.MESH
STEPS = 3
CAP = 2
EDGE = 2 * STEPS
LANES = 128
TOP = 8
PITCH = 32
UNIT = 4
HALF = 8
ROW = 8
PAIRS = 7
RUN = 8
LAGS = 4
AHEAD = (5, 2)
NEED = (EDGE, EDGE - 1, EDGE, EDGE - 3)
SHELF = (0, 12, 6, 17)
SLOT_LANES = 20
TRIPLE = 3
E_, N_, H_, C_ = range(4)


def lane_of(shape):
    return lax.broadcasted_iota(jnp.int32, shape, len(shape) - 1)


def east(cells, joined):
    turned = pltpu.roll(cells, LANES - 1, 2)
    if not joined:
        return turned
    following = jnp.concatenate([turned[1:], turned[:1]], axis=0)
    return jnp.where(lane_of(cells.shape) == LANES - 1, following, turned)


def west(cells, joined):
    turned = pltpu.roll(cells, 1, 2)
    if not joined:
        return turned
    preceding = jnp.concatenate([turned[-1:], turned[:-1]], axis=0)
    return jnp.where(lane_of(cells.shape) == 0, preceding, turned)


def flow(read, wet, turn, joined):
    e, n, h = read(E_, 0), read(N_, 0), read(H_, 0)
    e_new = wet * (
        (5.5 * e + turn * n)
        + (read(E_, 1) + read(E_, -1))
        + (east(e - h, joined) + west(e + h, joined))
    )
    n_new = wet * (
        (5.5 * n - turn * e)
        + (east(n, joined) + west(n, joined))
        + ((read(N_, 1) - read(H_, 1)) + (read(N_, -1) + read(H_, -1)))
    )
    return e_new, n_new


def level(read, read_new, depth, pull, last, joined):
    e, n = read_new(E_, 0), read_new(N_, 0)
    spread = (east(e, joined) - west(e, joined)) + (read_new(N_, 1) - read_new(N_, -1))
    h_new = ((0.18 if last else 0.9) * read(H_, 0) + pull) - depth * spread
    c = read(C_, 0)
    c_east, c_west = east(c, joined), west(c, joined)
    c_north, c_south = read(C_, 1), read(C_, -1)
    c_new = (
        (6.0 * c + ((c_east + c_west) + (c_north + c_south)))
        - e * (c_east - c_west)
        - n * (c_north - c_south)
    )
    if last:
        c_new = 0.001 * c_new
    return h_new, c_new


def level_of(levels, observed):
    return (
        jnp.where(levels > 0, 0.1, 0.0).astype(jnp.float32),
        1.25 * levels,
        0.25 * levels,
        0.5 * observed,
        0.1 * observed,
    )


def turn_of(ny, y0):
    y = lax.broadcasted_iota(jnp.int32, (1, HALF, LANES), 1).astype(jnp.float32) + float(y0)
    return 2.0 * (0.2 + 0.6 * y / ny)


def all_steps(first, s1, s2, ground, keep, joined, ny, parts):
    wet, depth, pull = ground
    count = len(parts)
    for step in range(STEPS):
        last = step == STEPS - 1
        old, new = (None, s1) if step == 0 else (s1, s2) if step == 1 else (s2, s1)

        def reader(ref, i, y0):
            return lambda field, up: parts[i](ref, field, pl.ds(TOP + y0 + up, HALF))[...]

        def read(i, y0):
            return (lambda field, up: first(i, field, y0, up)) if step == 0 else reader(old, i, y0)

        for i in range(count):
            for y0 in range(0, ny, HALF):
                e, n = flow(read(i, y0), wet(y0), turn_of(ny, y0), joined)
                now = pl.ds(TOP + y0, HALF)
                parts[i](new, E_, now)[...] = e
                parts[i](new, N_, now)[...] = n
                if last:
                    keep(i, E_, y0, e)
                    keep(i, N_, y0, n)
        for i in range(count):
            for y0 in range(0, ny, HALF):
                h, c = level(read(i, y0), reader(new, i, y0), depth(last, y0), pull(last, y0), last, joined)
                now = pl.ds(TOP + y0, HALF)
                if last:
                    keep(i, H_, y0, h)
                    keep(i, C_, y0, c)
                else:
                    parts[i](new, H_, now)[...] = h
                    parts[i](new, C_, now)[...] = c


def slot_parts():
    return [lambda ref, field, now, s=s: ref.at[s, field, :, now] for s in range(UNIT)]


def row_ground(gw, gd, go):
    return (
        lambda y0: gw[:, pl.ds(y0, HALF)],
        lambda last, y0: gd[int(last), :, pl.ds(y0, HALF)],
        lambda last, y0: go[int(last), :, pl.ds(y0, HALF)],
    )


def strip_ground(gs):
    return (
        lambda y0: gs[0, pl.ds(y0, HALF)][None],
        lambda last, y0: gs[2 if last else 1, pl.ds(y0, HALF)][None],
        lambda last, y0: gs[4 if last else 3, pl.ds(y0, HALF)][None],
    )


def step_strips(b0, b1, b2, b3, gs, groups, ny):
    parts = [lambda ref, field, now, g=g: ref.at[field, g, now] for g in groups]

    def keep(i, field, y0, value):
        b3[field, groups[i], pl.ds(y0, HALF)] = value

    all_steps(
        lambda i, field, y0, up: b0[field, groups[i], pl.ds(TOP + y0 + up, HALF)],
        b1, b2, strip_ground(gs), keep, False, ny, parts,
    )


def put_strips(b3, p, slots, out):
    done = b3[:, p]
    lane = lane_of(done.shape)
    final = out.shape[2] - 1
    for s, j in enumerate(slots):
        base = 64 * s
        at_left = pltpu.roll(done, LANES - EDGE - base, 2)
        at_right = pltpu.roll(done, (LANES - EDGE - (base + 32 + EDGE)) % LANES, 2)
        pltpu.store(out.at[j, :, 0], at_left, mask=lane < EDGE)
        pltpu.store(out.at[j, :, final], at_right, mask=lane >= LANES - EDGE)


def late_soon(k, me, doms):
    inner_end = (lax.rem(k, ROW) == ROW - 1) & (k < doms - 1)
    inner_start = (lax.rem(k, ROW) == 0) & (k > 0)
    return (lax.rem(me, RUN) == 0) & jnp.logical_not(inner_end | inner_start)


def clear_rows(ref, ny):
    @pl.loop(0, ref.shape[0])
    def _(i):
        blank = jnp.zeros(ref.shape[1:-2] + (8, LANES), jnp.float32)
        ref[i, ..., TOP - 8 : TOP, :] = blank
        ref[i, ..., TOP + ny : TOP + ny + 8, :] = blank


def kernel(
    anc_in, ens, pert, lev, obs, out, late_made, late0, late_strips, gs, gw, gd, go,
    anc, ends_of, inner, ext, h0, pv, lv, ov, s1, s2, b0, b1, b2, b3, out1, in1, edge_out, edge_in,
    in_sem, dom_out_sem, dom_in_sem, msg_out_sem, msg_in_sem, edge_out_sem, edge_in_sem, entered,
):
    pd = ens.shape[0]
    ny = ens.shape[2]
    tiles = ens.shape[3] // LANES
    doms, spaces = lax.axis_size("dom"), lax.axis_size("space")
    k, me = lax.axis_index("dom"), lax.axis_index("space")
    prev_space, next_space = lax.rem(me + spaces - 1, spaces), lax.rem(me + 1, spaces)
    early = pd - 2 * CAP
    rows = slice(TOP, TOP + ny)

    barrier = pltpu.get_barrier_semaphore()

    def signal(semaphore, dom, space):
        pl.semaphore_signal(semaphore, inc=1, device_id=(dom, space), device_id_type=MESH)

    def signal_side(semaphore, rightward):
        space = next_space if rightward else prev_space
        signal(semaphore, k, space)

        @pl.when(k > 0)
        def _():
            signal(semaphore, k - 1, space)

        @pl.when(k < doms - 1)
        def _():
            signal(semaphore, k + 1, space)

    place = lax.rem(me, RUN)
    late_side = (place == 0, place < LAGS)
    ahead_side = ((place > 0) & (place <= LAGS), place == RUN - 1)
    dom_peers = jnp.where(k > 0, 1, 0) + jnp.where(k < doms - 1, 1, 0)
    side_peers = 1 + dom_peers

    @pl.when(k > 0)
    def _():
        signal(barrier, k - 1, me)

    @pl.when(k < doms - 1)
    def _():
        signal(barrier, k + 1, me)

    for side in range(2):
        pl.when(jnp.logical_not(ahead_side[side]))(functools.partial(signal_side, barrier, side))

    def tile(q):
        return pl.ds(q * LANES, LANES)

    needed_first, needed_next = [pltpu.make_async_copy(anc_in, anc, in_sem.at[4, 0])], []
    for q in (0, tiles - 1, *range(1, tiles - 1)):
        at_end = q in (0, tiles - 1)
        loads = needed_first if at_end else needed_next
        here = ends_of.at[:, :, int(q > 0), rows] if at_end else inner.at[:, :, q - 1, rows]
        loads.append(pltpu.make_async_copy(ens.at[:, :, :, tile(q)], here, in_sem.at[3, q]))
        loads.append(pltpu.make_async_copy(pert.at[:, :, tile(q)], pv.at[:, q], in_sem.at[2, q]))
        loads.append(pltpu.make_async_copy(lev.at[:, tile(q)], lv.at[q], in_sem.at[0, q]))
        loads.append(pltpu.make_async_copy(obs.at[:, tile(q)], ov.at[q], in_sem.at[1, q]))
    for copy in needed_first + needed_next:
        copy.start()

    for ref in (ends_of, inner, h0, late0, s1, s2, b0, b1, b2, late_strips):
        clear_rows(ref, ny)

    def dom_copy(up, t):
        first, lands, to = (pd - CAP, 0, k + 1) if up else (0, CAP, k - 1)
        return pltpu.make_async_remote_copy(
            src_ref=ens.at[first + t],
            dst_ref=ext.at[lands + t],
            send_sem=dom_out_sem.at[int(up), t],
            recv_sem=dom_in_sem.at[int(up), t],
            device_id=(to, me),
            device_id_type=MESH,
        )

    def send_particles(up, on):
        @pl.when(on)
        def _():
            for t in range(CAP):
                dom_copy(up, t).start()

    pl.semaphore_wait(
        barrier, dom_peers + sum(jnp.where(late_side[side], 0, side_peers) for side in range(2))
    )
    for side in (1, 0):
        pl.when(ahead_side[side])(functools.partial(signal_side, entered.at[1 - side], side))
    odd = lax.rem(k, 2) == 1
    row_end, row_start = lax.rem(k, ROW) == ROW - 1, lax.rem(k, ROW) == 0
    far_up = row_end & (k < doms - 1) & (place < RUN - 1)
    far_down = row_start & (k > 0) & (place < RUN - 1)

    for copy in needed_first:
        copy.wait()

    def from_own(j):
        return jnp.clip(anc[k * pd + j] - k * pd, 0, pd - 1)

    def from_ext(j, low):
        parent = anc[k * pd + j]
        if low:
            return jnp.where(k == 0, j, jnp.clip(parent - (k * pd - CAP), 0, CAP - 1))
        return jnp.where(
            k == doms - 1, j - (pd - 2 * CAP), jnp.clip(parent - (k + 1) * pd, 0, CAP - 1) + CAP
        )

    def column(i, j, side):
        h = 5.0 * (ends_of[i, H_, side, rows] + pv[j, side * (tiles - 1)])
        return jnp.concatenate(
            [ends_of[i, E_ : N_ + 1, side, rows], h[None], ends_of[i, C_:, side, rows]], axis=0
        )

    flat = lane_of((ny, LANES))

    def message(rightward):
        return pltpu.make_async_remote_copy(
            src_ref=out1.at[int(rightward)],
            dst_ref=in1.at[int(rightward)],
            send_sem=msg_out_sem.at[int(rightward)],
            recv_sem=msg_in_sem.at[int(rightward)],
            device_id=(k, next_space if rightward else prev_space),
            device_id_type=MESH,
        )

    edge_to = (jnp.where(k < doms - 1, k + 1, k), jnp.where(k > 0, k - 1, k))
    edge_side = (jnp.where(k < doms - 1, 0, 1), jnp.where(k > 0, 1, 0))

    def edge_particle(up, t):
        if up:
            return jnp.where(k < doms - 1, pd - CAP + t, from_own(pd - CAP + t))
        return jnp.where(k > 0, t, from_own(t))

    def edge_message(up, rightward):
        at = 0 if up else 1
        return pltpu.make_async_remote_copy(
            src_ref=edge_out.at[at, int(rightward)],
            dst_ref=edge_in.at[edge_side[at], int(rightward)],
            send_sem=edge_out_sem.at[at, int(rightward)],
            recv_sem=edge_in_sem.at[edge_side[at], int(rightward)],
            device_id=(edge_to[at], next_space if rightward else prev_space),
            device_id_type=MESH,
        )

    def edge_arrival(side, rightward):
        return pltpu.make_async_remote_copy(
            src_ref=edge_out.at[side, int(rightward)],
            dst_ref=edge_in.at[side, int(rightward)],
            send_sem=edge_out_sem.at[side, int(rightward)],
            recv_sem=edge_in_sem.at[side, int(rightward)],
            device_id=(k, next_space if rightward else prev_space),
            device_id_type=MESH,
        )

    def shelve(columns, side, at, tile_so_far):
        for f in range(4):
            first = LANES - NEED[f] if side else 0
            to = at + SHELF[f]
            chosen = (flat >= to) & (flat < to + NEED[f])
            tile_so_far = jnp.where(chosen, pltpu.roll(columns[f], (to - first) % LANES, 1), tile_so_far)
        return tile_so_far

    shelves = -(-PAIRS // TRIPLE)

    def pack(side):
        @pl.loop(0, early // (2 * PAIRS))
        def _(m):
            for r in range(shelves):
                packed = jnp.zeros((ny, LANES), jnp.float32)
                for p in range(TRIPLE * r, min(PAIRS, TRIPLE * r + TRIPLE)):
                    for s in range(2):
                        j = CAP + 2 * (PAIRS * m + p) + s
                        at = 64 * s + SLOT_LANES * (p - TRIPLE * r)
                        packed = shelve(column(from_own(j), j, side), side, at, packed)
                out1[side, shelves * m + r] = packed

    extra = shelves * (early // (2 * PAIRS))
    late = [pd - 2, pd - 1, 0, 1]
    def pack_extra(rightward):
        q, end = (tiles - 1, EDGE) if rightward else (0, 0)
        got = jnp.zeros((ny, LANES), jnp.float32)
        parts = [(lv[q].astype(jnp.float32), at) for at in (0, 64)] + [(ov[q], at) for at in (8, 72)]
        parts += [(5.0 * pv[j, q], 64 * (t % 2) + 16 + 8 * (t // 2)) for t, j in enumerate(late)]
        for part, at in parts:
            got = jnp.where((flat >= at) & (flat < at + EDGE), pltpu.roll(part, at + end, 1), got)
        out1[rightward, extra] = got

    for rightward in range(2):
        for up in (True, False):
            got = jnp.zeros((ny, LANES), jnp.float32)
            for t in range(CAP):
                i = edge_particle(up, t)
                columns = [ends_of[i, f, rightward, rows] for f in range(4)]
                columns[H_] = 5.0 * columns[H_]
                got = shelve(columns, rightward, 64 * t, got)
            edge_out[0 if up else 1, rightward] = got

    def send_edges(rightward):
        for up in (False, True):
            edge_message(up, rightward).start()

    def send_message(rightward):
        message(rightward).start()

    for side in (1, 0):
        pl.when(jnp.logical_not(late_side[side]))(functools.partial(send_edges, side))
    send_particles(True, far_up)
    send_particles(False, far_down)
    for side in (1, 0):
        pack(side)
        pack_extra(side)
        pl.when(jnp.logical_not(late_side[side]))(functools.partial(send_message, side))
    send_particles(True, odd & (k < doms - 1) & jnp.logical_not(far_up))
    send_particles(False, jnp.logical_not(odd) & (k > 0) & jnp.logical_not(far_down))
    send_particles(True, jnp.logical_not(odd))
    send_particles(False, odd)

    def send_late(side):
        pl.semaphore_wait(entered.at[side], side_peers)
        send_edges(side)
        send_message(side)

    for copy in needed_next:
        copy.wait()

    levels = lv[...].astype(jnp.float32)
    gw[...], gd[0], gd[1], go[0], go[1] = level_of(levels, ov[...])

    def whole_rows(i, f, at):
        return jnp.concatenate([ends_of[i, f, :1, at], inner[i, f, :, at], ends_of[i, f, 1:, at]], axis=0)

    @pl.loop(0, early // UNIT)
    def _(u):
        for s in range(UNIT):
            j = CAP + u * UNIT + s
            h0[j, :, rows] = 5.0 * (whole_rows(from_own(j), H_, rows) + pv[j])

    @pl.loop(0, early // UNIT)
    def _(u):
        for side in range(2):
            pl.when(late_side[side] & (u == AHEAD[side]))(functools.partial(send_late, side))
        slots = [CAP + u * UNIT + s for s in range(UNIT)]
        where = [from_own(j) for j in slots]

        def first(i, field, y0, up):
            at = pl.ds(TOP + y0 + up, HALF)
            return h0[slots[i], :, at] if field == H_ else whole_rows(where[i], field, at)

        def keep(i, field, y0, value):
            out[slots[i], field, :, pl.ds(y0, HALF)] = value

        all_steps(first, s1, s2, row_ground(gw, gd, go), keep, True, ny, slot_parts())

    late_from = [from_ext(j, j < CAP) for j in late]
    soon = late_soon(k, me, doms)

    def take_late():
        @pl.when(k > 0)
        def _():
            for t in range(CAP):
                dom_copy(True, t).wait_recv()

        @pl.when(k < doms - 1)
        def _():
            for t in range(CAP):
                dom_copy(False, t).wait_recv()

        def own_particle(lands, j):
            for f in range(4):
                state = whole_rows(from_own(j), f, rows)
                for q in range(tiles):
                    ext[lands, f, :, tile(q)] = state[q]

        @pl.when(k == 0)
        def _():
            for s in range(CAP):
                own_particle(s, s)

        @pl.when(k == doms - 1)
        def _():
            for s in range(CAP, 2 * CAP):
                own_particle(s, pd - 2 * CAP + s)

        for t, j in enumerate(late):
            for f in range(4):
                state = jnp.stack([ext[late_from[t], f, :, tile(q)] for q in range(tiles)])
                late0[t, f, :, rows] = 5.0 * (state + pv[j]) if f == H_ else state

    @pl.when(soon)
    def _():
        take_late()

        def keep(i, field, y0, value):
            late_made[i, field, :, pl.ds(y0, HALF)] = value

        all_steps(
            lambda i, field, y0, up: late0[i, field, :, pl.ds(TOP + y0 + up, HALF)],
            s1, s2, row_ground(gw, gd, go), keep, True, ny, slot_parts(),
        )

    for rightward in (False, True):
        message(rightward).wait_recv()

    def ends(first, final, s, tile_so_far):
        base = 64 * s
        lane = lane_of(first.shape)
        chosen = (lane >= base + EDGE) & (lane < base + 3 * EDGE)
        tile_so_far = jnp.where(chosen, pltpu.roll(first, base + EDGE, 2), tile_so_far)
        chosen = (lane >= base + 32) & (lane < base + 32 + 2 * EDGE)
        return jnp.where(chosen, pltpu.roll(final, (base + 32 + 2 * EDGE) % LANES, 2), tile_so_far)

    def beyond(from_left, from_right, at, width=EDGE):
        half = lax.rem(lane_of(from_left.shape), 64)
        chosen = (half >= EDGE - width) & (half < EDGE)
        got = jnp.where(chosen, pltpu.roll(from_left, (LANES + EDGE - width - at) % LANES, 1), 0.0)
        chosen = (half >= 44) & (half < 44 + width)
        return jnp.where(chosen, pltpu.roll(from_right, (LANES + 44 - at) % LANES, 1), got)

    def unshelved(from_left, from_right, at):
        return [beyond(from_left, from_right, at + SHELF[f], NEED[f]) for f in range(4)]

    fields = []
    for i, field in enumerate((levels, ov[...])):
        got = beyond(in1[1, extra], in1[0, extra], 8 * i)[None]
        for s in range(2):
            got = ends(field[:1], field[tiles - 1 :], s, got)
        fields.append(got[0])
    gs[0], gs[1], gs[2], gs[3], gs[4] = level_of(*fields)

    @pl.loop(0, early // (2 * PAIRS))
    def _(m):
        slots = [[CAP + 2 * (PAIRS * m + p) + s for s in range(2)] for p in range(PAIRS)]
        for p in range(PAIRS):
            r = shelves * m + p // TRIPLE
            got = jnp.stack(unshelved(in1[1, r], in1[0, r], SLOT_LANES * (p % TRIPLE)))
            for s, j in enumerate(slots[p]):
                i = from_own(j)
                got = ends(column(i, j, 0), column(i, j, 1), s, got)
            b0[:, p, rows] = got
        step_strips(b0, b1, b2, b3, gs, [slice(0, 4), slice(4, PAIRS)], ny)
        for p in range(PAIRS):
            put_strips(b3, p, slots[p], out)

    pl.when(jnp.logical_not(soon))(take_late)

    for side in range(2):
        for rightward in (False, True):
            edge_arrival(side, rightward).wait_recv()
    for p in range(2):
        side = 1 - p
        where = [late_from[2 * p + s] - CAP * side for s in range(2)]
        ways = []
        for w in range(2):
            came = edge_in[side, w]
            turned = pltpu.roll(came, 64, 1)
            ways.append(jnp.where(flat < 64, *(jnp.where(where[s] == s, came, turned) for s in range(2))))
        got = unshelved(ways[1], ways[0], 0)
        got[H_] = got[H_] + beyond(in1[1, extra], in1[0, extra], 16 + 8 * p)
        got = jnp.stack(got)
        for s in range(2):
            got = ends(late0[2 * p + s, :, 0, rows], late0[2 * p + s, :, tiles - 1, rows], s, got)
        late_strips[:, p, rows] = got

    for rightward in (False, True):
        message(rightward).wait_send()
        for up in (False, True):
            edge_message(up, rightward).wait_send()

    @pl.when(k < doms - 1)
    def _():
        for t in range(CAP):
            dom_copy(True, t).wait_send()

    @pl.when(k > 0)
    def _():
        for t in range(CAP):
            dom_copy(False, t).wait_send()


def finish(made, late_made, late0, late_strips, gs, gw, gd, go, out, late_out, s1, s2, b1, b2, b3, sem):
    pd, nf, tiles, ny, _ = made.shape

    def tile(q):
        return pl.ds(q * LANES, LANES)

    copies = [
        pltpu.make_async_copy(made.at[CAP : pd - CAP, :, q], out.at[CAP : pd - CAP, :, :, tile(q)], sem.at[0, q])
        for q in range(tiles)
    ]
    for copy in copies:
        copy.start()
    for ref in (s1, s2, b1, b2):
        clear_rows(ref, ny)

    soon = late_soon(lax.axis_index("dom"), lax.axis_index("space"), lax.axis_size("dom"))

    @pl.when(soon)
    def _():
        late_out[...] = late_made[...]

    @pl.when(jnp.logical_not(soon))
    def _():
        def keep(i, field, y0, value):
            late_out[i, field, :, pl.ds(y0, HALF)] = value

        all_steps(
            lambda i, field, y0, up: late0[i, field, :, pl.ds(TOP + y0 + up, HALF)],
            s1, s2, row_ground(gw, gd, go), keep, True, ny, slot_parts(),
        )

    step_strips(late_strips, b1, b2, b3, gs, [slice(0, CAP)], ny)
    for p in range(2):
        put_strips(b3, p, [2 * p, 2 * p + 1], late_out)
    for p, first in enumerate((pd - CAP, 0)):
        for q in range(tiles):
            copy = pltpu.make_async_copy(
                late_out.at[CAP * p : CAP * p + CAP, :, q], out.at[first : first + CAP, :, :, tile(q)], sem.at[1 + p, q]
            )
            copy.start()
            copies.append(copy)
    for copy in copies:
        copy.wait()


def local(ensemble, ancestors, perturbation, levels, observed):
    pd, nf, ny, nx = ensemble.shape
    tiles = nx // LANES
    f32 = jnp.float32
    hbm = pl.BlockSpec(memory_space=pl.ANY)
    vmem = pl.BlockSpec(memory_space=pltpu.VMEM)
    state = (UNIT, nf, tiles, PITCH, LANES)
    handed = [
        pltpu.VMEM((pd, nf, tiles, ny, LANES), f32),
        pltpu.VMEM((UNIT, nf, tiles, ny, LANES), f32),
        pltpu.VMEM(state, f32),
        pltpu.VMEM((nf, CAP, PITCH, LANES), f32),
        pltpu.VMEM((5, ny, LANES), f32),
        pltpu.VMEM((tiles, ny, LANES), f32),
        pltpu.VMEM((2, tiles, ny, LANES), f32),
        pltpu.VMEM((2, tiles, ny, LANES), f32),
    ]
    between = pl.pallas_call(
        kernel,
        out_shape=handed,
        in_specs=[hbm] * 5,
        out_specs=[vmem] * len(handed),
        scratch_shapes=[
            pltpu.SMEM(ancestors.shape, jnp.int32),
            pltpu.VMEM((pd, nf, 2, PITCH, LANES), f32),
            pltpu.VMEM((pd, nf, tiles - 2, PITCH, LANES), f32),
            pltpu.VMEM((2 * CAP, nf, ny, nx), f32),
            pltpu.VMEM((pd, tiles, PITCH, LANES), f32),
            pltpu.VMEM((pd, tiles, ny, LANES), f32),
            pltpu.VMEM((tiles, ny, LANES), jnp.int32),
            pltpu.VMEM((tiles, ny, LANES), f32),
            pltpu.VMEM(state, f32),
            pltpu.VMEM(state, f32),
            pltpu.VMEM((nf, PAIRS, PITCH, LANES), f32),
            pltpu.VMEM((nf, PAIRS, PITCH, LANES), f32),
            pltpu.VMEM((nf, PAIRS, PITCH, LANES), f32),
            pltpu.VMEM((nf, PAIRS, ny, LANES), f32),
            pltpu.VMEM((2, 7, ny, LANES), f32),
            pltpu.VMEM((2, 7, ny, LANES), f32),
            pltpu.VMEM((2, 2, ny, LANES), f32),
            pltpu.VMEM((2, 2, ny, LANES), f32),
            pltpu.SemaphoreType.DMA((5, tiles)),
            pltpu.SemaphoreType.DMA((2, CAP)),
            pltpu.SemaphoreType.DMA((2, CAP)),
            pltpu.SemaphoreType.DMA((2,)),
            pltpu.SemaphoreType.DMA((2,)),
            pltpu.SemaphoreType.DMA((2, 2)),
            pltpu.SemaphoreType.DMA((2, 2)),
            pltpu.SemaphoreType.REGULAR((2,)),
        ],
        compiler_params=pltpu.CompilerParams(
            collective_id=0, has_side_effects=True, vmem_limit_bytes=40 * 1024 * 1024
        ),
        name="resample_and_step",
    )(*(pltpu.with_memory_space_constraint(x, pltpu.HBM) for x in (ancestors, ensemble, perturbation, levels, observed)))
    return pl.pallas_call(
        finish,
        out_shape=jax.ShapeDtypeStruct((pd, nf, ny, nx), f32),
        in_specs=[vmem] * len(handed),
        out_specs=hbm,
        scratch_shapes=[
            pltpu.VMEM((UNIT, nf, tiles, ny, LANES), f32),
            pltpu.VMEM(state, f32),
            pltpu.VMEM(state, f32),
            pltpu.VMEM((nf, CAP, PITCH, LANES), f32),
            pltpu.VMEM((nf, CAP, PITCH, LANES), f32),
            pltpu.VMEM((nf, CAP, ny, LANES), f32),
            pltpu.SemaphoreType.DMA((3, tiles)),
        ],
        compiler_params=pltpu.CompilerParams(vmem_limit_bytes=24 * 1024 * 1024),
        name="finish",
    )(*between)


def solution(mesh):
    return jax.shard_map(
        local,
        mesh=mesh,
        in_specs=(
            P("dom", None, None, "space"),
            P(),
            P("dom", None, "space"),
            P(None, "space"),
            P(None, "space"),
        ),
        out_specs=P("dom", None, None, "space"),
        check_vma=False,
    )
```

```python
import functools

import jax
import jax.numpy as jnp
from jax import lax
from jax.experimental import pallas as pl
from jax.experimental.pallas import tpu as pltpu
from jax.sharding import PartitionSpec as P

MESH = pl.DeviceIdType.MESH
STEPS = 3
CAP = 2
EDGE = 2 * STEPS
LANES = 128
TOP = 8
PITCH = 32
UNIT = 4
HALF = 8
PAIRS = 7
RUN = 8
LAGS = 4
AHEAD = (5, 2)
NEED = (EDGE, EDGE - 1, EDGE, EDGE - 3)
SHELF = (0, 12, 6, 17)
SLOT_LANES = 20
TRIPLE = 3
E_, N_, H_, C_ = range(4)


def lane_of(shape):
    return lax.broadcasted_iota(jnp.int32, shape, len(shape) - 1)


def east(cells, joined):
    turned = pltpu.roll(cells, LANES - 1, 2)
    if not joined:
        return turned
    following = jnp.concatenate([turned[1:], turned[:1]], axis=0)
    return jnp.where(lane_of(cells.shape) == LANES - 1, following, turned)


def west(cells, joined):
    turned = pltpu.roll(cells, 1, 2)
    if not joined:
        return turned
    preceding = jnp.concatenate([turned[-1:], turned[:-1]], axis=0)
    return jnp.where(lane_of(cells.shape) == 0, preceding, turned)


def flow(read, wet, turn, joined):
    e, n, h = read(E_, 0), read(N_, 0), read(H_, 0)
    e_new = wet * (
        (5.5 * e + turn * n)
        + (read(E_, 1) + read(E_, -1))
        + (east(e - h, joined) + west(e + h, joined))
    )
    n_new = wet * (
        (5.5 * n - turn * e)
        + (east(n, joined) + west(n, joined))
        + ((read(N_, 1) - read(H_, 1)) + (read(N_, -1) + read(H_, -1)))
    )
    return e_new, n_new


def level(read, read_new, depth, pull, last, joined):
    e, n = read_new(E_, 0), read_new(N_, 0)
    spread = (east(e, joined) - west(e, joined)) + (read_new(N_, 1) - read_new(N_, -1))
    h_new = ((0.18 if last else 0.9) * read(H_, 0) + pull) - depth * spread
    c = read(C_, 0)
    c_east, c_west = east(c, joined), west(c, joined)
    c_north, c_south = read(C_, 1), read(C_, -1)
    c_new = (
        (6.0 * c + ((c_east + c_west) + (c_north + c_south)))
        - e * (c_east - c_west)
        - n * (c_north - c_south)
    )
    if last:
        c_new = 0.001 * c_new
    return h_new, c_new


def level_of(levels, observed):
    return (
        jnp.where(levels > 0, 0.1, 0.0).astype(jnp.float32),
        1.25 * levels,
        0.25 * levels,
        0.5 * observed,
        0.1 * observed,
    )


def turn_of(ny, y0):
    y = lax.broadcasted_iota(jnp.int32, (1, HALF, LANES), 1).astype(jnp.float32) + float(y0)
    return 2.0 * (0.2 + 0.6 * y / ny)


def all_steps(first, s1, s2, ground, keep, joined, ny, parts):
    wet, depth, pull = ground
    count = len(parts)
    for step in range(STEPS):
        last = step == STEPS - 1
        old, new = (None, s1) if step == 0 else (s1, s2) if step == 1 else (s2, s1)

        def reader(ref, i, y0):
            return lambda field, up: parts[i](ref, field, pl.ds(TOP + y0 + up, HALF))[...]

        def read(i, y0):
            return (lambda field, up: first(i, field, y0, up)) if step == 0 else reader(old, i, y0)

        for i in range(count):
            for y0 in range(0, ny, HALF):
                e, n = flow(read(i, y0), wet(y0), turn_of(ny, y0), joined)
                now = pl.ds(TOP + y0, HALF)
                parts[i](new, E_, now)[...] = e
                parts[i](new, N_, now)[...] = n
                if last:
                    keep(i, E_, y0, e)
                    keep(i, N_, y0, n)
        for i in range(count):
            for y0 in range(0, ny, HALF):
                h, c = level(read(i, y0), reader(new, i, y0), depth(last, y0), pull(last, y0), last, joined)
                now = pl.ds(TOP + y0, HALF)
                if last:
                    keep(i, H_, y0, h)
                    keep(i, C_, y0, c)
                else:
                    parts[i](new, H_, now)[...] = h
                    parts[i](new, C_, now)[...] = c


def slot_parts():
    return [lambda ref, field, now, s=s: ref.at[s, field, :, now] for s in range(UNIT)]


def row_ground(gw, gd, go):
    return (
        lambda y0: gw[:, pl.ds(y0, HALF)],
        lambda last, y0: gd[int(last), :, pl.ds(y0, HALF)],
        lambda last, y0: go[int(last), :, pl.ds(y0, HALF)],
    )


def strip_ground(gs):
    return (
        lambda y0: gs[0, pl.ds(y0, HALF)][None],
        lambda last, y0: gs[2 if last else 1, pl.ds(y0, HALF)][None],
        lambda last, y0: gs[4 if last else 3, pl.ds(y0, HALF)][None],
    )


def step_strips(b0, b1, b2, b3, gs, groups, ny):
    parts = [lambda ref, field, now, g=g: ref.at[field, g, now] for g in groups]

    def keep(i, field, y0, value):
        b3[field, groups[i], pl.ds(y0, HALF)] = value

    all_steps(
        lambda i, field, y0, up: b0[field, groups[i], pl.ds(TOP + y0 + up, HALF)],
        b1, b2, strip_ground(gs), keep, False, ny, parts,
    )


def put_strips(b3, p, slots, out):
    done = b3[:, p]
    lane = lane_of(done.shape)
    final = out.shape[2] - 1
    for s, j in enumerate(slots):
        base = 64 * s
        at_left = pltpu.roll(done, LANES - EDGE - base, 2)
        at_right = pltpu.roll(done, (LANES - EDGE - (base + 32 + EDGE)) % LANES, 2)
        pltpu.store(out.at[j, :, 0], at_left, mask=lane < EDGE)
        pltpu.store(out.at[j, :, final], at_right, mask=lane >= LANES - EDGE)


def clear_rows(ref, ny):
    @pl.loop(0, ref.shape[0])
    def _(i):
        blank = jnp.zeros(ref.shape[1:-2] + (8, LANES), jnp.float32)
        ref[i, ..., TOP - 8 : TOP, :] = blank
        ref[i, ..., TOP + ny : TOP + ny + 8, :] = blank


def kernel(
    anc_in, ens, pert, lev, obs, out, late0, late_strips, gs, gw, gd, go,
    anc, ends_of, inner, ext, h0, pv, lv, ov, s1, s2, b0, b1, b2, b3, out1, in1, edge_out, edge_in,
    in_sem, dom_out_sem, dom_in_sem, msg_out_sem, msg_in_sem, edge_out_sem, edge_in_sem, entered,
):
    pd = ens.shape[0]
    ny = ens.shape[2]
    tiles = ens.shape[3] // LANES
    doms, spaces = lax.axis_size("dom"), lax.axis_size("space")
    k, me = lax.axis_index("dom"), lax.axis_index("space")
    prev_space, next_space = lax.rem(me + spaces - 1, spaces), lax.rem(me + 1, spaces)
    early = pd - 2 * CAP
    rows = slice(TOP, TOP + ny)

    barrier = pltpu.get_barrier_semaphore()

    def signal(semaphore, dom, space):
        pl.semaphore_signal(semaphore, inc=1, device_id=(dom, space), device_id_type=MESH)

    def signal_side(semaphore, rightward):
        space = next_space if rightward else prev_space
        signal(semaphore, k, space)

        @pl.when(k > 0)
        def _():
            signal(semaphore, k - 1, space)

        @pl.when(k < doms - 1)
        def _():
            signal(semaphore, k + 1, space)

    place = lax.rem(me, RUN)
    late_side = (place == 0, place < LAGS)
    ahead_side = ((place > 0) & (place <= LAGS), place == RUN - 1)
    dom_peers = jnp.where(k > 0, 1, 0) + jnp.where(k < doms - 1, 1, 0)
    side_peers = 1 + dom_peers

    @pl.when(k > 0)
    def _():
        signal(barrier, k - 1, me)

    @pl.when(k < doms - 1)
    def _():
        signal(barrier, k + 1, me)

    for side in range(2):
        pl.when(jnp.logical_not(ahead_side[side]))(functools.partial(signal_side, barrier, side))

    def tile(q):
        return pl.ds(q * LANES, LANES)

    needed_first, needed_next = [pltpu.make_async_copy(anc_in, anc, in_sem.at[4, 0])], []
    for q in (0, tiles - 1, *range(1, tiles - 1)):
        at_end = q in (0, tiles - 1)
        loads = needed_first if at_end else needed_next
        here = ends_of.at[:, :, int(q > 0), rows] if at_end else inner.at[:, :, q - 1, rows]
        loads.append(pltpu.make_async_copy(ens.at[:, :, :, tile(q)], here, in_sem.at[3, q]))
        loads.append(pltpu.make_async_copy(pert.at[:, :, tile(q)], pv.at[:, q], in_sem.at[2, q]))
        loads.append(pltpu.make_async_copy(lev.at[:, tile(q)], lv.at[q], in_sem.at[0, q]))
        loads.append(pltpu.make_async_copy(obs.at[:, tile(q)], ov.at[q], in_sem.at[1, q]))
    for copy in needed_first + needed_next:
        copy.start()

    for ref in (ends_of, inner, h0, late0, s1, s2, b0, b1, b2, late_strips):
        clear_rows(ref, ny)

    for copy in needed_first:
        copy.wait()

    def from_own(j):
        return jnp.clip(anc[k * pd + j] - k * pd, 0, pd - 1)

    def from_ext(j, low):
        parent = anc[k * pd + j]
        if low:
            return jnp.where(k == 0, j, jnp.clip(parent - (k * pd - CAP), 0, CAP - 1))
        return jnp.where(
            k == doms - 1, j - (pd - 2 * CAP), jnp.clip(parent - (k + 1) * pd, 0, CAP - 1) + CAP
        )

    def column(i, j, side):
        h = 5.0 * (ends_of[i, H_, side, rows] + pv[j, side * (tiles - 1)])
        return jnp.concatenate(
            [ends_of[i, E_ : N_ + 1, side, rows], h[None], ends_of[i, C_:, side, rows]], axis=0
        )

    flat = lane_of((ny, LANES))

    def message(rightward):
        return pltpu.make_async_remote_copy(
            src_ref=out1.at[int(rightward)],
            dst_ref=in1.at[int(rightward)],
            send_sem=msg_out_sem.at[int(rightward)],
            recv_sem=msg_in_sem.at[int(rightward)],
            device_id=(k, next_space if rightward else prev_space),
            device_id_type=MESH,
        )

    edge_to = (jnp.where(k < doms - 1, k + 1, k), jnp.where(k > 0, k - 1, k))
    edge_side = (jnp.where(k < doms - 1, 0, 1), jnp.where(k > 0, 1, 0))

    def edge_particle(up, t):
        if up:
            return jnp.where(k < doms - 1, pd - CAP + t, from_own(pd - CAP + t))
        return jnp.where(k > 0, t, from_own(t))

    def edge_message(up, rightward):
        at = 0 if up else 1
        return pltpu.make_async_remote_copy(
            src_ref=edge_out.at[at, int(rightward)],
            dst_ref=edge_in.at[edge_side[at], int(rightward)],
            send_sem=edge_out_sem.at[at, int(rightward)],
            recv_sem=edge_in_sem.at[edge_side[at], int(rightward)],
            device_id=(edge_to[at], next_space if rightward else prev_space),
            device_id_type=MESH,
        )

    def edge_arrival(side, rightward):
        return pltpu.make_async_remote_copy(
            src_ref=edge_out.at[side, int(rightward)],
            dst_ref=edge_in.at[side, int(rightward)],
            send_sem=edge_out_sem.at[side, int(rightward)],
            recv_sem=edge_in_sem.at[side, int(rightward)],
            device_id=(k, next_space if rightward else prev_space),
            device_id_type=MESH,
        )

    def shelve(columns, side, at, tile_so_far):
        for f in range(4):
            first = LANES - NEED[f] if side else 0
            to = at + SHELF[f]
            chosen = (flat >= to) & (flat < to + NEED[f])
            tile_so_far = jnp.where(chosen, pltpu.roll(columns[f], (to - first) % LANES, 1), tile_so_far)
        return tile_so_far

    shelves = -(-PAIRS // TRIPLE)

    @pl.loop(0, early // (2 * PAIRS))
    def _(m):
        for r in range(shelves):
            packed = [jnp.zeros((ny, LANES), jnp.float32)] * 2
            for p in range(TRIPLE * r, min(PAIRS, TRIPLE * r + TRIPLE)):
                for s in range(2):
                    j = CAP + 2 * (PAIRS * m + p) + s
                    i = from_own(j)
                    for side in range(2):
                        at = 64 * s + SLOT_LANES * (p - TRIPLE * r)
                        packed[side] = shelve(column(i, j, side), side, at, packed[side])
            for side in range(2):
                out1[side, shelves * m + r] = packed[side]

    extra = shelves * (early // (2 * PAIRS))
    late = [pd - 2, pd - 1, 0, 1]
    for rightward in range(2):
        q, end = (tiles - 1, EDGE) if rightward else (0, 0)
        got = jnp.zeros((ny, LANES), jnp.float32)
        parts = [(lv[q].astype(jnp.float32), at) for at in (0, 64)] + [(ov[q], at) for at in (8, 72)]
        parts += [(5.0 * pv[j, q], 64 * (t % 2) + 16 + 8 * (t // 2)) for t, j in enumerate(late)]
        for part, at in parts:
            got = jnp.where((flat >= at) & (flat < at + EDGE), pltpu.roll(part, at + end, 1), got)
        out1[rightward, extra] = got
        for up in (True, False):
            got = jnp.zeros((ny, LANES), jnp.float32)
            for t in range(CAP):
                i = edge_particle(up, t)
                columns = [ends_of[i, f, rightward, rows] for f in range(4)]
                columns[H_] = 5.0 * columns[H_]
                got = shelve(columns, rightward, 64 * t, got)
            edge_out[0 if up else 1, rightward] = got

    def dom_copy(up, t):
        first, lands, to = (pd - CAP, 0, k + 1) if up else (0, CAP, k - 1)
        return pltpu.make_async_remote_copy(
            src_ref=ens.at[first + t],
            dst_ref=ext.at[lands + t],
            send_sem=dom_out_sem.at[int(up), t],
            recv_sem=dom_in_sem.at[int(up), t],
            device_id=(to, me),
            device_id_type=MESH,
        )

    def send_particles(up, on):
        @pl.when(on)
        def _():
            for t in range(CAP):
                dom_copy(up, t).start()

    odd = lax.rem(k, 2) == 1

    def send_side(rightward):
        message(rightward).start()
        for up in (False, True):
            edge_message(up, rightward).start()

    pl.semaphore_wait(
        barrier, dom_peers + sum(jnp.where(late_side[side], 0, side_peers) for side in range(2))
    )
    for side in (1, 0):
        pl.when(ahead_side[side])(functools.partial(signal_side, entered.at[1 - side], side))
    for side in (1, 0):
        pl.when(jnp.logical_not(late_side[side]))(functools.partial(send_side, side))
    send_particles(True, odd & (k < doms - 1))
    send_particles(False, jnp.logical_not(odd) & (k > 0))
    send_particles(True, jnp.logical_not(odd))
    send_particles(False, odd)

    def send_late(side):
        pl.semaphore_wait(entered.at[side], side_peers)
        send_side(side)

    for copy in needed_next:
        copy.wait()

    levels = lv[...].astype(jnp.float32)
    gw[...], gd[0], gd[1], go[0], go[1] = level_of(levels, ov[...])

    def whole_rows(i, f, at):
        return jnp.concatenate([ends_of[i, f, :1, at], inner[i, f, :, at], ends_of[i, f, 1:, at]], axis=0)

    @pl.loop(0, early // UNIT)
    def _(u):
        for s in range(UNIT):
            j = CAP + u * UNIT + s
            h0[j, :, rows] = 5.0 * (whole_rows(from_own(j), H_, rows) + pv[j])

    @pl.loop(0, early // UNIT)
    def _(u):
        for side in range(2):
            pl.when(late_side[side] & (u == AHEAD[side]))(functools.partial(send_late, side))
        slots = [CAP + u * UNIT + s for s in range(UNIT)]
        where = [from_own(j) for j in slots]

        def first(i, field, y0, up):
            at = pl.ds(TOP + y0 + up, HALF)
            return h0[slots[i], :, at] if field == H_ else whole_rows(where[i], field, at)

        def keep(i, field, y0, value):
            out[slots[i], field, :, pl.ds(y0, HALF)] = value

        all_steps(first, s1, s2, row_ground(gw, gd, go), keep, True, ny, slot_parts())

    for rightward in (False, True):
        message(rightward).wait_recv()

    def ends(first, final, s, tile_so_far):
        base = 64 * s
        lane = lane_of(first.shape)
        chosen = (lane >= base + EDGE) & (lane < base + 3 * EDGE)
        tile_so_far = jnp.where(chosen, pltpu.roll(first, base + EDGE, 2), tile_so_far)
        chosen = (lane >= base + 32) & (lane < base + 32 + 2 * EDGE)
        return jnp.where(chosen, pltpu.roll(final, (base + 32 + 2 * EDGE) % LANES, 2), tile_so_far)

    def beyond(from_left, from_right, at, width=EDGE):
        half = lax.rem(lane_of(from_left.shape), 64)
        chosen = (half >= EDGE - width) & (half < EDGE)
        got = jnp.where(chosen, pltpu.roll(from_left, (LANES + EDGE - width - at) % LANES, 1), 0.0)
        chosen = (half >= 44) & (half < 44 + width)
        return jnp.where(chosen, pltpu.roll(from_right, (LANES + 44 - at) % LANES, 1), got)

    def unshelved(from_left, from_right, at):
        return [beyond(from_left, from_right, at + SHELF[f], NEED[f]) for f in range(4)]

    fields = []
    for i, field in enumerate((levels, ov[...])):
        got = beyond(in1[1, extra], in1[0, extra], 8 * i)[None]
        for s in range(2):
            got = ends(field[:1], field[tiles - 1 :], s, got)
        fields.append(got[0])
    gs[0], gs[1], gs[2], gs[3], gs[4] = level_of(*fields)

    @pl.loop(0, early // (2 * PAIRS))
    def _(m):
        slots = [[CAP + 2 * (PAIRS * m + p) + s for s in range(2)] for p in range(PAIRS)]
        for p in range(PAIRS):
            r = shelves * m + p // TRIPLE
            got = jnp.stack(unshelved(in1[1, r], in1[0, r], SLOT_LANES * (p % TRIPLE)))
            for s, j in enumerate(slots[p]):
                i = from_own(j)
                got = ends(column(i, j, 0), column(i, j, 1), s, got)
            b0[:, p, rows] = got
        step_strips(b0, b1, b2, b3, gs, [slice(0, 4), slice(4, PAIRS)], ny)
        for p in range(PAIRS):
            put_strips(b3, p, slots[p], out)

    @pl.when(k > 0)
    def _():
        for t in range(CAP):
            dom_copy(True, t).wait_recv()

    @pl.when(k < doms - 1)
    def _():
        for t in range(CAP):
            dom_copy(False, t).wait_recv()

    def own_particle(lands, j):
        for f in range(4):
            state = whole_rows(from_own(j), f, rows)
            for q in range(tiles):
                ext[lands, f, :, tile(q)] = state[q]

    @pl.when(k == 0)
    def _():
        for s in range(CAP):
            own_particle(s, s)

    @pl.when(k == doms - 1)
    def _():
        for s in range(CAP, 2 * CAP):
            own_particle(s, pd - 2 * CAP + s)

    late_from = [from_ext(j, j < CAP) for j in late]
    for t, j in enumerate(late):
        for f in range(4):
            state = jnp.stack([ext[late_from[t], f, :, tile(q)] for q in range(tiles)])
            late0[t, f, :, rows] = 5.0 * (state + pv[j]) if f == H_ else state

    for side in range(2):
        for rightward in (False, True):
            edge_arrival(side, rightward).wait_recv()
    for p in range(2):
        side = 1 - p
        where = [late_from[2 * p + s] - CAP * side for s in range(2)]
        ways = []
        for w in range(2):
            came = edge_in[side, w]
            turned = pltpu.roll(came, 64, 1)
            ways.append(jnp.where(flat < 64, *(jnp.where(where[s] == s, came, turned) for s in range(2))))
        got = unshelved(ways[1], ways[0], 0)
        got[H_] = got[H_] + beyond(in1[1, extra], in1[0, extra], 16 + 8 * p)
        got = jnp.stack(got)
        for s in range(2):
            got = ends(late0[2 * p + s, :, 0, rows], late0[2 * p + s, :, tiles - 1, rows], s, got)
        late_strips[:, p, rows] = got

    for rightward in (False, True):
        message(rightward).wait_send()
        for up in (False, True):
            edge_message(up, rightward).wait_send()

    @pl.when(k < doms - 1)
    def _():
        for t in range(CAP):
            dom_copy(True, t).wait_send()

    @pl.when(k > 0)
    def _():
        for t in range(CAP):
            dom_copy(False, t).wait_send()


def finish(made, late0, late_strips, gs, gw, gd, go, out, late_out, s1, s2, b1, b2, b3, sem):
    pd, nf, tiles, ny, _ = made.shape

    def tile(q):
        return pl.ds(q * LANES, LANES)

    copies = [
        pltpu.make_async_copy(made.at[CAP : pd - CAP, :, q], out.at[CAP : pd - CAP, :, :, tile(q)], sem.at[0, q])
        for q in range(tiles)
    ]
    for copy in copies:
        copy.start()
    for ref in (s1, s2, b1, b2):
        clear_rows(ref, ny)

    def keep(i, field, y0, value):
        late_out[i, field, :, pl.ds(y0, HALF)] = value

    all_steps(
        lambda i, field, y0, up: late0[i, field, :, pl.ds(TOP + y0 + up, HALF)],
        s1, s2, row_ground(gw, gd, go), keep, True, ny, slot_parts(),
    )
    step_strips(late_strips, b1, b2, b3, gs, [slice(0, CAP)], ny)
    for p in range(2):
        put_strips(b3, p, [2 * p, 2 * p + 1], late_out)
    for p, first in enumerate((pd - CAP, 0)):
        for q in range(tiles):
            copy = pltpu.make_async_copy(
                late_out.at[CAP * p : CAP * p + CAP, :, q], out.at[first : first + CAP, :, :, tile(q)], sem.at[1 + p, q]
            )
            copy.start()
            copies.append(copy)
    for copy in copies:
        copy.wait()


def local(ensemble, ancestors, perturbation, levels, observed):
    pd, nf, ny, nx = ensemble.shape
    tiles = nx // LANES
    f32 = jnp.float32
    hbm = pl.BlockSpec(memory_space=pl.ANY)
    vmem = pl.BlockSpec(memory_space=pltpu.VMEM)
    state = (UNIT, nf, tiles, PITCH, LANES)
    handed = [
        pltpu.VMEM((pd, nf, tiles, ny, LANES), f32),
        pltpu.VMEM(state, f32),
        pltpu.VMEM((nf, CAP, PITCH, LANES), f32),
        pltpu.VMEM((5, ny, LANES), f32),
        pltpu.VMEM((tiles, ny, LANES), f32),
        pltpu.VMEM((2, tiles, ny, LANES), f32),
        pltpu.VMEM((2, tiles, ny, LANES), f32),
    ]
    between = pl.pallas_call(
        kernel,
        out_shape=handed,
        in_specs=[hbm] * 5,
        out_specs=[vmem] * len(handed),
        scratch_shapes=[
            pltpu.SMEM(ancestors.shape, jnp.int32),
            pltpu.VMEM((pd, nf, 2, PITCH, LANES), f32),
            pltpu.VMEM((pd, nf, tiles - 2, PITCH, LANES), f32),
            pltpu.VMEM((2 * CAP, nf, ny, nx), f32),
            pltpu.VMEM((pd, tiles, PITCH, LANES), f32),
            pltpu.VMEM((pd, tiles, ny, LANES), f32),
            pltpu.VMEM((tiles, ny, LANES), jnp.int32),
            pltpu.VMEM((tiles, ny, LANES), f32),
            pltpu.VMEM(state, f32),
            pltpu.VMEM(state, f32),
            pltpu.VMEM((nf, PAIRS, PITCH, LANES), f32),
            pltpu.VMEM((nf, PAIRS, PITCH, LANES), f32),
            pltpu.VMEM((nf, PAIRS, PITCH, LANES), f32),
            pltpu.VMEM((nf, PAIRS, ny, LANES), f32),
            pltpu.VMEM((2, 7, ny, LANES), f32),
            pltpu.VMEM((2, 7, ny, LANES), f32),
            pltpu.VMEM((2, 2, ny, LANES), f32),
            pltpu.VMEM((2, 2, ny, LANES), f32),
            pltpu.SemaphoreType.DMA((5, tiles)),
            pltpu.SemaphoreType.DMA((2, CAP)),
            pltpu.SemaphoreType.DMA((2, CAP)),
            pltpu.SemaphoreType.DMA((2,)),
            pltpu.SemaphoreType.DMA((2,)),
            pltpu.SemaphoreType.DMA((2, 2)),
            pltpu.SemaphoreType.DMA((2, 2)),
            pltpu.SemaphoreType.REGULAR((2,)),
        ],
        compiler_params=pltpu.CompilerParams(
            collective_id=0, has_side_effects=True, vmem_limit_bytes=40 * 1024 * 1024
        ),
        name="resample_and_step",
    )(*(pltpu.with_memory_space_constraint(x, pltpu.HBM) for x in (ancestors, ensemble, perturbation, levels, observed)))
    return pl.pallas_call(
        finish,
        out_shape=jax.ShapeDtypeStruct((pd, nf, ny, nx), f32),
        in_specs=[vmem] * len(handed),
        out_specs=hbm,
        scratch_shapes=[
            pltpu.VMEM((UNIT, nf, tiles, ny, LANES), f32),
            pltpu.VMEM(state, f32),
            pltpu.VMEM(state, f32),
            pltpu.VMEM((nf, CAP, PITCH, LANES), f32),
            pltpu.VMEM((nf, CAP, PITCH, LANES), f32),
            pltpu.VMEM((nf, CAP, ny, LANES), f32),
            pltpu.SemaphoreType.DMA((3, tiles)),
        ],
        compiler_params=pltpu.CompilerParams(vmem_limit_bytes=24 * 1024 * 1024),
        name="finish",
    )(*between)


def solution(mesh):
    return jax.shard_map(
        local,
        mesh=mesh,
        in_specs=(
            P("dom", None, None, "space"),
            P(),
            P("dom", None, "space"),
            P(None, "space"),
            P(None, "space"),
        ),
        out_specs=P("dom", None, None, "space"),
        check_vma=False,
    )
```
